32 devices in a mesh: gx: 4 (over y, core), gy: 8 (over z, x).
Axes of the slice: x: 2, y: 2, z: 4, core: 2. Of those that a mesh axis runs over, the one named last changes fastest.
Arguments:
- positions: float32 [3, 524288], P(None, ('gx', 'gy')), may hold values from 0 to 128, as said below
- point_feat: float32 [32, 524288], P(None, ('gx', 'gy')), may hold values from -1.8 to 1.8
- area: float32 [524288], P(('gx', 'gy')), may hold values from 0.3 to 3
- block_brick: int32 [4096], P(('gx', 'gy')), may hold values from 0 to 4095, as said below
- block_count: int32 [32], P(('gx', 'gy')), may hold values from 16 to 128, as said below
- sdf: float32 [128, 128, 128], P('gx', 'gy'), may hold values from -6 to 6
- grid_gain: float32 [32], replicated, may hold values from -4 to 4
- mix_w: float32 [2, 32, 32], replicated, may hold values from -1 to 1
- mix_b: float32 [2, 32], replicated, may hold values from -1.8 to 1.8
- spec_w: float32 [2, 2, 16, 32, 1024], P(None, None, 'gy', 'gx'), may hold values from -18 to 18
- readout_w: float32 [32], replicated, may hold values from -1 to 1
Outputs:
- pressure: float32 [524288], P(('gx', 'gy'))
The draws below stay inside these ranges and needn't reach their ends.
Inputs may be any that keep to these rules, and one draw needn't show every extreme that they name: `block_brick`: block n belongs to partition d = n // 128. Its brick b lies in the grid pencil row of that partition: (b // 256) // 4 == d // 8. Of the blocks of one partition at most 16 lie in the bricks of one pencil, the pencil of b being ((b // 16) % 16) // 2; in every pencil row some pencil holds exactly 16 of the first 16 blocks of every partition of that row. The live blocks of partition d are its first block_count[d] blocks; some partition has all 128 live and some has exactly 16. `positions`: every point lies inside its block's brick, 0.5 or more from each of the brick's faces.
All inputs are finite; a program needn't handle non-finite values.
Results may differ from the reference program's by a relative error of at most 0.0003.
Values sent between devices are 32-bit elements; how exact they have to be, the bound alone decides.
No kernel may reach another device: no remote copies, remote signals or barrier semaphores. Data moves between devices by JAX's collectives and lax.ppermute only.
A program may use at most 192 MiB of HBM per device.

```python
import math
import jax
import jax.numpy as jnp
from jax import lax

G = 128
C = 32
M = 32
B = 8
PB = 128
LAYERS = 2
BLK_DEV = 128
KZ = 16
NB = 16
NBX = 4
NBY = 2
CAP = 16
PARTITIONS = 32
NBLK = 4096
NPTS = 524288


def brick_layout(key):
    base_key = jax.random.fold_in(key, 101)
    key_full, key_perm, key_x, key_y, key_z = jax.random.split(base_key, 5)
    rows_x = NB // NBX
    owners = NB // NBY
    favored = jax.random.randint(key_full, (rows_x,), 0, owners)
    part_index = jnp.arange(PARTITIONS, dtype=jnp.int32)
    part_row = part_index // owners
    spare_slots = BLK_DEV - CAP
    perm_keys = jax.random.split(key_perm, PARTITIONS)
    shuffled = jax.vmap(lambda one_key: jax.random.permutation(one_key, spare_slots))(perm_keys)
    shuffled = shuffled.astype(jnp.int32) + CAP
    leading = jnp.broadcast_to(jnp.arange(CAP, dtype=jnp.int32)[None, :], (PARTITIONS, CAP))
    slot_order = jnp.concatenate([leading, shuffled], axis=1)
    target = (slot_order // CAP + favored[part_row][:, None]) % owners
    local_x = jax.random.randint(key_x, (PARTITIONS, BLK_DEV), 0, NBX)
    local_y = jax.random.randint(key_y, (PARTITIONS, BLK_DEV), 0, NBY)
    local_z = jax.random.randint(key_z, (PARTITIONS, BLK_DEV), 0, NB)
    brick_x = part_row[:, None] * NBX + local_x
    brick_y = target * NBY + local_y
    return ((brick_x * NB + brick_y) * NB + local_z).reshape(NBLK).astype(jnp.int32)


def draw_block_brick(key, part):
    return brick_layout(key)


def draw_positions(key, part):
    bricks = brick_layout(key)
    corners = jnp.stack([bricks // (NB * NB), bricks // NB % NB, bricks % NB]).astype(jnp.float32) * B
    spread = jax.random.uniform(jax.random.fold_in(key, 202), (3, NBLK, PB), dtype=jnp.float32)
    placed = corners[:, :, None] + 0.5 + (B - 1.0) * spread
    return placed.reshape(3, NPTS)


def draw_block_count(key, part):
    base_key = jax.random.fold_in(key, 303)
    key_a, key_b, key_c, key_d = jax.random.split(base_key, 4)
    spare_slots = BLK_DEV - CAP
    factor_one = jax.random.randint(key_a, (PARTITIONS,), 0, spare_slots + 1)
    factor_two = jax.random.randint(key_b, (PARTITIONS,), 0, spare_slots + 1)
    counts = BLK_DEV // 2 + factor_one * factor_two // (2 * spare_slots)
    fullest = jax.random.randint(key_c, (), 0, PARTITIONS)
    emptiest = (fullest + 1 + jax.random.randint(key_d, (), 0, PARTITIONS - 1)) % PARTITIONS
    counts = counts.at[fullest].set(BLK_DEV).at[emptiest].set(CAP)
    return counts.astype(jnp.int32)


def block_levels(key, shape, cuts, smallest, high):
    def one(dim, parts):
        heights = jax.random.uniform(jax.random.fold_in(jax.random.fold_in(key, 6), dim), (parts,), jnp.float32, smallest / len(cuts), high / len(cuts))
        return jnp.repeat(jnp.exp(heights), shape[dim] // parts).reshape((-1,) + (1,) * (len(shape) - dim - 1))

    factor_of = one(*cuts[0])
    for cut in cuts[1:]:
        factor_of = factor_of * one(*cut)
    return factor_of


def centred(stream_key, extent, width, limit, cuts=(), kind=jnp.bfloat16):
    factor_of = block_levels(stream_key, extent, cuts, -0.22, 0.18) if cuts else 1.0
    entries = jax.random.normal(stream_key, extent, jnp.float32) * width * factor_of
    return jnp.minimum(jnp.maximum(entries, -limit), limit).astype(kind)


def setup_inputs(seed: int = 0) -> dict:
    splits = jax.random.split(jax.random.key(seed), 12)
    return {
        "positions": draw_positions(jax.random.fold_in(splits[11], 71), 0),
        "point_feat": centred(splits[1], (C, NPTS), 0.3, 1.8, ((1, 32),), jnp.float32),
        "area": jnp.clip(jnp.exp(math.log(3.0) - 2.3025851 * jax.random.uniform(splits[2], (NPTS,), jnp.float32) ** block_levels(splits[2], (NPTS,), ((0, 32),), -0.2, 0.2)), 0.3, 3.0),
        "block_brick": draw_block_brick(jax.random.fold_in(splits[11], 71), 0),
        "block_count": draw_block_count(jax.random.fold_in(splits[11], 71), 0),
        "sdf": centred(splits[5], (G, G, G), 1.0, 6.0, ((0, 4), (1, 8)), jnp.float32),
        "grid_gain": centred(splits[6], (C,), 1.0, 4.0, (), jnp.float32),
        "mix_w": centred(splits[7], (LAYERS, C, C), C ** -0.5, 1.0, (), jnp.float32),
        "mix_b": centred(splits[8], (LAYERS, C), 0.3, 1.8, (), jnp.float32),
        "spec_w": centred(splits[9], (LAYERS, 2, KZ, C, M * M), 3.0, 18.0, ((2, 8), (3, 4)), jnp.float32),
        "readout_w": centred(splits[10], (C,), C ** -0.5, 1.0, (), jnp.float32),
    }


highest = lax.Precision.HIGHEST


def cell_offsets(brick_edge):
    cell_index = jnp.arange(brick_edge * brick_edge * brick_edge, dtype=jnp.int32)
    coords = jnp.stack([cell_index // (brick_edge * brick_edge), (cell_index // brick_edge) % brick_edge, cell_index % brick_edge])
    return coords.astype(jnp.float32) + 0.5


def kernel_weights(corners, points, offsets, radius):
    distance = jnp.zeros((corners.shape[0], offsets.shape[1], points.shape[2]), dtype=points.dtype)
    for axis_id in range(3):
        centre_line = corners[:, axis_id][:, None] + offsets[axis_id][None, :]
        gap_line = centre_line[:, :, None] - points[:, axis_id][:, None, :]
        distance = distance + gap_line * gap_line
    return jnp.square(jnp.maximum(1.0 - distance / (radius * radius), 0.0))


def spectral_channel(values, weights):
    half_modes = M // 2
    spectrum = jnp.fft.rfftn(values)
    spectrum = jnp.concatenate([spectrum[:half_modes], spectrum[G - half_modes:]], axis=0)
    spectrum = jnp.concatenate([spectrum[:, :half_modes], spectrum[:, G - half_modes:]], axis=1)
    spectrum = spectrum[:, :, :KZ]
    factor = (weights[0] + 1j * weights[1]).reshape(KZ, M, M).transpose(1, 2, 0)
    scaled = spectrum * factor
    padded = jnp.zeros((G, G, G // 2 + 1), dtype=scaled.dtype)
    padded = padded.at[:half_modes, :half_modes, :KZ].set(scaled[:half_modes, :half_modes])
    padded = padded.at[:half_modes, G - half_modes:, :KZ].set(scaled[:half_modes, half_modes:])
    padded = padded.at[G - half_modes:, :half_modes, :KZ].set(scaled[half_modes:, :half_modes])
    padded = padded.at[G - half_modes:, G - half_modes:, :KZ].set(scaled[half_modes:, half_modes:])
    return jnp.fft.irfftn(padded, s=(G, G, G))


def reference(positions, point_feat, area, block_brick, block_count, sdf, grid_gain, mix_w, mix_b, spec_w, readout_w):
    side_bricks = G // B
    cell_count = B * B * B
    block_index = jnp.arange(NBLK, dtype=jnp.int32)
    live_mask = (block_index % BLK_DEV) < block_count[block_index // BLK_DEV]
    live_scale = jnp.where(live_mask, 1.0, 0.0).astype(positions.dtype)
    brick_x = block_brick // (side_bricks * side_bricks)
    brick_y = (block_brick // side_bricks) % side_bricks
    brick_z = block_brick % side_bricks
    corners = jnp.stack([brick_x, brick_y, brick_z], axis=1).astype(positions.dtype) * B
    block_pos = positions.reshape(3, NBLK, PB).transpose(1, 0, 2)
    block_feat = point_feat.reshape(C, NBLK, PB).transpose(1, 0, 2) * area.reshape(NBLK, 1, PB)
    offsets = cell_offsets(B).astype(positions.dtype)
    group_count = NBLK // BLK_DEV
    grouped = (corners.reshape(group_count, BLK_DEV, 3), block_pos.reshape(group_count, BLK_DEV, 3, PB),
               block_feat.reshape(group_count, BLK_DEV, C, PB), block_brick.reshape(group_count, BLK_DEV),
               live_scale.reshape(group_count, BLK_DEV))

    def encode_step(bricks, group_items):
        corner_set, point_set, feature_set, brick_ids, scale_set = group_items
        weights = kernel_weights(corner_set, point_set, offsets, B)
        contrib = jnp.einsum("rcp,rgp->rcg", feature_set, weights, precision=highest) * scale_set[:, None, None]
        return bricks.at[brick_ids].add(contrib.reshape(BLK_DEV, C * cell_count)), None

    bricks = jnp.zeros((side_bricks ** 3, C * cell_count), dtype=positions.dtype)
    bricks, unused = lax.scan(encode_step, bricks, grouped)
    grid_field = bricks.reshape(side_bricks, side_bricks, side_bricks, C, B, B, B).transpose(3, 0, 4, 1, 5, 2, 6).reshape(C, G, G, G)
    grid_field = grid_field + grid_gain[:, None, None, None] * sdf[None]

    def channel_step(channel_items):
        return spectral_channel(channel_items[0], channel_items[1])

    for layer_index in range(LAYERS):
        per_channel = spec_w[layer_index].transpose(2, 0, 1, 3)
        spectral = lax.map(channel_step, (grid_field, per_channel))
        mixed_sum = jnp.einsum("oc,cxyz->oxyz", mix_w[layer_index], grid_field, precision=highest)
        mixed_sum = mixed_sum + mix_b[layer_index][:, None, None, None] + spectral
        grid_field = jax.nn.gelu(mixed_sum) if layer_index < LAYERS - 1 else mixed_sum

    final_bricks = grid_field.reshape(C, side_bricks, B, side_bricks, B, side_bricks, B).transpose(1, 3, 5, 0, 2, 4, 6)
    final_bricks = final_bricks.reshape(side_bricks ** 3, C * cell_count)

    def decode_group(group_items):
        corner_set, point_set, brick_ids = group_items
        weights = kernel_weights(corner_set, point_set, offsets, B)
        brick_vals = final_bricks[brick_ids].reshape(BLK_DEV, C, cell_count)
        decoded = jnp.einsum("rcg,rgp->rcp", brick_vals, weights, precision=highest) / jnp.sum(weights, axis=1)[:, None, :]
        return jnp.einsum("c,rcp->rp", readout_w, decoded, precision=highest)

    pressure = lax.map(decode_group, (grouped[0], grouped[1], grouped[3])).reshape(NBLK, PB)
    return jnp.where(live_mask[:, None], pressure, 0.0).reshape(NPTS)
```

```python
import functools
import math

import jax
import jax.numpy as jnp
import ml_dtypes
import numpy as np
from jax import lax
from jax.experimental import pallas as pl
from jax.experimental.pallas import tpu as pltpu
from jax.sharding import PartitionSpec as P

B = 8
BF = jnp.bfloat16
F32 = jnp.float32
VM = pl.BlockSpec(memory_space=pltpu.VMEM)
SM = pl.BlockSpec(memory_space=pltpu.SMEM)
LIMIT = 56 * 1024 * 1024


def split(x):
    hi = x.astype(BF)
    lo = (x - hi.astype(F32)).astype(BF)
    return hi, lo


def np_split(table):
    table = np.asarray(table, np.float64).astype(np.float32)
    hi = table.astype(ml_dtypes.bfloat16)
    lo = (table - hi.astype(np.float32)).astype(ml_dtypes.bfloat16)
    return hi, lo


def dot(a, b, contract=((1,), (0,))):
    return lax.dot_general(a, b, (contract, ((), ())), preferred_element_type=F32)


NT = ((1,), (1,))


def call(body, name, out_shape, in_specs, out_specs, flops, moved, grid=None, scratch=(), aliases=None):
    extra = {} if grid is None else {"grid": grid}
    return pl.pallas_call(
        body,
        name=name,
        out_shape=out_shape,
        in_specs=in_specs,
        out_specs=out_specs,
        scratch_shapes=list(scratch),
        input_output_aliases=aliases or {},
        compiler_params=pltpu.CompilerParams(vmem_limit_bytes=LIMIT),
        cost_estimate=pl.CostEstimate(flops=int(flops), bytes_accessed=int(moved), transcendentals=0),
        **extra,
    )


class Sizes:
    def __init__(self, nx, ny, grid, channels, modes, kz):
        self.nx, self.ny, self.G, self.C, self.M, self.KZ = nx, ny, grid, channels, modes, kz
        self.NB = grid // B
        self.bxn = self.NB // nx
        self.byn = self.NB // ny
        self.Xl = grid // nx
        self.Yl = grid // ny
        self.cp = channels // nx
        self.KL = kz // ny
        self.L = channels * self.bxn
        self.LY = self.Yl * self.cp
        self.LK = 2 * self.KL * modes
        self.K2 = 2 * kz
        self.LB = self.NB * self.bxn * self.byn
        self.freq = np.where(np.arange(modes) < modes // 2, np.arange(modes), np.arange(modes) - modes)


def trig(s, places, freqs):
    angle = (np.asarray(places)[:, None] * np.asarray(freqs)[None, :]) % s.G * (2.0 * np.pi / s.G)
    return np.cos(angle), np.sin(angle)


def stack_left(table):
    hi, lo = np_split(table)
    zero = np.zeros_like(lo)
    return np.concatenate([np.concatenate([hi, hi], 1), np.concatenate([lo, zero], 1)], 0)


def wide_left(table):
    hi, lo = np_split(table)
    return np.concatenate([hi, hi, lo], 1)


def make_tables(s):
    t = {}
    c, n = trig(s, np.arange(s.KZ), np.arange(s.G))
    t["z_fwd"] = stack_left(np.concatenate([c, -n], 0))
    back = np.where(np.arange(s.KZ) == 0, 1.0, 2.0)[None, :] / s.G
    c, n = trig(s, np.arange(s.G), np.arange(s.KZ))
    t["z_inv"] = wide_left(np.concatenate([c * back, -n * back], 1))
    order = np.arange(s.G).reshape(s.nx, s.bxn, B).transpose(0, 2, 1).reshape(-1)
    c, n = trig(s, s.freq, order)
    hi, lo = np_split(np.concatenate([np.concatenate([c, n], 1), np.concatenate([-n, c], 1)], 0))
    t["x_fwd"] = np.concatenate([hi, lo], 0)
    c, n = trig(s, s.freq, np.arange(s.G))
    t["y_fwd"] = stack_left(np.concatenate([c, n], 0))
    t["y_inv"] = wide_left(np.concatenate([c.T, n.T], 1) / s.G)
    c, n = trig(s, order, s.freq)
    table = np.zeros((s.KL, 2, s.G, 2, s.KL, s.M))
    for k in range(s.KL):
        table[k, 0, :, 0, k], table[k, 0, :, 1, k] = c, -n
        table[k, 1, :, 0, k], table[k, 1, :, 1, k] = n, c
    t["x_inv"] = wide_left(table.reshape(2 * s.KL * s.G, s.LK) / s.G)
    xs = (np.arange(s.bxn)[:, None] * B + np.arange(B)[None, :]).T.reshape(B, 1, s.bxn, 1)
    ys = (np.arange(s.byn)[:, None] * B + np.arange(B)[None, :]).T.reshape(1, B, 1, s.byn)
    full = (B, B, s.bxn, s.byn)
    xs, ys = np.broadcast_to(xs, full).reshape(-1), np.broadcast_to(ys, full).reshape(-1)
    turn = s.freq[None, :, None] * xs[None, None, :] + s.freq[:, None, None] * ys[None, None, :]
    angle = (turn % s.G).reshape(s.M * s.M, -1) * (2.0 * np.pi / s.G)
    t["xy_hi"], t["xy_lo"] = np_split(np.concatenate([np.cos(angle), np.sin(angle)], 0) / (s.G * s.G))
    return t


def block_turn(tiles, blocks, width):
    count = len(tiles)
    if count == blocks and count * width == 128:
        lane = lax.broadcasted_iota(jnp.int32, tiles[0].shape, 1) // width
        tiles = list(tiles)
        step = 1
        while step < count:
            upper = (lane & step) != 0
            for i in range(count):
                if i & step == 0:
                    a, b = tiles[i], tiles[i | step]
                    up = pltpu.roll(b, step * width, 1)
                    down = pltpu.roll(a, 128 - step * width, 1)
                    tiles[i] = jnp.where(upper, up, a)
                    tiles[i | step] = jnp.where(upper, b, down)
            step *= 2
        return tiles
    return [
        jnp.concatenate([tile[:, b * width : (b + 1) * width] for tile in tiles], axis=1)
        for b in range(blocks)
    ]


def swap_halves(x):
    half = x.shape[1] // 2
    if x.shape[1] == 128:
        return pltpu.roll(x, half, 1)
    return jnp.concatenate([x[:, half:], x[:, :half]], axis=1)


def half_signs(rows, width, first):
    lane = lax.broadcasted_iota(jnp.int32, (rows, width), 1)
    return jnp.where(lane < width // 2, first, -first).astype(F32)


def pack_kernel(s, cap, brick_ref, count_ref, pos_ref, feat_ref, area_ref, out_ref, slot_ref, fill_ref):
    blocks = brick_ref.shape[0]
    C = s.C
    for i in range(s.ny):
        fill_ref[i] = 0
        out_ref[i] = jnp.full(out_ref.shape[1:], -1.0, F32)
    live = count_ref[0]

    def step(n, carry):
        @pl.when(n < live)
        def _():
            brick = brick_ref[n]
            dest = (brick // s.NB) % s.NB // s.byn
            order = fill_ref[dest]
            fill_ref[dest] = order + 1
            slot_ref[n] = dest * cap + order
            lanes = pl.ds(pl.multiple_of(n * 128, 128), 128)
            out_ref[dest, pl.ds(pl.multiple_of(order * C, 8), C), :] = feat_ref[:, lanes] * area_ref[pl.ds(n, 1), :]
            points = pos_ref[:, lanes]
            for d in range(3):
                out_ref[dest, pl.ds(cap * C + d * cap + order, 1), :] = points[d : d + 1, :]

        @pl.when(n >= live)
        def _():
            slot_ref[n] = -1

        return carry

    lax.fori_loop(0, blocks, step, 0)


def field_kernel(s, sdf_ref, gain_ref, out_ref):
    rows = sdf_ref[...].reshape(s.bxn * s.Yl, s.G).T
    hi, lo = split(rows)
    ghi, glo = split(gain_ref[...])
    wide = dot(hi, ghi) + dot(lo, ghi) + dot(hi, glo)
    for y in range(s.Yl):
        out_ref[0, y] = wide[:, y * s.L : (y + 1) * s.L]


def kernel_tiles(points):
    px, py, pz = points
    scale = 1.0 / B
    sub = lax.broadcasted_iota(jnp.int32, pz.shape, 0).astype(F32)
    gz = ((sub + 0.5) - pz) * scale
    gz = gz * gz
    gx = []
    gy = []
    for a in range(B):
        d = (px - (a + 0.5)) * scale
        gx.append(1.0 - d * d)
        d = (py - (a + 0.5)) * scale
        gy.append(d * d + gz)
    tiles = []
    for a in range(B):
        for b in range(B):
            t = jnp.maximum(gx[a] - gy[b], 0.0)
            tiles.append(t * t)
    return tiles


def grid_to_spectrum(s, rows_of, table):
    tiles = []
    for y in range(0, s.Yl, 2):
        both = jnp.concatenate([rows_of(y), rows_of(y + 1)], axis=1)
        hi, lo = split(both)
        res = dot(table, jnp.concatenate([hi, lo], axis=0))
        res = res[: s.K2] + res[s.K2 :]
        tiles += [res[:, : s.L], res[:, s.L :]]
    return block_turn(tiles, s.nx * s.bxn, s.cp)


def encode_kernel(s, cap, id_ref, num_ref, in_ref, init_ref, table_ref, grid_ref, spec_ref):
    C = s.C
    for a in range(B):
        grid_ref[a] = init_ref[a]
    group = lax.broadcasted_iota(jnp.int32, (s.L, 128), 0) // s.cp % s.bxn

    def per_source(src, carry):
        def per_block(j, inner):
            slot = src * cap + j
            bx, by, bz = id_ref[0, slot], id_ref[1, slot], id_ref[2, slot]
            points = [
                jnp.broadcast_to(in_ref[src, pl.ds(cap * C + d * cap + j, 1), :], (8, 128))
                for d in range(3)
            ]
            points = [p - id_ref[3 + d, slot].astype(F32) for d, p in enumerate(points)]
            weights = jnp.concatenate(kernel_tiles(points), axis=0)
            feats = in_ref[src, pl.ds(pl.multiple_of(j * C, 8), C), :]
            spread = []
            for g in range(s.nx):
                spread += [feats[g * s.cp : (g + 1) * s.cp]] * s.bxn
            spread = jnp.where(group == bx, jnp.concatenate(spread, axis=0), 0.0)
            whi, wlo = split(weights)
            fhi, flo = split(spread)
            left = jnp.concatenate([whi, wlo], axis=1)
            right = jnp.concatenate([fhi, fhi], axis=1)
            if s.L == 128:
                under = jnp.concatenate([flo, jnp.zeros_like(flo)], axis=1)
                res = dot(left, jnp.concatenate([right, under], axis=0), NT)
                res = res[:, : s.L] + res[:, s.L :]
            else:
                res = dot(left, right, NT) + dot(whi, flo, NT)
            ys = pl.ds(pl.multiple_of(by * B, B), B)
            zs = pl.ds(pl.multiple_of(bz * B, B), B)
            grid_ref[:, ys, zs, :] = grid_ref[:, ys, zs, :] + res.reshape(B, B, B, s.L)
            return inner

        return lax.fori_loop(0, num_ref[src], per_block, carry)

    lax.fori_loop(0, s.ny, per_source, 0)

    def transform(a, carry):
        out = grid_to_spectrum(s, lambda y: grid_ref[a, y], table_ref[...])
        for g in range(s.nx):
            for b in range(s.bxn):
                spec_ref[g, a, b] = out[g * s.bxn + b]
        return carry

    lax.fori_loop(0, B, transform, 0)


def mixed_rows(rows, whi, wlo):
    hi, lo = split(rows)
    width = whi.shape[1]
    if width == 128 and rows.shape[1] == 128:
        left = jnp.concatenate([hi, lo], axis=1)
        right = jnp.concatenate(
            [jnp.concatenate([whi, wlo], axis=1), jnp.concatenate([whi, jnp.zeros_like(wlo)], axis=1)], axis=0
        )
        res = dot(left, right)
        return res[:, :128] + res[:, 128:]
    return dot(hi, whi) + dot(lo, whi) + dot(hi, wlo)


def mix_kernel(s, grid_ref, mix_ref, bias_ref, out_ref):
    whi, wlo = split(mix_ref[...])
    for y in range(s.Yl):
        out_ref[0, y] = mixed_rows(grid_ref[0, y], whi, wlo) + bias_ref[...]


def readout_kernel(s, grid_ref, mix_ref, out_ref):
    whi, wlo = split(mix_ref[...])
    lane = lax.broadcasted_iota(jnp.int32, (B, s.LB), 1)
    for a in range(B):
        total = jnp.zeros((B, s.LB), F32)
        for by in range(s.byn):
            res = mixed_rows(grid_ref[0, by * B + a], whi, wlo)
            for bz in range(s.NB):
                mine = (lane // (s.bxn * s.byn) == bz) & (lane % s.byn == by)
                total = jnp.where(mine, res[bz * B : (bz + 1) * B], total)
        out_ref[0, a * B : (a + 1) * B, :] = total


def x_forward_kernel(s, in_ref, table_ref, out_ref):
    M = s.M
    thi = table_ref[: 2 * M]
    for i in range(s.ny):
        parts = []
        for k in range(s.KL):
            kz = i * s.KL + k
            parts.append(
                jnp.concatenate(
                    [in_ref[pl.ds(kz, s.G, stride=s.K2), :], in_ref[pl.ds(s.KZ + kz, s.G, stride=s.K2), :]], axis=0
                )
            )
        hi, lo = split(jnp.concatenate(parts, axis=1))
        res = dot(table_ref[...], hi)
        res = res[: 2 * M] + res[2 * M :] + dot(thi, lo)
        rows = []
        for ri in range(2):
            for k in range(s.KL):
                rows.append(res[ri * M : (ri + 1) * M, k * s.LY : (k + 1) * s.LY])
        out_ref[i] = jnp.concatenate(rows, axis=0).T


def y_spectrum(s, in_ref, table, u_ref, v_ref, cs):
    M = s.M
    both = jnp.concatenate([in_ref[pl.ds(c, s.G, stride=s.cp), :] for c in cs], axis=1)
    hi, lo = split(both)
    res = dot(table, jnp.concatenate([hi, lo], axis=0))
    res = res[: 2 * M] + res[2 * M :]
    out = []
    plus = half_signs(M, s.LK, 1.0)
    for i, c in enumerate(cs):
        part = res[:, i * s.LK : (i + 1) * s.LK]
        wave = part[:M] + plus * swap_halves(part[M:])
        out.append(wave * u_ref[c] + swap_halves(wave) * v_ref[c])
    return out


def y_kernel(s, in_ref, fwd_ref, inv_ref, u_ref, v_ref, out_ref):
    minus = half_signs(s.M, s.LK, -1.0)
    for c in range(0, s.cp, 2):
        prods = y_spectrum(s, in_ref, fwd_ref[...], u_ref, v_ref, (c, c + 1))
        both = jnp.concatenate(
            [jnp.concatenate([p, minus * swap_halves(p)], axis=0) for p in prods], axis=1
        )
        hi, lo = split(both)
        res = dot(inv_ref[...], jnp.concatenate([hi, lo, hi], axis=0))
        for i in range(2):
            out_ref[pl.ds(c + i, s.G, stride=s.cp), :] = res[:, i * s.LK : (i + 1) * s.LK]


def y_last_kernel(s, in_ref, fwd_ref, u_ref, v_ref, out_ref):
    total = jnp.zeros((s.M, s.LK), F32)
    for c in range(0, s.cp, 2):
        prods = y_spectrum(s, in_ref, fwd_ref[...], u_ref, v_ref, (c, c + 1))
        total = total + prods[0] + prods[1]
    out_ref[...] = total


def x_inverse_kernel(s, in_ref, table_ref, out_ref):
    for i in range(s.ny):
        hi, lo = split(in_ref[i])
        if s.LK == 128:
            res = dot(table_ref[...], jnp.concatenate([hi, lo, hi], axis=1), NT)
        else:
            t = table_ref[...]
            res = dot(t[:, : s.LK], hi, NT) + dot(t[:, : s.LK], lo, NT) + dot(t[:, 2 * s.LK :], hi, NT)
        for k in range(s.KL):
            for ri in range(2):
                at = (k * 2 + ri) * s.G
                out_ref[pl.ds(ri * s.KZ + i * s.KL + k, s.G, stride=s.K2), :] = res[at : at + s.G]


def gelu(x):
    inner = math.sqrt(2.0 / math.pi) * (x + 0.044715 * (x * x * x))
    return 0.5 * x * (1.0 + jnp.tanh(inner))


def layer_kernel(s, mixed_ref, in_ref, inv_ref, fwd_ref, grid_ref, spec_ref):
    tiles = [in_ref[g, 0, b] for g in range(s.nx) for b in range(s.bxn)]
    tiles = block_turn(tiles, s.Yl, s.cp)
    for y in range(0, s.Yl, 2):
        hi, lo = split(jnp.concatenate([tiles[y], tiles[y + 1]], axis=1))
        res = dot(inv_ref[...], jnp.concatenate([hi, lo, hi], axis=0))
        for i in range(2):
            grid_ref[0, y + i] = gelu(mixed_ref[0, y + i] + res[:, i * s.L : (i + 1) * s.L])
    out = grid_to_spectrum(s, lambda y: grid_ref[0, y], fwd_ref[...])
    for g in range(s.nx):
        for b in range(s.bxn):
            spec_ref[g, 0, b] = out[g * s.bxn + b]


def decode_kernel(s, cap, id_ref, num_ref, base_ref, pos_ref, spec_ref, mix_ref, hi_ref, lo_ref, inv_ref, out_ref, s_ref):
    mhi, mlo = split(spec_ref[...])
    wave = dot(jnp.concatenate([mhi, mlo], axis=0), hi_ref[...])
    wave = wave[: s.K2] + wave[s.K2 :] + dot(mhi, lo_ref[...])
    hi, lo = split(wave)
    field = dot(inv_ref[...], jnp.concatenate([hi, lo, hi], axis=0))
    width = s.bxn * s.byn
    per = 128 // width
    for q in range(field.shape[1] // 128):
        tiles = [field[z * B : (z + 1) * B, q * 128 : (q + 1) * 128] for z in range(s.NB)]
        for i, tile in enumerate(block_turn(tiles, per, width)):
            at = (q * per + i) * B
            s_ref[at : at + B, :] = tile + mix_ref[at : at + B, :] + base_ref[0]
    out_ref[...] = jnp.zeros(out_ref.shape, F32)
    cell = lax.broadcasted_iota(jnp.int32, (s.LB, 128), 0)

    def per_source(src, carry):
        def per_pair(h, inner):
            shi, slo = split(s_ref[...])
            picks = []
            for i in range(2):
                j = h * 2 + i
                at = id_ref[6, src * cap + j]
                picks.append(jnp.where(cell == at, 1.0, 0.0).astype(BF))
            pick = jnp.concatenate(picks, axis=1)
            if s.LB == 128:
                vals = dot(jnp.concatenate([shi, slo], axis=1), jnp.concatenate([pick, pick], axis=0))
            else:
                vals = dot(shi, pick) + dot(slo, pick)
            for i in range(2):
                j = h * 2 + i
                slot = src * cap + j
                points = [
                    jnp.broadcast_to(pos_ref[src, pl.ds(d * cap + j, 1), :], (8, 128))
                    - id_ref[3 + d, slot].astype(F32)
                    for d in range(3)
                ]
                top = jnp.zeros((B, 128), F32)
                low = jnp.zeros((B, 128), F32)
                for n, tile in enumerate(kernel_tiles(points)):
                    top = top + tile * vals[n * B : (n + 1) * B, i * 128 : (i + 1) * 128]
                    low = low + tile
                top = jnp.sum(top, axis=0, keepdims=True)
                low = jnp.sum(low, axis=0, keepdims=True)
                out_ref[pl.ds(slot, 1), :] = top / jnp.where(low > 0.0, low, 1.0)
            return inner

        return lax.fori_loop(0, (num_ref[src] + 1) // 2, per_pair, carry)

    lax.fori_loop(0, s.ny, per_source, 0)


def per_device(
    positions,
    point_feat,
    area,
    block_brick,
    block_count,
    sdf,
    grid_gain,
    mix_w,
    mix_b,
    spec_w,
    readout_w,
):
    nx, ny = lax.axis_size("gx"), lax.axis_size("gy")
    row_x, row_y = lax.axis_index("gx"), lax.axis_index("gy")
    modes = math.isqrt(spec_w.shape[4])
    s = Sizes(nx, ny, sdf.shape[2], point_feat.shape[0], modes, spec_w.shape[2] * ny)
    t = {name: jnp.asarray(value) for name, value in make_tables(s).items()}
    shape = lambda *dims: jax.ShapeDtypeStruct(dims, F32)
    blocks = block_brick.shape[0]
    cap = blocks // ny
    PB = positions.shape[1] // blocks
    C, G, M, L = s.C, s.G, s.M, s.L
    rows = cap * (C + 3)

    outgoing, slot_of = call(
        functools.partial(pack_kernel, s, cap),
        "pack",
        (shape(ny, rows, PB), jax.ShapeDtypeStruct((blocks,), jnp.int32)),
        [SM, SM, VM, VM, VM],
        (VM, SM),
        1e6,
        6e6,
        scratch=[pltpu.SMEM((ny,), jnp.int32)],
    )(block_brick, block_count, positions, point_feat, area.reshape(blocks, PB))
    incoming = lax.all_to_all(outgoing, "gy", split_axis=0, concat_axis=0, tiled=True)
    in_pos = incoming[:, cap * C :, :]
    first = in_pos.reshape(ny, 3, cap, PB)[..., 0].transpose(1, 0, 2).reshape(3, ny * cap)
    counts = jnp.sum((first[0].reshape(ny, cap) >= 0.0).astype(jnp.int32), axis=1)
    brick = jnp.floor(first / B).astype(jnp.int32)
    start = jnp.stack([row_x * s.bxn, row_y * s.byn, jnp.zeros_like(row_x)])
    limit = jnp.array([s.bxn - 1, s.byn - 1, s.NB - 1], jnp.int32)
    local = jnp.clip(brick - start[:, None], 0, limit[:, None])
    corner = (local + start[:, None]) * B
    flat = local[2] * (s.bxn * s.byn) + local[0] * s.byn + local[1]
    ids = jnp.concatenate([local, corner, flat[None], flat[None]], axis=0)

    lane = jnp.arange(L)
    lane_bx = lane // s.cp % s.bxn
    lane_c = lane // (s.bxn * s.cp) * s.cp + lane % s.cp
    same_bx = lane_bx[:, None] == lane_bx[None, :]
    gain_l = grid_gain[lane_c]
    spread = (
        (jnp.arange(s.bxn)[:, None, None, None] == lane_bx[None, None, None, :])
        & (jnp.arange(s.Yl)[None, :, None, None] == jnp.arange(s.Yl)[None, None, :, None])
    )
    gains = jnp.where(spread, gain_l, 0.0).reshape(s.bxn * s.Yl, s.Yl * L)
    grid_shape = shape(B, s.Yl, G, L)
    grid_block = pl.BlockSpec((1, s.Yl, G, L), lambda a: (a, 0, 0, 0))
    whole = lambda array: pl.BlockSpec(array.shape, lambda a: (0,) * array.ndim)
    init = call(
        functools.partial(field_kernel, s),
        "field",
        grid_shape,
        [pl.BlockSpec((s.bxn, None, s.Yl, G), lambda a: (0, a, 0, 0)), whole(gains)],
        grid_block,
        3e9,
        1e7,
        grid=(B,),
    )(sdf.reshape(s.bxn, B, s.Yl, G), gains)

    mixing = jnp.where(same_bx, mix_w[0][lane_c[None, :], lane_c[:, None]], 0.0)
    bias = mix_b[0][lane_c][None, :]
    read_mix = jnp.sum(readout_w[:, None] * mix_w[1], axis=0)
    base = jnp.sum(readout_w * mix_b[1]).reshape(1)
    out_lane = jnp.arange(s.LB)
    reading = jnp.where(lane_bx[:, None] == out_lane[None, :] // s.byn % s.bxn, read_mix[lane_c][:, None], 0.0)
    mine = lax.dynamic_slice_in_dim(readout_w, row_x * s.cp, s.cp)

    def multipliers(w, scale):
        w = w.reshape(2, s.KL, s.cp, M, M)
        if scale is not None:
            w = w * scale[None, None, :, None, None]
        w = w.transpose(2, 4, 0, 1, 3)
        u = jnp.concatenate([w[:, :, 0:1], w[:, :, 0:1]], axis=2).reshape(s.cp, M, s.LK)
        v = jnp.concatenate([-w[:, :, 1:2], w[:, :, 1:2]], axis=2).reshape(s.cp, M, s.LK)
        return u, v

    u0, v0 = multipliers(spec_w[0], None)
    u1, v1 = multipliers(spec_w[1], mine)

    spec_shape = shape(nx, B, s.bxn, s.K2, s.LY)
    grid0, spec = call(
        functools.partial(encode_kernel, s, cap),
        "encode",
        (grid_shape, spec_shape),
        [SM, SM, VM, VM, VM],
        (VM, VM),
        4e9,
        2.2e7,
    )(ids, counts, incoming, init, t["z_fwd"])

    def to_modes(spec):
        spec = spec.reshape(nx, B * s.bxn * s.K2, s.LY)
        spec = lax.all_to_all(spec, "gx", split_axis=0, concat_axis=0, tiled=True)
        spec = call(
            functools.partial(x_forward_kernel, s),
            "x_forward",
            shape(ny, s.LY, s.LK),
            [VM, VM],
            VM,
            1e9,
            3e6,
        )(spec.reshape(G * s.K2, s.LY), t["x_fwd"])
        spec = lax.all_to_all(spec, "gy", split_axis=0, concat_axis=0, tiled=True)
        return spec.reshape(G * s.cp, s.LK)

    spec = to_modes(spec)
    mixed = call(
        functools.partial(mix_kernel, s),
        "mix",
        grid_shape,
        [grid_block, whole(mixing), whole(bias)],
        grid_block,
        2e9,
        1.7e7,
        grid=(B,),
    )(grid0, mixing, bias)
    spec = call(
        functools.partial(y_kernel, s), "y_both", shape(G * s.cp, s.LK), [VM] * 5, VM, 1e9, 2e6
    )(spec, t["y_fwd"], t["y_inv"], u0, v0)
    spec = lax.all_to_all(spec.reshape(ny, s.LY, s.LK), "gy", split_axis=0, concat_axis=0, tiled=True)
    spec = call(
        functools.partial(x_inverse_kernel, s), "x_inverse", shape(G * s.K2, s.LY), [VM, VM], VM, 1e9, 3e6
    )(spec, t["x_inv"])
    spec = lax.all_to_all(
        spec.reshape(nx, B * s.bxn * s.K2, s.LY), "gx", split_axis=0, concat_axis=0, tiled=True
    ).reshape(nx, B, s.bxn, s.K2, s.LY)
    spec_block = pl.BlockSpec((nx, 1, s.bxn, s.K2, s.LY), lambda a: (0, a, 0, 0, 0))
    grid1, spec = call(
        functools.partial(layer_kernel, s),
        "layer",
        (grid_shape, spec_shape),
        [grid_block, spec_block, whole(t["z_inv"]), whole(t["z_fwd"])],
        (grid_block, spec_block),
        4e9,
        2.1e7,
        grid=(B,),
    )(mixed, spec, t["z_inv"], t["z_fwd"])
    spec = to_modes(spec)
    read = call(
        functools.partial(readout_kernel, s),
        "readout",
        shape(B, B * B, s.LB),
        [grid_block, whole(reading)],
        pl.BlockSpec((1, B * B, s.LB), lambda a: (a, 0, 0)),
        2e9,
        9e6,
        grid=(B,),
    )(grid1, reading)
    last = call(
        functools.partial(y_last_kernel, s), "y_last", shape(M, s.LK), [VM] * 4, VM, 1e9, 1e6
    )(spec, t["y_fwd"], u1, v1)

    last = lax.all_gather(last, ("gx", "gy"), axis=0, tiled=False)
    last = jnp.sum(last.reshape(nx, ny, M, 2, s.KL, M), axis=0)
    last = last.transpose(2, 0, 3, 1, 4).reshape(2, s.KZ, M * M)
    freq = jnp.asarray(s.freq, jnp.int32)
    turn = jnp.mod(freq[None, :] * (row_x * s.Xl) + freq[:, None] * (row_y * s.Yl), G).reshape(-1)
    angle = turn.astype(F32) * (2.0 * math.pi / G)
    cos, sin = jnp.cos(angle), jnp.sin(angle)
    real = last[0] * cos - last[1] * sin
    imag = last[1] * cos + last[0] * sin
    left = jnp.concatenate(
        [jnp.concatenate([real, -imag], axis=1), jnp.concatenate([imag, real], axis=1)], axis=0
    )
    values = call(
        functools.partial(decode_kernel, s, cap),
        "decode",
        shape(ny * cap, PB),
        [SM, SM, SM] + [VM] * 6,
        VM,
        4e9,
        6e6,
        scratch=[pltpu.VMEM((B * B * B, s.LB), F32)],
    )(ids, counts, base, in_pos, left, read.reshape(B * B * B, s.LB), t["xy_hi"], t["xy_lo"], t["z_inv"])
    returned = lax.all_to_all(values.reshape(ny, cap, PB), "gy", split_axis=0, concat_axis=0, tiled=True)
    choose = (slot_of[:, None] == jnp.arange(ny * cap, dtype=jnp.int32)[None, :]).astype(F32)
    pressure = jnp.dot(choose, returned.reshape(ny * cap, PB), precision=lax.Precision.HIGHEST)
    return pressure.reshape(blocks * PB)


def solution(mesh):
    placed = (
        P(None, ("gx", "gy")),
        P(None, ("gx", "gy")),
        P(("gx", "gy")),
        P(("gx", "gy")),
        P(("gx", "gy")),
        P("gx", "gy", None),
        P(),
        P(),
        P(),
        P(None, None, "gy", "gx", None),
        P(),
    )
    return jax.shard_map(
        per_device, mesh=mesh, in_specs=placed, out_specs=P(("gx", "gy")), check_vma=False
    )
```

```python
import functools
import math

import jax
import jax.numpy as jnp
import ml_dtypes
import numpy as np
from jax import lax
from jax.experimental import pallas as pl
from jax.experimental.pallas import tpu as pltpu
from jax.sharding import PartitionSpec as P

B = 8
BF = jnp.bfloat16
F32 = jnp.float32
VM = pl.BlockSpec(memory_space=pltpu.VMEM)
SM = pl.BlockSpec(memory_space=pltpu.SMEM)
LIMIT = 32 * 1024 * 1024


def split(x):
    hi = x.astype(BF)
    lo = (x - hi.astype(F32)).astype(BF)
    return hi, lo


def np_split(table):
    table = np.asarray(table, np.float64).astype(np.float32)
    hi = table.astype(ml_dtypes.bfloat16)
    lo = (table - hi.astype(np.float32)).astype(ml_dtypes.bfloat16)
    return hi, lo


def dot(a, b, contract=((1,), (0,))):
    return lax.dot_general(a, b, (contract, ((), ())), preferred_element_type=F32)


NT = ((1,), (1,))


def call(body, name, out_shape, in_specs, out_specs, flops, moved, grid=None, scratch=(), aliases=None):
    extra = {} if grid is None else {"grid": grid}
    return pl.pallas_call(
        body,
        name=name,
        out_shape=out_shape,
        in_specs=in_specs,
        out_specs=out_specs,
        scratch_shapes=list(scratch),
        input_output_aliases=aliases or {},
        compiler_params=pltpu.CompilerParams(vmem_limit_bytes=LIMIT),
        cost_estimate=pl.CostEstimate(flops=int(flops), bytes_accessed=int(moved), transcendentals=0),
        **extra,
    )


class Sizes:
    def __init__(self, nx, ny, grid, channels, modes, kz):
        self.nx, self.ny, self.G, self.C, self.M, self.KZ = nx, ny, grid, channels, modes, kz
        self.NB = grid // B
        self.bxn = self.NB // nx
        self.byn = self.NB // ny
        self.Xl = grid // nx
        self.Yl = grid // ny
        self.cp = channels // nx
        self.KL = kz // ny
        self.L = channels * self.bxn
        self.LY = self.Yl * self.cp
        self.LK = 2 * self.KL * modes
        self.K2 = 2 * kz
        self.LB = self.NB * self.bxn * self.byn
        self.freq = np.where(np.arange(modes) < modes // 2, np.arange(modes), np.arange(modes) - modes)


def trig(s, places, freqs):
    angle = (np.asarray(places)[:, None] * np.asarray(freqs)[None, :]) % s.G * (2.0 * np.pi / s.G)
    return np.cos(angle), np.sin(angle)


def stack_left(table):
    hi, lo = np_split(table)
    zero = np.zeros_like(lo)
    return np.concatenate([np.concatenate([hi, hi], 1), np.concatenate([lo, zero], 1)], 0)


def wide_left(table):
    hi, lo = np_split(table)
    return np.concatenate([hi, hi, lo], 1)


def make_tables(s):
    t = {}
    c, n = trig(s, np.arange(s.KZ), np.arange(s.G))
    t["z_fwd"] = stack_left(np.concatenate([c, -n], 0))
    back = np.where(np.arange(s.KZ) == 0, 1.0, 2.0)[None, :] / s.G
    c, n = trig(s, np.arange(s.G), np.arange(s.KZ))
    c, n = c * back, -n * back
    t["z_inv"] = wide_left(np.concatenate([c, n], 1))
    t["z_last"] = wide_left(np.stack([c.reshape(s.G, s.ny, s.KL), n.reshape(s.G, s.ny, s.KL)], 2).reshape(s.G, -1))
    order = np.arange(s.G).reshape(s.nx, s.bxn, B).transpose(0, 2, 1).reshape(-1)
    c, n = trig(s, s.freq, order)
    hi, lo = np_split(np.concatenate([np.concatenate([c, n], 1), np.concatenate([-n, c], 1)], 0))
    t["x_fwd"] = np.concatenate([hi, lo], 0)
    c, n = trig(s, s.freq, np.arange(s.G))
    t["y_fwd"] = stack_left(np.concatenate([c, n], 0))
    t["y_inv"] = wide_left(np.concatenate([c.T, n.T], 1) / s.G)
    c, n = trig(s, order, s.freq)
    table = np.zeros((s.KL, 2, s.G, 2, s.KL, s.M))
    for k in range(s.KL):
        table[k, 0, :, 0, k], table[k, 0, :, 1, k] = c, -n
        table[k, 1, :, 0, k], table[k, 1, :, 1, k] = n, c
    t["x_inv"] = wide_left(table.reshape(2 * s.KL * s.G, s.LK) / s.G)
    xs = (np.arange(s.bxn)[:, None] * B + np.arange(B)[None, :]).T.reshape(B, 1, s.bxn, 1)
    ys = (np.arange(s.byn)[:, None] * B + np.arange(B)[None, :]).T.reshape(1, B, 1, s.byn)
    full = (B, B, s.bxn, s.byn)
    xs, ys = np.broadcast_to(xs, full).reshape(-1), np.broadcast_to(ys, full).reshape(-1)
    turn = s.freq[None, :, None] * xs[None, None, :] + s.freq[:, None, None] * ys[None, None, :]
    angle = (turn % s.G).reshape(s.M * s.M, -1) * (2.0 * np.pi / s.G)
    t["xy_hi"], t["xy_lo"] = np_split(np.concatenate([np.cos(angle), np.sin(angle)], 0) / (s.G * s.G))
    return t


def block_turn(tiles, blocks, width):
    count = len(tiles)
    if count == blocks and count * width == 128:
        lane = lax.broadcasted_iota(jnp.int32, tiles[0].shape, 1) // width
        tiles = list(tiles)
        step = 1
        while step < count:
            upper = (lane & step) != 0
            for i in range(count):
                if i & step == 0:
                    a, b = tiles[i], tiles[i | step]
                    up = pltpu.roll(b, step * width, 1)
                    down = pltpu.roll(a, 128 - step * width, 1)
                    tiles[i] = jnp.where(upper, up, a)
                    tiles[i | step] = jnp.where(upper, b, down)
            step *= 2
        return tiles
    return [
        jnp.concatenate([tile[:, b * width : (b + 1) * width] for tile in tiles], axis=1)
        for b in range(blocks)
    ]


def swap_halves(x):
    half = x.shape[1] // 2
    if x.shape[1] == 128:
        return pltpu.roll(x, half, 1)
    return jnp.concatenate([x[:, half:], x[:, :half]], axis=1)


def half_signs(rows, width, first):
    lane = lax.broadcasted_iota(jnp.int32, (rows, width), 1)
    return jnp.where(lane < width // 2, first, -first).astype(F32)


def pack_kernel(s, cap, brick_ref, count_ref, pos_ref, feat_ref, area_ref, out_ref, slot_ref, fill_ref):
    blocks = brick_ref.shape[0]
    C = s.C
    for i in range(s.ny):
        fill_ref[i] = 0
        out_ref[i] = jnp.full(out_ref.shape[1:], -1.0, F32)
    live = count_ref[0]

    def step(n, carry):
        @pl.when(n < live)
        def _():
            brick = brick_ref[n]
            dest = (brick // s.NB) % s.NB // s.byn
            order = fill_ref[dest]
            fill_ref[dest] = order + 1
            slot_ref[n] = dest * cap + order
            lanes = pl.ds(pl.multiple_of(n * 128, 128), 128)
            out_ref[dest, pl.ds(pl.multiple_of(order * C, 8), C), :] = feat_ref[:, lanes] * area_ref[pl.ds(n, 1), :]
            points = pos_ref[:, lanes]
            for d in range(3):
                out_ref[dest, pl.ds(cap * C + d * cap + order, 1), :] = points[d : d + 1, :]

        @pl.when(n >= live)
        def _():
            slot_ref[n] = -1

        return carry

    lax.fori_loop(0, blocks, step, 0)


def field_kernel(s, sdf_ref, gain_ref, out_ref):
    rows = sdf_ref[...].reshape(s.bxn * s.Yl, s.G).T
    hi, lo = split(rows)
    ghi, glo = split(gain_ref[...])
    wide = dot(hi, ghi) + dot(lo, ghi) + dot(hi, glo)
    for y in range(s.Yl):
        out_ref[0, y] = wide[:, y * s.L : (y + 1) * s.L]


def kernel_tiles(points):
    px, py, pz = points
    scale = 1.0 / B
    sub = lax.broadcasted_iota(jnp.int32, pz.shape, 0).astype(F32)
    gz = ((sub + 0.5) - pz) * scale
    gz = gz * gz
    gx = []
    gy = []
    for a in range(B):
        d = (px - (a + 0.5)) * scale
        gx.append(1.0 - d * d)
        d = (py - (a + 0.5)) * scale
        gy.append(d * d + gz)
    tiles = []
    for a in range(B):
        for b in range(B):
            t = jnp.maximum(gx[a] - gy[b], 0.0)
            tiles.append(t * t)
    return tiles


def grid_to_spectrum(s, rows_of, table):
    tiles = []
    for y in range(0, s.Yl, 2):
        both = jnp.concatenate([rows_of(y), rows_of(y + 1)], axis=1)
        hi, lo = split(both)
        res = dot(table, jnp.concatenate([hi, lo], axis=0))
        res = res[: s.K2] + res[s.K2 :]
        tiles += [res[:, : s.L], res[:, s.L :]]
    return block_turn(tiles, s.nx * s.bxn, s.cp)


def encode_kernel(s, cap, id_ref, num_ref, in_ref, init_ref, table_ref, grid_ref, spec_ref):
    C = s.C
    for a in range(B):
        grid_ref[a] = init_ref[a]
    group = lax.broadcasted_iota(jnp.int32, (s.L, 128), 0) // s.cp % s.bxn

    def per_source(src, carry):
        def per_pair(h, inner):
            results = []
            for i in range(2):
                j = h * 2 + i
                slot = src * cap + j
                points = [
                    jnp.broadcast_to(in_ref[src, pl.ds(cap * C + d * cap + j, 1), :], (8, 128))
                    - id_ref[3 + d, slot].astype(F32)
                    for d in range(3)
                ]
                weights = jnp.concatenate(kernel_tiles(points), axis=0)
                feats = in_ref[src, pl.ds(pl.multiple_of(j * C, 8), C), :]
                spread = []
                for g in range(s.nx):
                    spread += [feats[g * s.cp : (g + 1) * s.cp]] * s.bxn
                spread = jnp.where(group == id_ref[0, slot], jnp.concatenate(spread, axis=0), 0.0)
                whi, wlo = split(weights)
                fhi, flo = split(spread)
                left = jnp.concatenate([whi, wlo], axis=1)
                right = jnp.concatenate([fhi, fhi], axis=1)
                if s.L == 128:
                    under = jnp.concatenate([flo, jnp.zeros_like(flo)], axis=1)
                    res = dot(left, jnp.concatenate([right, under], axis=0), NT)
                    res = res[:, : s.L] + res[:, s.L :]
                else:
                    res = dot(left, right, NT) + dot(whi, flo, NT)
                results.append(res.reshape(B, B, B, s.L))
            for i in range(2):
                slot = src * cap + h * 2 + i
                ys = pl.ds(pl.multiple_of(id_ref[1, slot] * B, B), B)
                zs = pl.ds(pl.multiple_of(id_ref[2, slot] * B, B), B)
                grid_ref[:, ys, zs, :] = grid_ref[:, ys, zs, :] + results[i]
            return inner

        return lax.fori_loop(0, (num_ref[src] + 1) // 2, per_pair, carry)

    lax.fori_loop(0, s.ny, per_source, 0)

    def transform(a, carry):
        out = grid_to_spectrum(s, lambda y: grid_ref[a, y], table_ref[...])
        for g in range(s.nx):
            for b in range(s.bxn):
                spec_ref[g, a, b] = out[g * s.bxn + b]
        return carry

    lax.fori_loop(0, B, transform, 0)


def mixed_rows(rows, whi, wlo):
    hi, lo = split(rows)
    width = whi.shape[1]
    if width == 128 and rows.shape[1] == 128:
        left = jnp.concatenate([hi, lo], axis=1)
        right = jnp.concatenate(
            [jnp.concatenate([whi, wlo], axis=1), jnp.concatenate([whi, jnp.zeros_like(wlo)], axis=1)], axis=0
        )
        res = dot(left, right)
        return res[:, :128] + res[:, 128:]
    return dot(hi, whi) + dot(lo, whi) + dot(hi, wlo)


def mix_kernel(s, grid_ref, mix_ref, bias_ref, out_ref):
    whi, wlo = split(mix_ref[...])
    for y in range(s.Yl):
        out_ref[0, y] = mixed_rows(grid_ref[0, y], whi, wlo) + bias_ref[...]


def readout_kernel(s, grid_ref, mix_ref, out_ref):
    whi, wlo = split(mix_ref[...])
    lane = lax.broadcasted_iota(jnp.int32, (B, s.LB), 1)
    for a in range(B):
        total = jnp.zeros((B, s.LB), F32)
        for by in range(s.byn):
            res = mixed_rows(grid_ref[0, by * B + a], whi, wlo)
            for bz in range(s.NB):
                mine = (lane // (s.bxn * s.byn) == bz) & (lane % s.byn == by)
                total = jnp.where(mine, res[bz * B : (bz + 1) * B], total)
        out_ref[0, a * B : (a + 1) * B, :] = total


def x_forward_kernel(s, in_ref, table_ref, out_ref):
    M = s.M
    thi = table_ref[: 2 * M]
    for i in range(s.ny):
        parts = []
        for k in range(s.KL):
            kz = i * s.KL + k
            parts.append(
                jnp.concatenate(
                    [in_ref[pl.ds(kz, s.G, stride=s.K2), :], in_ref[pl.ds(s.KZ + kz, s.G, stride=s.K2), :]], axis=0
                )
            )
        hi, lo = split(jnp.concatenate(parts, axis=1))
        res = dot(table_ref[...], hi)
        res = res[: 2 * M] + res[2 * M :] + dot(thi, lo)
        rows = []
        for ri in range(2):
            for k in range(s.KL):
                rows.append(res[ri * M : (ri + 1) * M, k * s.LY : (k + 1) * s.LY])
        out_ref[i] = jnp.concatenate(rows, axis=0).T


def y_spectrum(s, in_ref, table, u_ref, v_ref, cs):
    M = s.M
    both = jnp.concatenate([in_ref[pl.ds(c, s.G, stride=s.cp), :] for c in cs], axis=1)
    hi, lo = split(both)
    res = dot(table, jnp.concatenate([hi, lo], axis=0))
    res = res[: 2 * M] + res[2 * M :]
    out = []
    plus = half_signs(M, s.LK, 1.0)
    for i, c in enumerate(cs):
        part = res[:, i * s.LK : (i + 1) * s.LK]
        wave = part[:M] + plus * swap_halves(part[M:])
        out.append(wave * u_ref[c] + swap_halves(wave) * v_ref[c])
    return out


def y_kernel(s, in_ref, fwd_ref, inv_ref, u_ref, v_ref, out_ref):
    minus = half_signs(s.M, s.LK, -1.0)
    for c in range(0, s.cp, 2):
        prods = y_spectrum(s, in_ref, fwd_ref[...], u_ref, v_ref, (c, c + 1))
        both = jnp.concatenate(
            [jnp.concatenate([p, minus * swap_halves(p)], axis=0) for p in prods], axis=1
        )
        hi, lo = split(both)
        res = dot(inv_ref[...], jnp.concatenate([hi, lo, hi], axis=0))
        for i in range(2):
            out_ref[pl.ds(c + i, s.G, stride=s.cp), :] = res[:, i * s.LK : (i + 1) * s.LK]


def y_last_kernel(s, in_ref, fwd_ref, u_ref, v_ref, out_ref):
    total = jnp.zeros((s.M, s.LK), F32)
    for c in range(0, s.cp, 2):
        prods = y_spectrum(s, in_ref, fwd_ref[...], u_ref, v_ref, (c, c + 1))
        total = total + prods[0] + prods[1]
    M = s.M
    for r in range(2 * s.KL):
        part = total[:, r * M : (r + 1) * M]
        out_ref[r : r + 1, :] = jnp.concatenate([part[m : m + 1] for m in range(M)], axis=1)


def x_inverse_kernel(s, in_ref, table_ref, out_ref):
    for i in range(s.ny):
        hi, lo = split(in_ref[i])
        if s.LK == 128:
            res = dot(table_ref[...], jnp.concatenate([hi, lo, hi], axis=1), NT)
        else:
            t = table_ref[...]
            res = dot(t[:, : s.LK], hi, NT) + dot(t[:, : s.LK], lo, NT) + dot(t[:, 2 * s.LK :], hi, NT)
        for k in range(s.KL):
            for ri in range(2):
                at = (k * 2 + ri) * s.G
                out_ref[pl.ds(ri * s.KZ + i * s.KL + k, s.G, stride=s.K2), :] = res[at : at + s.G]


def gelu(x):
    inner = math.sqrt(2.0 / math.pi) * (x + 0.044715 * (x * x * x))
    return 0.5 * x * (1.0 + jnp.tanh(inner))


def layer_kernel(s, mixed_ref, in_ref, inv_ref, fwd_ref, grid_ref, spec_ref):
    tiles = [in_ref[g, 0, b] for g in range(s.nx) for b in range(s.bxn)]
    tiles = block_turn(tiles, s.Yl, s.cp)
    for y in range(0, s.Yl, 2):
        hi, lo = split(jnp.concatenate([tiles[y], tiles[y + 1]], axis=1))
        res = dot(inv_ref[...], jnp.concatenate([hi, lo, hi], axis=0))
        for i in range(2):
            grid_ref[0, y + i] = gelu(mixed_ref[0, y + i] + res[:, i * s.L : (i + 1) * s.L])
    out = grid_to_spectrum(s, lambda y: grid_ref[0, y], fwd_ref[...])
    for g in range(s.nx):
        for b in range(s.bxn):
            spec_ref[g, 0, b] = out[g * s.bxn + b]


def decode_kernel(s, cap, id_ref, num_ref, base_ref, pos_ref, spec_ref, turn_ref, mix_ref, hi_ref, lo_ref, inv_ref, out_ref, s_ref):
    modes = jnp.concatenate([spec_ref[i] for i in range(s.ny)], axis=0)
    real_row = lax.broadcasted_iota(jnp.int32, modes.shape, 0) // s.KL % 2 == 0

    def partner(x):
        return jnp.where(real_row, -pltpu.roll(x, s.K2 - s.KL, 0), pltpu.roll(x, s.KL, 0))

    modes = modes * turn_ref[0:1, :] + partner(modes) * turn_ref[1:2, :]
    mhi, mlo = split(jnp.concatenate([modes, partner(modes)], axis=1))
    wave = dot(jnp.concatenate([mhi, mlo], axis=0), hi_ref[...])
    wave = wave[: s.K2] + wave[s.K2 :] + dot(mhi, lo_ref[...])
    hi, lo = split(wave)
    field = dot(inv_ref[...], jnp.concatenate([hi, lo, hi], axis=0))
    width = s.bxn * s.byn
    per = 128 // width
    for q in range(field.shape[1] // 128):
        tiles = [field[z * B : (z + 1) * B, q * 128 : (q + 1) * 128] for z in range(s.NB)]
        for i, tile in enumerate(block_turn(tiles, per, width)):
            at = (q * per + i) * B
            s_ref[at : at + B, :] = tile + mix_ref[at : at + B, :] + base_ref[0]
    out_ref[...] = jnp.zeros(out_ref.shape, F32)
    cell = lax.broadcasted_iota(jnp.int32, (s.LB, 128), 0)

    def per_source(src, carry):
        def per_pair(h, inner):
            shi, slo = split(s_ref[...])
            picks = []
            for i in range(2):
                j = h * 2 + i
                at = id_ref[6, src * cap + j]
                picks.append(jnp.where(cell == at, 1.0, 0.0).astype(BF))
            pick = jnp.concatenate(picks, axis=1)
            if s.LB == 128:
                vals = dot(jnp.concatenate([shi, slo], axis=1), jnp.concatenate([pick, pick], axis=0))
            else:
                vals = dot(shi, pick) + dot(slo, pick)
            for i in range(2):
                j = h * 2 + i
                slot = src * cap + j
                points = [
                    jnp.broadcast_to(pos_ref[src, pl.ds(d * cap + j, 1), :], (8, 128))
                    - id_ref[3 + d, slot].astype(F32)
                    for d in range(3)
                ]
                top = jnp.zeros((B, 128), F32)
                low = jnp.zeros((B, 128), F32)
                for n, tile in enumerate(kernel_tiles(points)):
                    top = top + tile * vals[n * B : (n + 1) * B, i * 128 : (i + 1) * 128]
                    low = low + tile
                top = jnp.sum(top, axis=0, keepdims=True)
                low = jnp.sum(low, axis=0, keepdims=True)
                out_ref[pl.ds(slot, 1), :] = top / jnp.where(low > 0.0, low, 1.0)
            return inner

        return lax.fori_loop(0, (num_ref[src] + 1) // 2, per_pair, carry)

    lax.fori_loop(0, s.ny, per_source, 0)


def per_device(
    positions,
    point_feat,
    area,
    block_brick,
    block_count,
    sdf,
    grid_gain,
    mix_w,
    mix_b,
    spec_w,
    readout_w,
):
    nx, ny = lax.axis_size("gx"), lax.axis_size("gy")
    row_x, row_y = lax.axis_index("gx"), lax.axis_index("gy")
    modes = math.isqrt(spec_w.shape[4])
    s = Sizes(nx, ny, sdf.shape[2], point_feat.shape[0], modes, spec_w.shape[2] * ny)
    t = {name: jnp.asarray(value) for name, value in make_tables(s).items()}
    shape = lambda *dims: jax.ShapeDtypeStruct(dims, F32)
    blocks = block_brick.shape[0]
    cap = blocks // ny
    PB = positions.shape[1] // blocks
    C, G, M, L = s.C, s.G, s.M, s.L
    rows = cap * (C + 3)

    outgoing, slot_of = call(
        functools.partial(pack_kernel, s, cap),
        "pack",
        (shape(ny, rows, PB), jax.ShapeDtypeStruct((blocks,), jnp.int32)),
        [SM, SM, VM, VM, VM],
        (VM, SM),
        1e6,
        6e6,
        scratch=[pltpu.SMEM((ny,), jnp.int32)],
    )(block_brick, block_count, positions, point_feat, area.reshape(blocks, PB))
    incoming = lax.all_to_all(outgoing, "gy", split_axis=0, concat_axis=0, tiled=True)

    def placement(incoming):
        in_pos = incoming[:, cap * C :, :]
        first = in_pos.reshape(ny, 3, cap, PB)[..., 0].transpose(1, 0, 2).reshape(3, ny * cap)
        counts = jnp.sum((first[0].reshape(ny, cap) >= 0.0).astype(jnp.int32), axis=1)
        brick = jnp.floor(first / B).astype(jnp.int32)
        start = jnp.stack([row_x * s.bxn, row_y * s.byn, jnp.zeros_like(row_x)])
        limit = jnp.array([s.bxn - 1, s.byn - 1, s.NB - 1], jnp.int32)
        local = jnp.clip(brick - start[:, None], 0, limit[:, None])
        corner = (local + start[:, None]) * B
        flat = local[2] * (s.bxn * s.byn) + local[0] * s.byn + local[1]
        owned = jnp.where(first[0:1] >= 0.0, local[0:1], -1)
        ids = jnp.concatenate([owned, local[1:], corner, flat[None], flat[None]], axis=0)
        return ids, counts, in_pos

    lane = jnp.arange(L)
    lane_bx = lane // s.cp % s.bxn
    same_bx = lane_bx[:, None] == lane_bx[None, :]
    gain_l = jnp.broadcast_to(grid_gain.reshape(nx, 1, s.cp), (nx, s.bxn, s.cp)).reshape(L)
    spread = (
        (jnp.arange(s.bxn)[:, None, None, None] == lane_bx[None, None, None, :])
        & (jnp.arange(s.Yl)[None, :, None, None] == jnp.arange(s.Yl)[None, None, :, None])
    )
    gains = jnp.where(spread, gain_l, 0.0).reshape(s.bxn * s.Yl, s.Yl * L)
    grid_shape = shape(B, s.Yl, G, L)
    grid_block = pl.BlockSpec((1, s.Yl, G, L), lambda a: (a, 0, 0, 0))
    whole = lambda array: pl.BlockSpec(array.shape, lambda a: (0,) * array.ndim)
    init = call(
        functools.partial(field_kernel, s),
        "field",
        grid_shape,
        [pl.BlockSpec((s.bxn, None, s.Yl, G), lambda a: (0, a, 0, 0)), whole(gains)],
        grid_block,
        3e9,
        1e7,
        grid=(B,),
    )(sdf.reshape(s.bxn, B, s.Yl, G), gains)

    on_lanes = lambda v: jnp.broadcast_to(v.reshape(nx, 1, s.cp), (nx, s.bxn, s.cp)).reshape(1, L)
    mixing = mix_w[0].T.reshape(nx, 1, s.cp, nx, 1, s.cp)
    mixing = jnp.broadcast_to(mixing, (nx, s.bxn, s.cp, nx, s.bxn, s.cp)).reshape(L, L)
    mixing = jnp.where(same_bx, mixing, 0.0)
    bias = on_lanes(mix_b[0])
    read_mix = jnp.sum(readout_w[:, None] * mix_w[1], axis=0)
    base = jnp.sum(readout_w * mix_b[1]).reshape(1)
    out_lane = jnp.arange(s.LB)
    reading = jnp.where(lane_bx[:, None] == out_lane[None, :] // s.byn % s.bxn, on_lanes(read_mix).reshape(L, 1), 0.0)
    mine = lax.dynamic_slice_in_dim(readout_w, row_x * s.cp, s.cp)

    def multipliers(w, scale):
        w = w.reshape(2, s.KL, s.cp, M, M)
        if scale is not None:
            w = w * scale[None, None, :, None, None]
        w = w.transpose(2, 4, 0, 1, 3)
        u = jnp.concatenate([w[:, :, 0:1], w[:, :, 0:1]], axis=2).reshape(s.cp, M, s.LK)
        v = jnp.concatenate([-w[:, :, 1:2], w[:, :, 1:2]], axis=2).reshape(s.cp, M, s.LK)
        return u, v

    u0, v0 = multipliers(spec_w[0], None)
    u1, v1 = multipliers(spec_w[1], mine)

    freq = jnp.asarray(s.freq, jnp.int32)
    turn = jnp.mod(freq[None, :] * (row_x * s.Xl) + freq[:, None] * (row_y * s.Yl), G).reshape(1, -1)
    angle = turn.astype(F32) * (2.0 * math.pi / G)
    turns = jnp.concatenate([jnp.cos(angle), jnp.sin(angle)], axis=0)
    prepared = (incoming, init, mixing, bias, base, reading, u0, v0, u1, v1, turns)
    incoming, init, mixing, bias, base, reading, u0, v0, u1, v1, turns = lax.optimization_barrier(prepared)
    ids, counts, in_pos = placement(incoming)

    spec_shape = shape(nx, B, s.bxn, s.K2, s.LY)
    grid0, spec = call(
        functools.partial(encode_kernel, s, cap),
        "encode",
        (grid_shape, spec_shape),
        [SM, SM, VM, VM, VM],
        (VM, VM),
        4e9,
        2.2e7,
    )(ids, counts, incoming, init, t["z_fwd"])

    def to_modes(spec):
        spec = spec.reshape(nx, B * s.bxn * s.K2, s.LY)
        spec = lax.all_to_all(spec, "gx", split_axis=0, concat_axis=0, tiled=True)
        spec = call(
            functools.partial(x_forward_kernel, s),
            "x_forward",
            shape(ny, s.LY, s.LK),
            [VM, VM],
            VM,
            1e9,
            3e6,
        )(spec.reshape(G * s.K2, s.LY), t["x_fwd"])
        spec = lax.all_to_all(spec, "gy", split_axis=0, concat_axis=0, tiled=True)
        return spec.reshape(G * s.cp, s.LK)

    spec = to_modes(spec)
    mixed = call(
        functools.partial(mix_kernel, s),
        "mix",
        grid_shape,
        [grid_block, whole(mixing), whole(bias)],
        grid_block,
        2e9,
        1.7e7,
        grid=(B,),
    )(grid0, mixing, bias)
    spec = call(
        functools.partial(y_kernel, s), "y_both", shape(G * s.cp, s.LK), [VM] * 5, VM, 1e9, 2e6
    )(spec, t["y_fwd"], t["y_inv"], u0, v0)
    spec = lax.all_to_all(spec.reshape(ny, s.LY, s.LK), "gy", split_axis=0, concat_axis=0, tiled=True)
    spec = call(
        functools.partial(x_inverse_kernel, s), "x_inverse", shape(G * s.K2, s.LY), [VM, VM], VM, 1e9, 3e6
    )(spec, t["x_inv"])
    spec = lax.all_to_all(
        spec.reshape(nx, B * s.bxn * s.K2, s.LY), "gx", split_axis=0, concat_axis=0, tiled=True
    ).reshape(nx, B, s.bxn, s.K2, s.LY)
    spec_block = pl.BlockSpec((nx, 1, s.bxn, s.K2, s.LY), lambda a: (0, a, 0, 0, 0))
    grid1, spec = call(
        functools.partial(layer_kernel, s),
        "layer",
        (grid_shape, spec_shape),
        [grid_block, spec_block, whole(t["z_inv"]), whole(t["z_fwd"])],
        (grid_block, spec_block),
        4e9,
        2.1e7,
        grid=(B,),
    )(mixed, spec, t["z_inv"], t["z_fwd"])
    spec = to_modes(spec)
    read = call(
        functools.partial(readout_kernel, s),
        "readout",
        shape(B, B * B, s.LB),
        [grid_block, whole(reading)],
        pl.BlockSpec((1, B * B, s.LB), lambda a: (a, 0, 0)),
        2e9,
        9e6,
        grid=(B,),
    )(grid1, reading)
    last = call(
        functools.partial(y_last_kernel, s), "y_last", shape(2 * s.KL, M * M), [VM] * 4, VM, 1e9, 1e6
    )(spec, t["y_fwd"], u1, v1)

    step = 1
    while step < nx:
        last = last + lax.ppermute(last, "gx", [(i, i ^ step) for i in range(nx)])
        step *= 2
    last = jnp.broadcast_to(last[None], (ny,) + last.shape)
    last = lax.all_to_all(last, "gy", split_axis=0, concat_axis=0, tiled=True)
    values = call(
        functools.partial(decode_kernel, s, cap),
        "decode",
        shape(ny * cap, PB),
        [SM, SM, SM] + [VM] * 7,
        VM,
        4e9,
        6e6,
        scratch=[pltpu.VMEM((B * B * B, s.LB), F32)],
    )(ids, counts, base, in_pos, last, turns, read.reshape(B * B * B, s.LB), t["xy_hi"], t["xy_lo"], t["z_last"])
    returned = lax.all_to_all(values.reshape(ny, cap, PB), "gy", split_axis=0, concat_axis=0, tiled=True)
    choose = (slot_of[:, None] == jnp.arange(ny * cap, dtype=jnp.int32)[None, :]).astype(F32)
    pressure = jnp.dot(choose, returned.reshape(ny * cap, PB), precision=lax.Precision.HIGHEST)
    return pressure.reshape(blocks * PB)


def solution(mesh):
    placed = (
        P(None, ("gx", "gy")),
        P(None, ("gx", "gy")),
        P(("gx", "gy")),
        P(("gx", "gy")),
        P(("gx", "gy")),
        P("gx", "gy", None),
        P(),
        P(),
        P(),
        P(None, None, "gy", "gx", None),
        P(),
    )
    return jax.shard_map(
        per_device, mesh=mesh, in_specs=placed, out_specs=P(("gx", "gy")), check_vma=False
    )
```

```python
import functools
import math

import jax
import jax.numpy as jnp
import ml_dtypes
import numpy as np
from jax import lax
from jax.experimental import pallas as pl
from jax.experimental.pallas import tpu as pltpu
from jax.sharding import PartitionSpec as P

B = 8
BF = jnp.bfloat16
F32 = jnp.float32
VM = pl.BlockSpec(memory_space=pltpu.VMEM)
SM = pl.BlockSpec(memory_space=pltpu.SMEM)
LIMIT = 32 * 1024 * 1024


def split(x):
    hi = x.astype(BF)
    lo = (x - hi.astype(F32)).astype(BF)
    return hi, lo


def np_split(table):
    table = np.asarray(table, np.float64).astype(np.float32)
    hi = table.astype(ml_dtypes.bfloat16)
    lo = (table - hi.astype(np.float32)).astype(ml_dtypes.bfloat16)
    return hi, lo


def dot(a, b, contract=((1,), (0,))):
    return lax.dot_general(a, b, (contract, ((), ())), preferred_element_type=F32)


NT = ((1,), (1,))


def call(body, name, out_shape, in_specs, out_specs, flops, moved, grid=None, scratch=(), aliases=None):
    extra = {} if grid is None else {"grid": grid}
    return pl.pallas_call(
        body,
        name=name,
        out_shape=out_shape,
        in_specs=in_specs,
        out_specs=out_specs,
        scratch_shapes=list(scratch),
        input_output_aliases=aliases or {},
        compiler_params=pltpu.CompilerParams(vmem_limit_bytes=LIMIT),
        cost_estimate=pl.CostEstimate(flops=int(flops), bytes_accessed=int(moved), transcendentals=0),
        **extra,
    )


class Sizes:
    def __init__(self, nx, ny, grid, channels, modes, kz):
        self.nx, self.ny, self.G, self.C, self.M, self.KZ = nx, ny, grid, channels, modes, kz
        self.NB = grid // B
        self.bxn = self.NB // nx
        self.byn = self.NB // ny
        self.Xl = grid // nx
        self.Yl = grid // ny
        self.cp = channels // nx
        self.KL = kz // ny
        self.L = channels * self.bxn
        self.LY = self.Yl * self.cp
        self.LK = 2 * self.KL * modes
        self.K2 = 2 * kz
        self.LB = self.NB * self.bxn * self.byn
        self.freq = np.where(np.arange(modes) < modes // 2, np.arange(modes), np.arange(modes) - modes)


def trig(s, places, freqs):
    angle = (np.asarray(places)[:, None] * np.asarray(freqs)[None, :]) % s.G * (2.0 * np.pi / s.G)
    return np.cos(angle), np.sin(angle)


def stack_left(table):
    hi, lo = np_split(table)
    zero = np.zeros_like(lo)
    return np.concatenate([np.concatenate([hi, hi], 1), np.concatenate([lo, zero], 1)], 0)


def wide_left(table):
    hi, lo = np_split(table)
    return np.concatenate([hi, hi, lo], 1)


def make_tables(s):
    t = {}
    c, n = trig(s, np.arange(s.KZ), np.arange(s.G))
    t["z_fwd"] = stack_left(np.concatenate([c, -n], 0))
    back = np.where(np.arange(s.KZ) == 0, 1.0, 2.0)[None, :] / s.G
    c, n = trig(s, np.arange(s.G), np.arange(s.KZ))
    c, n = c * back, -n * back
    t["z_inv"] = wide_left(np.concatenate([c, n], 1))
    t["z_last"] = wide_left(np.stack([c.reshape(s.G, s.ny, s.KL), n.reshape(s.G, s.ny, s.KL)], 2).reshape(s.G, -1))
    local = np.arange(s.Xl).reshape(s.bxn, B).T.reshape(-1)
    fwd, inv = [], []
    for row in range(s.nx):
        places = np.concatenate([row * s.Xl + local, (row ^ 1) * s.Xl + local])
        c, n = trig(s, s.freq, places)
        fwd.append(stack_left(np.concatenate([np.concatenate([c, n], 1), np.concatenate([-n, c], 1)], 0)))
        c, n = c.T, n.T
        table = np.zeros((s.KL, 2, 2 * s.Xl, 2, s.KL, s.M))
        for k in range(s.KL):
            table[k, 0, :, 0, k], table[k, 0, :, 1, k] = c, -n
            table[k, 1, :, 0, k], table[k, 1, :, 1, k] = n, c
        inv.append(wide_left(table.reshape(4 * s.KL * s.Xl, s.LK) / s.G))
    t["x_fwd"] = np.stack(fwd)
    t["x_inv"] = np.stack(inv)
    c, n = trig(s, s.freq, np.arange(s.G))
    t["y_fwd"] = stack_left(np.concatenate([c, n], 0))
    t["y_inv"] = wide_left(np.concatenate([c.T, n.T], 1) / s.G)
    xs = (np.arange(s.bxn)[:, None] * B + np.arange(B)[None, :]).T.reshape(B, 1, s.bxn, 1)
    ys = (np.arange(s.byn)[:, None] * B + np.arange(B)[None, :]).T.reshape(1, B, 1, s.byn)
    full = (B, B, s.bxn, s.byn)
    xs, ys = np.broadcast_to(xs, full).reshape(-1), np.broadcast_to(ys, full).reshape(-1)
    turn = s.freq[None, :, None] * xs[None, None, :] + s.freq[:, None, None] * ys[None, None, :]
    angle = (turn % s.G).reshape(s.M * s.M, -1) * (2.0 * np.pi / s.G)
    t["xy_hi"], t["xy_lo"] = np_split(np.concatenate([np.cos(angle), np.sin(angle)], 0) / (s.G * s.G))
    return t


def block_turn(tiles, blocks, width):
    count = len(tiles)
    if count == blocks and count * width == 128:
        lane = lax.broadcasted_iota(jnp.int32, tiles[0].shape, 1) // width
        tiles = list(tiles)
        step = 1
        while step < count:
            upper = (lane & step) != 0
            for i in range(count):
                if i & step == 0:
                    a, b = tiles[i], tiles[i | step]
                    up = pltpu.roll(b, step * width, 1)
                    down = pltpu.roll(a, 128 - step * width, 1)
                    tiles[i] = jnp.where(upper, up, a)
                    tiles[i | step] = jnp.where(upper, b, down)
            step *= 2
        return tiles
    return [
        jnp.concatenate([tile[:, b * width : (b + 1) * width] for tile in tiles], axis=1)
        for b in range(blocks)
    ]


def swap_halves(x):
    half = x.shape[1] // 2
    if x.shape[1] == 128:
        return pltpu.roll(x, half, 1)
    return jnp.concatenate([x[:, half:], x[:, :half]], axis=1)


def half_signs(rows, width, first):
    lane = lax.broadcasted_iota(jnp.int32, (rows, width), 1)
    return jnp.where(lane < width // 2, first, -first).astype(F32)


def pack_kernel(s, cap, brick_ref, count_ref, pos_ref, feat_ref, area_ref, out_ref, slot_ref, fill_ref):
    blocks = brick_ref.shape[0]
    C = s.C
    for i in range(s.ny):
        fill_ref[i] = 0
        out_ref[i] = jnp.full(out_ref.shape[1:], -1.0, F32)
    live = count_ref[0]

    def step(n, carry):
        @pl.when(n < live)
        def _():
            brick = brick_ref[n]
            dest = (brick // s.NB) % s.NB // s.byn
            order = fill_ref[dest]
            fill_ref[dest] = order + 1
            slot_ref[n] = dest * cap + order
            lanes = pl.ds(pl.multiple_of(n * 128, 128), 128)
            out_ref[dest, pl.ds(pl.multiple_of(order * C, 8), C), :] = feat_ref[:, lanes] * area_ref[pl.ds(n, 1), :]
            points = pos_ref[:, lanes]
            for d in range(3):
                out_ref[dest, pl.ds(cap * C + d * cap + order, 1), :] = points[d : d + 1, :]

        @pl.when(n >= live)
        def _():
            slot_ref[n] = -1

        return carry

    lax.fori_loop(0, blocks, step, 0)


def field_kernel(s, sdf_ref, gain_ref, out_ref):
    ghi, glo = split(gain_ref[...])

    def step(a, carry):
        hi, lo = split(sdf_ref[:, a].reshape(s.bxn * s.Yl, s.G).T)
        wide = dot(hi, ghi) + dot(lo, ghi) + dot(hi, glo)
        for y in range(s.Yl):
            out_ref[a, y] = wide[:, y * s.L : (y + 1) * s.L]
        return carry

    lax.fori_loop(0, B, step, 0)


def kernel_tiles(points):
    px, py, pz = points
    scale = 1.0 / B
    sub = lax.broadcasted_iota(jnp.int32, pz.shape, 0).astype(F32)
    gz = ((sub + 0.5) - pz) * scale
    gz = gz * gz
    gx = []
    gy = []
    for a in range(B):
        d = (px - (a + 0.5)) * scale
        gx.append(1.0 - d * d)
        d = (py - (a + 0.5)) * scale
        gy.append(d * d + gz)
    tiles = []
    for a in range(B):
        for b in range(B):
            t = jnp.maximum(gx[a] - gy[b], 0.0)
            tiles.append(t * t)
    return tiles


def by_distance(s, row, items):
    bit = 1
    while bit < s.nx:
        far = row & bit != 0
        items = [
            [jnp.where(far, b, a) for a, b in zip(items[e], items[e ^ bit])] for e in range(s.nx)
        ]
        bit *= 2
    return items


def store_spectrum(s, row, a, tiles, keep_ref, send_ref):
    groups = by_distance(s, row, [tiles[g * s.bxn : (g + 1) * s.bxn] for g in range(s.nx)])
    for e in range(s.nx):
        for b in range(s.bxn):
            (send_ref if e & 1 else keep_ref)[e // 2, a, b] = groups[e][b]


def grid_to_spectrum(s, rows_of, table):
    tiles = []
    for y in range(0, s.Yl, 2):
        both = jnp.concatenate([rows_of(y), rows_of(y + 1)], axis=1)
        hi, lo = split(both)
        res = dot(table, jnp.concatenate([hi, lo], axis=0))
        res = res[: s.K2] + res[s.K2 :]
        tiles += [res[:, : s.L], res[:, s.L :]]
    return block_turn(tiles, s.nx * s.bxn, s.cp)


def encode_kernel(s, cap, row_ref, id_ref, num_ref, in_ref, init_ref, table_ref, grid_ref, keep_ref, send_ref):
    C = s.C
    for a in range(B):
        grid_ref[a] = init_ref[a]
    group = lax.broadcasted_iota(jnp.int32, (s.L, 128), 0) // s.cp % s.bxn

    def per_source(src, carry):
        def per_pair(h, inner):
            results = []
            for i in range(2):
                j = h * 2 + i
                slot = src * cap + j
                points = [
                    jnp.broadcast_to(in_ref[src, pl.ds(cap * C + d * cap + j, 1), :], (8, 128))
                    - id_ref[3 + d, slot].astype(F32)
                    for d in range(3)
                ]
                weights = jnp.concatenate(kernel_tiles(points), axis=0)
                feats = in_ref[src, pl.ds(pl.multiple_of(j * C, 8), C), :]
                spread = []
                for g in range(s.nx):
                    spread += [feats[g * s.cp : (g + 1) * s.cp]] * s.bxn
                spread = jnp.where(group == id_ref[0, slot], jnp.concatenate(spread, axis=0), 0.0)
                whi, wlo = split(weights)
                fhi, flo = split(spread)
                left = jnp.concatenate([whi, wlo], axis=1)
                right = jnp.concatenate([fhi, fhi], axis=1)
                if s.L == 128:
                    under = jnp.concatenate([flo, jnp.zeros_like(flo)], axis=1)
                    res = dot(left, jnp.concatenate([right, under], axis=0), NT)
                    res = res[:, : s.L] + res[:, s.L :]
                else:
                    res = dot(left, right, NT) + dot(whi, flo, NT)
                results.append(res.reshape(B, B, B, s.L))
            for i in range(2):
                slot = src * cap + h * 2 + i
                ys = pl.ds(pl.multiple_of(id_ref[1, slot] * B, B), B)
                zs = pl.ds(pl.multiple_of(id_ref[2, slot] * B, B), B)
                grid_ref[:, ys, zs, :] = grid_ref[:, ys, zs, :] + results[i]
            return inner

        return lax.fori_loop(0, (num_ref[src] + 1) // 2, per_pair, carry)

    lax.fori_loop(0, s.ny, per_source, 0)

    def transform(a, carry):
        out = grid_to_spectrum(s, lambda y: grid_ref[a, y], table_ref[...])
        store_spectrum(s, row_ref[0], a, out, keep_ref, send_ref)
        return carry

    lax.fori_loop(0, B, transform, 0)


def mixed_rows(rows, whi, wlo):
    hi, lo = split(rows)
    width = whi.shape[1]
    if width == 128 and rows.shape[1] == 128:
        left = jnp.concatenate([hi, lo], axis=1)
        right = jnp.concatenate(
            [jnp.concatenate([whi, wlo], axis=1), jnp.concatenate([whi, jnp.zeros_like(wlo)], axis=1)], axis=0
        )
        res = dot(left, right)
        return res[:, :128] + res[:, 128:]
    return dot(hi, whi) + dot(lo, whi) + dot(hi, wlo)


def mix_kernel(s, grid_ref, mix_ref, bias_ref, out_ref):
    whi, wlo = split(mix_ref[...])

    def step(a, carry):
        for y in range(s.Yl):
            out_ref[a, y] = mixed_rows(grid_ref[a, y], whi, wlo) + bias_ref[...]
        return carry

    lax.fori_loop(0, B, step, 0)


def readout_kernel(s, grid_ref, mix_ref, out_ref):
    whi, wlo = split(mix_ref[...])
    lane = lax.broadcasted_iota(jnp.int32, (B, s.LB), 1)

    def step(a0, carry):
        for a in range(B):
            total = jnp.zeros((B, s.LB), F32)
            for by in range(s.byn):
                res = mixed_rows(grid_ref[a0, by * B + a], whi, wlo)
                for bz in range(s.NB):
                    mine = (lane // (s.bxn * s.byn) == bz) & (lane % s.byn == by)
                    total = jnp.where(mine, res[bz * B : (bz + 1) * B], total)
            out_ref[a0, a * B : (a + 1) * B, :] = total
        return carry

    lax.fori_loop(0, B, step, 0)


def x_forward_kernel(s, keep_ref, recv_ref, table_ref, out_ref):
    M = s.M
    for i in range(s.ny):
        parts = []
        for k in range(s.KL):
            kz = i * s.KL + k
            parts.append(
                jnp.concatenate(
                    [
                        ref[0, pl.ds(ri * s.KZ + kz, s.Xl, stride=s.K2), :]
                        for ri in range(2)
                        for ref in (keep_ref, recv_ref)
                    ],
                    axis=0,
                )
            )
        hi, lo = split(jnp.concatenate(parts, axis=1))
        res = dot(table_ref[...], jnp.concatenate([hi, lo], axis=0))
        res = res[: 2 * M] + res[2 * M :]
        rows = []
        for ri in range(2):
            for k in range(s.KL):
                rows.append(res[ri * M : (ri + 1) * M, k * s.LY : (k + 1) * s.LY])
        out_ref[i] = jnp.concatenate(rows, axis=0).T


def y_spectrum(s, in_ref, table, u_ref, v_ref, cs):
    M = s.M
    both = jnp.concatenate([in_ref[pl.ds(c, s.G, stride=s.cp), :] for c in cs], axis=1)
    hi, lo = split(both)
    res = dot(table, jnp.concatenate([hi, lo], axis=0))
    res = res[: 2 * M] + res[2 * M :]
    out = []
    plus = half_signs(M, s.LK, 1.0)
    for i, c in enumerate(cs):
        part = res[:, i * s.LK : (i + 1) * s.LK]
        wave = part[:M] + plus * swap_halves(part[M:])
        out.append(wave * u_ref[c] + swap_halves(wave) * v_ref[c])
    return out


def y_kernel(s, in_ref, fwd_ref, inv_ref, u_ref, v_ref, out_ref):
    minus = half_signs(s.M, s.LK, -1.0)
    for c in range(0, s.cp, 2):
        prods = y_spectrum(s, in_ref, fwd_ref[...], u_ref, v_ref, (c, c + 1))
        both = jnp.concatenate(
            [jnp.concatenate([p, minus * swap_halves(p)], axis=0) for p in prods], axis=1
        )
        hi, lo = split(both)
        res = dot(inv_ref[...], jnp.concatenate([hi, lo, hi], axis=0))
        for i in range(2):
            out_ref[pl.ds(c + i, s.G, stride=s.cp), :] = res[:, i * s.LK : (i + 1) * s.LK]


def y_last_kernel(s, in_ref, fwd_ref, u_ref, v_ref, out_ref):
    total = jnp.zeros((s.M, s.LK), F32)
    for c in range(0, s.cp, 2):
        prods = y_spectrum(s, in_ref, fwd_ref[...], u_ref, v_ref, (c, c + 1))
        total = total + prods[0] + prods[1]
    M = s.M
    for r in range(2 * s.KL):
        part = total[:, r * M : (r + 1) * M]
        out_ref[r : r + 1, :] = jnp.concatenate([part[m : m + 1] for m in range(M)], axis=1)


def x_inverse_kernel(s, in_ref, table_ref, keep_ref, send_ref):
    for i in range(s.ny):
        hi, lo = split(in_ref[i])
        if s.LK == 128:
            res = dot(table_ref[...], jnp.concatenate([hi, lo, hi], axis=1), NT)
        else:
            t = table_ref[...]
            res = dot(t[:, : s.LK], hi, NT) + dot(t[:, : s.LK], lo, NT) + dot(t[:, 2 * s.LK :], hi, NT)
        for k in range(s.KL):
            for ri in range(2):
                at = (k * 2 + ri) * 2 * s.Xl
                places = pl.ds(ri * s.KZ + i * s.KL + k, s.Xl, stride=s.K2)
                keep_ref[places, :] = res[at : at + s.Xl]
                send_ref[places, :] = res[at + s.Xl : at + 2 * s.Xl]


def gelu(x):
    inner = math.sqrt(2.0 / math.pi) * (x + 0.044715 * (x * x * x))
    return 0.5 * x * (1.0 + jnp.tanh(inner))


def layer_kernel(s, row_ref, mixed_ref, inv_ref, fwd_ref, *refs):
    in_refs, (grid_ref, keep_ref, send_ref) = refs[: s.nx], refs[s.nx :]
    row = row_ref[0]

    def step(a, carry):
        groups = by_distance(s, row, [[ref[a, b] for b in range(s.bxn)] for ref in in_refs])
        tiles = block_turn([tile for group in groups for tile in group], s.Yl, s.cp)
        for y in range(0, s.Yl, 2):
            hi, lo = split(jnp.concatenate([tiles[y], tiles[y + 1]], axis=1))
            res = dot(inv_ref[...], jnp.concatenate([hi, lo, hi], axis=0))
            for i in range(2):
                grid_ref[a, y + i] = gelu(mixed_ref[a, y + i] + res[:, i * s.L : (i + 1) * s.L])
        out = grid_to_spectrum(s, lambda y: grid_ref[a, y], fwd_ref[...])
        store_spectrum(s, row, a, out, keep_ref, send_ref)
        return carry

    lax.fori_loop(0, B, step, 0)


def decode_kernel(s, cap, id_ref, num_ref, base_ref, pos_ref, spec_ref, turn_ref, mix_ref, hi_ref, lo_ref, inv_ref, out_ref, s_ref):
    modes = jnp.concatenate([spec_ref[i] for i in range(s.ny)], axis=0)
    real_row = lax.broadcasted_iota(jnp.int32, modes.shape, 0) // s.KL % 2 == 0

    def partner(x):
        return jnp.where(real_row, -pltpu.roll(x, s.K2 - s.KL, 0), pltpu.roll(x, s.KL, 0))

    modes = modes * turn_ref[0:1, :] + partner(modes) * turn_ref[1:2, :]
    mhi, mlo = split(jnp.concatenate([modes, partner(modes)], axis=1))
    wave = dot(jnp.concatenate([mhi, mlo], axis=0), hi_ref[...])
    wave = wave[: s.K2] + wave[s.K2 :] + dot(mhi, lo_ref[...])
    hi, lo = split(wave)
    field = dot(inv_ref[...], jnp.concatenate([hi, lo, hi], axis=0))
    width = s.bxn * s.byn
    per = 128 // width
    for q in range(field.shape[1] // 128):
        tiles = [field[z * B : (z + 1) * B, q * 128 : (q + 1) * 128] for z in range(s.NB)]
        for i, tile in enumerate(block_turn(tiles, per, width)):
            at = (q * per + i) * B
            s_ref[at : at + B, :] = tile + mix_ref[at : at + B, :] + base_ref[0]
    out_ref[...] = jnp.zeros(out_ref.shape, F32)
    cell = lax.broadcasted_iota(jnp.int32, (s.LB, 128), 0)

    def per_source(src, carry):
        def per_pair(h, inner):
            shi, slo = split(s_ref[...])
            picks = []
            for i in range(2):
                j = h * 2 + i
                at = id_ref[6, src * cap + j]
                picks.append(jnp.where(cell == at, 1.0, 0.0).astype(BF))
            pick = jnp.concatenate(picks, axis=1)
            if s.LB == 128:
                vals = dot(jnp.concatenate([shi, slo], axis=1), jnp.concatenate([pick, pick], axis=0))
            else:
                vals = dot(shi, pick) + dot(slo, pick)
            for i in range(2):
                j = h * 2 + i
                slot = src * cap + j
                points = [
                    jnp.broadcast_to(pos_ref[src, pl.ds(d * cap + j, 1), :], (8, 128))
                    - id_ref[3 + d, slot].astype(F32)
                    for d in range(3)
                ]
                top = jnp.zeros((B, 128), F32)
                low = jnp.zeros((B, 128), F32)
                for n, tile in enumerate(kernel_tiles(points)):
                    top = top + tile * vals[n * B : (n + 1) * B, i * 128 : (i + 1) * 128]
                    low = low + tile
                top = jnp.sum(top, axis=0, keepdims=True)
                low = jnp.sum(low, axis=0, keepdims=True)
                out_ref[pl.ds(slot, 1), :] = top / jnp.where(low > 0.0, low, 1.0)
            return inner

        return lax.fori_loop(0, (num_ref[src] + 1) // 2, per_pair, carry)

    lax.fori_loop(0, s.ny, per_source, 0)


def per_device(
    positions,
    point_feat,
    area,
    block_brick,
    block_count,
    sdf,
    grid_gain,
    mix_w,
    mix_b,
    spec_w,
    readout_w,
):
    nx, ny = lax.axis_size("gx"), lax.axis_size("gy")
    row_x, row_y = lax.axis_index("gx"), lax.axis_index("gy")
    modes = math.isqrt(spec_w.shape[4])
    s = Sizes(nx, ny, sdf.shape[2], point_feat.shape[0], modes, spec_w.shape[2] * ny)
    t = {name: jnp.asarray(value) for name, value in make_tables(s).items()}
    shape = lambda *dims: jax.ShapeDtypeStruct(dims, F32)
    blocks = block_brick.shape[0]
    cap = blocks // ny
    PB = positions.shape[1] // blocks
    C, G, M, L = s.C, s.G, s.M, s.L
    rows = cap * (C + 3)

    outgoing, slot_of = call(
        functools.partial(pack_kernel, s, cap),
        "pack",
        (shape(ny, rows, PB), jax.ShapeDtypeStruct((blocks,), jnp.int32)),
        [SM, SM, VM, VM, VM],
        (VM, SM),
        1e6,
        6e6,
        scratch=[pltpu.SMEM((ny,), jnp.int32)],
    )(block_brick, block_count, positions, point_feat, area.reshape(blocks, PB))
    incoming = lax.all_to_all(outgoing, "gy", split_axis=0, concat_axis=0, tiled=True)

    def placement(incoming):
        in_pos = incoming[:, cap * C :, :]
        first = in_pos.reshape(ny, 3, cap, PB)[..., 0].transpose(1, 0, 2).reshape(3, ny * cap)
        counts = jnp.sum((first[0].reshape(ny, cap) >= 0.0).astype(jnp.int32), axis=1)
        brick = jnp.floor(first / B).astype(jnp.int32)
        start = jnp.stack([row_x * s.bxn, row_y * s.byn, jnp.zeros_like(row_x)])
        limit = jnp.array([s.bxn - 1, s.byn - 1, s.NB - 1], jnp.int32)
        local = jnp.clip(brick - start[:, None], 0, limit[:, None])
        corner = (local + start[:, None]) * B
        flat = local[2] * (s.bxn * s.byn) + local[0] * s.byn + local[1]
        owned = jnp.where(first[0:1] >= 0.0, local[0:1], -1)
        ids = jnp.concatenate([owned, local[1:], corner, flat[None], flat[None]], axis=0)
        return ids, counts, in_pos

    lane = jnp.arange(L)
    lane_bx = lane // s.cp % s.bxn
    same_bx = lane_bx[:, None] == lane_bx[None, :]
    gain_l = jnp.broadcast_to(grid_gain.reshape(nx, 1, s.cp), (nx, s.bxn, s.cp)).reshape(L)
    spread = (
        (jnp.arange(s.bxn)[:, None, None, None] == lane_bx[None, None, None, :])
        & (jnp.arange(s.Yl)[None, :, None, None] == jnp.arange(s.Yl)[None, None, :, None])
    )
    gains = jnp.where(spread, gain_l, 0.0).reshape(s.bxn * s.Yl, s.Yl * L)
    grid_shape = shape(B, s.Yl, G, L)
    init = call(functools.partial(field_kernel, s), "field", grid_shape, [VM, VM], VM, 3e9, 1e7)(
        sdf.reshape(s.bxn, B, s.Yl, G), gains
    )

    on_lanes = lambda v: jnp.broadcast_to(v.reshape(nx, 1, s.cp), (nx, s.bxn, s.cp)).reshape(1, L)
    mixing = mix_w[0].T.reshape(nx, 1, s.cp, nx, 1, s.cp)
    mixing = jnp.broadcast_to(mixing, (nx, s.bxn, s.cp, nx, s.bxn, s.cp)).reshape(L, L)
    mixing = jnp.where(same_bx, mixing, 0.0)
    bias = on_lanes(mix_b[0])
    read_mix = jnp.sum(readout_w[:, None] * mix_w[1], axis=0)
    base = jnp.sum(readout_w * mix_b[1]).reshape(1)
    out_lane = jnp.arange(s.LB)
    reading = jnp.where(lane_bx[:, None] == out_lane[None, :] // s.byn % s.bxn, on_lanes(read_mix).reshape(L, 1), 0.0)
    mine = lax.dynamic_slice_in_dim(readout_w, row_x * s.cp, s.cp)

    def multipliers(w, scale):
        w = w.reshape(2, s.KL, s.cp, M, M)
        if scale is not None:
            w = w * scale[None, None, :, None, None]
        w = w.transpose(2, 4, 0, 1, 3)
        u = jnp.concatenate([w[:, :, 0:1], w[:, :, 0:1]], axis=2).reshape(s.cp, M, s.LK)
        v = jnp.concatenate([-w[:, :, 1:2], w[:, :, 1:2]], axis=2).reshape(s.cp, M, s.LK)
        return u, v

    u0, v0 = multipliers(spec_w[0], None)
    u1, v1 = multipliers(spec_w[1], mine)

    freq = jnp.asarray(s.freq, jnp.int32)
    turn = jnp.mod(freq[None, :] * (row_x * s.Xl) + freq[:, None] * (row_y * s.Yl), G).reshape(1, -1)
    angle = turn.astype(F32) * (2.0 * math.pi / G)
    turns = jnp.concatenate([jnp.cos(angle), jnp.sin(angle)], axis=0)
    x_fwd = lax.dynamic_index_in_dim(t["x_fwd"], row_x, 0, False)
    x_inv = lax.dynamic_index_in_dim(t["x_inv"], row_x, 0, False)
    row = row_x.astype(jnp.int32).reshape(1)
    prepared = (incoming, init, mixing, bias, base, reading, u0, v0, u1, v1, turns, x_fwd, x_inv, row)
    incoming, init, mixing, bias, base, reading, u0, v0, u1, v1, turns, x_fwd, x_inv, row = (
        lax.optimization_barrier(prepared)
    )
    ids, counts, in_pos = placement(incoming)

    half = s.nx // 2
    spec_shape = shape(half, B, s.bxn, s.K2, s.LY)
    grid, keep, send = call(
        functools.partial(encode_kernel, s, cap),
        "encode",
        (grid_shape, spec_shape, spec_shape),
        [SM, SM, SM, VM, VM, VM],
        (VM, VM, VM),
        4e9,
        2.2e7,
        aliases={4: 0},
    )(row, ids, counts, incoming, init, t["z_fwd"])

    def exchange(array, distance):
        return lax.ppermute(array, "gx", [(i, i ^ distance) for i in range(nx)])

    def to_modes(keep, send):
        recv = exchange(send, 1).reshape(half, s.Xl * s.K2, s.LY)
        keep = keep.reshape(half, s.Xl * s.K2, s.LY)

        def part(d):
            block = pl.BlockSpec((1, s.Xl * s.K2, s.LY), lambda i: (d, 0, 0))
            return call(
                functools.partial(x_forward_kernel, s),
                "x_forward",
                shape(ny, s.LY, s.LK),
                [block, block, pl.BlockSpec(x_fwd.shape, lambda i: (0, 0))],
                pl.BlockSpec((ny, s.LY, s.LK), lambda i: (0, 0, 0)),
                2e8,
                3e6,
                grid=(1,),
            )(keep, recv, x_fwd)

        others = [exchange(part(d), 2 * d) for d in range(1, half)]
        spec = part(0)
        for other in others:
            spec = spec + other
        spec = lax.all_to_all(spec, "gy", split_axis=0, concat_axis=0, tiled=True)
        return spec.reshape(G * s.cp, s.LK)

    spec = to_modes(keep, send)
    mixed = call(
        functools.partial(mix_kernel, s), "mix", grid_shape, [VM] * 3, VM, 2e9, 1.7e7, aliases={0: 0}
    )(grid, mixing, bias)
    spec = call(
        functools.partial(y_kernel, s), "y_both", shape(G * s.cp, s.LK), [VM] * 5, VM, 1e9, 2e6
    )(spec, t["y_fwd"], t["y_inv"], u0, v0)
    spec = lax.all_to_all(spec.reshape(ny, s.LY, s.LK), "gy", split_axis=0, concat_axis=0, tiled=True)
    near = [spec] + [exchange(spec, 2 * d) for d in range(1, half)]
    fields = []
    for item in near:
        own, other = call(
            functools.partial(x_inverse_kernel, s),
            "x_inverse",
            (shape(s.Xl * s.K2, s.LY),) * 2,
            [VM, VM],
            (VM, VM),
            3e8,
            3e6,
        )(item, x_inv)
        fields += [own, exchange(other, 1)]
    fields = [f.reshape(B, s.bxn, s.K2, s.LY) for f in fields]
    grid, keep, send = call(
        functools.partial(layer_kernel, s),
        "layer",
        (grid_shape, spec_shape, spec_shape),
        [SM] + [VM] * (3 + nx),
        (VM, VM, VM),
        4e9,
        2.1e7,
        aliases={1: 0},
    )(row, mixed, t["z_inv"], t["z_fwd"], *fields)
    spec = to_modes(keep, send)
    read = call(
        functools.partial(readout_kernel, s), "readout", shape(B, B * B, s.LB), [VM, VM], VM, 2e9, 9e6
    )(grid, reading)
    last = call(
        functools.partial(y_last_kernel, s), "y_last", shape(2 * s.KL, M * M), [VM] * 4, VM, 1e9, 1e6
    )(spec, t["y_fwd"], u1, v1)

    step = 1
    while step < nx:
        last = last + lax.ppermute(last, "gx", [(i, i ^ step) for i in range(nx)])
        step *= 2
    last = jnp.broadcast_to(last[None], (ny,) + last.shape)
    last = lax.all_to_all(last, "gy", split_axis=0, concat_axis=0, tiled=True)
    values = call(
        functools.partial(decode_kernel, s, cap),
        "decode",
        shape(ny * cap, PB),
        [SM, SM, SM] + [VM] * 7,
        VM,
        4e9,
        6e6,
        scratch=[pltpu.VMEM((B * B * B, s.LB), F32)],
    )(ids, counts, base, in_pos, last, turns, read.reshape(B * B * B, s.LB), t["xy_hi"], t["xy_lo"], t["z_last"])
    returned = lax.all_to_all(values.reshape(ny, cap, PB), "gy", split_axis=0, concat_axis=0, tiled=True)
    choose = (slot_of[:, None] == jnp.arange(ny * cap, dtype=jnp.int32)[None, :]).astype(F32)
    pressure = jnp.dot(choose, returned.reshape(ny * cap, PB), precision=lax.Precision.HIGHEST)
    return pressure.reshape(blocks * PB)


def solution(mesh):
    placed = (
        P(None, ("gx", "gy")),
        P(None, ("gx", "gy")),
        P(("gx", "gy")),
        P(("gx", "gy")),
        P(("gx", "gy")),
        P("gx", "gy", None),
        P(),
        P(),
        P(),
        P(None, None, "gy", "gx", None),
        P(),
    )
    return jax.shard_map(
        per_device, mesh=mesh, in_specs=placed, out_specs=P(("gx", "gy")), check_vma=False
    )
```

```python
import functools
import math

import jax
import jax.numpy as jnp
import ml_dtypes
import numpy as np
from jax import lax
from jax.experimental import pallas as pl
from jax.experimental.pallas import tpu as pltpu
from jax.sharding import PartitionSpec as P

B = 8
BF = jnp.bfloat16
F32 = jnp.float32
VM = pl.BlockSpec(memory_space=pltpu.VMEM)
SM = pl.BlockSpec(memory_space=pltpu.SMEM)
MIB = 1024 * 1024


def split(x):
    hi = x.astype(BF)
    lo = (x - hi.astype(F32)).astype(BF)
    return hi, lo


def np_split(table):
    table = np.asarray(table, np.float64).astype(np.float32)
    hi = table.astype(ml_dtypes.bfloat16)
    lo = (table - hi.astype(np.float32)).astype(ml_dtypes.bfloat16)
    return hi, lo


def dot(a, b, contract=((1,), (0,))):
    return lax.dot_general(a, b, (contract, ((), ())), preferred_element_type=F32)


NT = ((1,), (1,))


def call(body, name, out_shape, in_specs, out_specs, flops, moved, grid=None, scratch=(), room=58):
    extra = {} if grid is None else {"grid": grid}
    return pl.pallas_call(
        body,
        name=name,
        out_shape=out_shape,
        in_specs=in_specs,
        out_specs=out_specs,
        scratch_shapes=list(scratch),
        compiler_params=pltpu.CompilerParams(vmem_limit_bytes=room * MIB),
        cost_estimate=pl.CostEstimate(flops=int(flops), bytes_accessed=int(moved), transcendentals=0),
        **extra,
    )


class Sizes:
    def __init__(self, nx, ny, grid, channels, modes, kz):
        self.nx, self.ny, self.G, self.C, self.M, self.KZ = nx, ny, grid, channels, modes, kz
        self.NB = grid // B
        self.bxn = self.NB // nx
        self.byn = self.NB // ny
        self.Xl = grid // nx
        self.Yl = grid // ny
        self.cp = channels // nx
        self.KL = kz // ny
        self.L = channels * self.bxn
        self.LY = self.Yl * self.cp
        self.LK = 2 * self.KL * modes
        self.K2 = 2 * kz
        self.LB = self.NB * self.bxn * self.byn
        self.freq = np.where(np.arange(modes) < modes // 2, np.arange(modes), np.arange(modes) - modes)


def trig(s, places, freqs):
    angle = (np.asarray(places)[:, None] * np.asarray(freqs)[None, :]) % s.G * (2.0 * np.pi / s.G)
    return np.cos(angle), np.sin(angle)


def stack_left(table):
    hi, lo = np_split(table)
    zero = np.zeros_like(lo)
    return np.concatenate([np.concatenate([hi, hi], 1), np.concatenate([lo, zero], 1)], 0)


def wide_left(table):
    hi, lo = np_split(table)
    return np.concatenate([hi, hi, lo], 1)


def make_tables(s):
    t = {}
    c, n = trig(s, np.arange(s.KZ), np.arange(s.G))
    t["z_fwd"] = stack_left(np.concatenate([c, -n], 0))
    back = np.where(np.arange(s.KZ) == 0, 1.0, 2.0)[None, :] / s.G
    c, n = trig(s, np.arange(s.G), np.arange(s.KZ))
    c, n = c * back, -n * back
    t["z_inv"] = wide_left(np.concatenate([c, n], 1))
    t["z_last"] = wide_left(np.stack([c.reshape(s.G, s.ny, s.KL), n.reshape(s.G, s.ny, s.KL)], 2).reshape(s.G, -1))
    local = np.arange(s.Xl).reshape(s.bxn, B).T.reshape(-1)
    fwd, inv = [], []
    for row in range(s.nx):
        places = np.concatenate([row * s.Xl + local, (row ^ 1) * s.Xl + local])
        c, n = trig(s, s.freq, places)
        fwd.append(stack_left(np.concatenate([np.concatenate([c, n], 1), np.concatenate([-n, c], 1)], 0)))
        c, n = c.T, n.T
        table = np.zeros((s.KL, 2, 2 * s.Xl, 2, s.KL, s.M))
        for k in range(s.KL):
            table[k, 0, :, 0, k], table[k, 0, :, 1, k] = c, -n
            table[k, 1, :, 0, k], table[k, 1, :, 1, k] = n, c
        inv.append(wide_left(table.reshape(4 * s.KL * s.Xl, s.LK) / s.G))
    t["x_fwd"] = np.stack(fwd)
    t["x_inv"] = np.stack(inv)
    c, n = trig(s, s.freq, np.arange(s.G))
    t["y_fwd"] = stack_left(np.concatenate([c, n], 0))
    t["y_inv"] = wide_left(np.concatenate([c.T, n.T], 1) / s.G)
    xs = (np.arange(s.bxn)[:, None] * B + np.arange(B)[None, :]).T.reshape(B, 1, s.bxn, 1)
    ys = (np.arange(s.byn)[:, None] * B + np.arange(B)[None, :]).T.reshape(1, B, 1, s.byn)
    full = (B, B, s.bxn, s.byn)
    xs, ys = np.broadcast_to(xs, full).reshape(-1), np.broadcast_to(ys, full).reshape(-1)
    turn = s.freq[None, :, None] * xs[None, None, :] + s.freq[:, None, None] * ys[None, None, :]
    angle = (turn % s.G).reshape(s.M * s.M, -1) * (2.0 * np.pi / s.G)
    t["xy_hi"], t["xy_lo"] = np_split(np.concatenate([np.cos(angle), np.sin(angle)], 0) / (s.G * s.G))
    return t


def block_turn(tiles, blocks, width):
    count = len(tiles)
    if count == blocks and count * width == 128:
        lane = lax.broadcasted_iota(jnp.int32, tiles[0].shape, 1) // width
        tiles = list(tiles)
        step = 1
        while step < count:
            upper = (lane & step) != 0
            for i in range(count):
                if i & step == 0:
                    a, b = tiles[i], tiles[i | step]
                    up = pltpu.roll(b, step * width, 1)
                    down = pltpu.roll(a, 128 - step * width, 1)
                    tiles[i] = jnp.where(upper, up, a)
                    tiles[i | step] = jnp.where(upper, b, down)
            step *= 2
        return tiles
    return [
        jnp.concatenate([tile[:, b * width : (b + 1) * width] for tile in tiles], axis=1)
        for b in range(blocks)
    ]


def swap_halves(x):
    half = x.shape[1] // 2
    if x.shape[1] == 128:
        return pltpu.roll(x, half, 1)
    return jnp.concatenate([x[:, half:], x[:, :half]], axis=1)


def half_signs(rows, width, first):
    lane = lax.broadcasted_iota(jnp.int32, (rows, width), 1)
    return jnp.where(lane < width // 2, first, -first).astype(F32)


def pack_kernel(s, caps, brick_ref, count_ref, pos_ref, feat_ref, area_ref, *refs):
    out_refs, (slot_ref, fill_ref) = refs[: len(caps)], refs[len(caps) :]
    blocks = brick_ref.shape[0]
    C = s.C
    for i in range(s.ny):
        fill_ref[i] = 0
        for out_ref in out_refs:
            out_ref[i] = jnp.full(out_ref.shape[1:], -1.0, F32)
    live = count_ref[0]

    def step(n, carry):
        @pl.when(n < live)
        def _():
            brick = brick_ref[n]
            dest = (brick // s.NB) % s.NB // s.byn
            order = fill_ref[dest]
            fill_ref[dest] = order + 1
            slot_ref[n] = dest * sum(caps) + order
            lanes = pl.ds(pl.multiple_of(n * 128, 128), 128)
            first = 0
            for cap, out_ref in zip(caps, out_refs):
                place = order - first

                @pl.when((place >= 0) & (place < cap))
                def _():
                    feats = feat_ref[:, lanes] * area_ref[pl.ds(n, 1), :]
                    out_ref[dest, pl.ds(pl.multiple_of(place * C, 8), C), :] = feats
                    points = pos_ref[:, lanes]
                    for d in range(3):
                        out_ref[dest, pl.ds(cap * C + d * cap + place, 1), :] = points[d : d + 1, :]

                first += cap

        @pl.when(n >= live)
        def _():
            slot_ref[n] = -1

        return carry

    lax.fori_loop(0, blocks, step, 0)


def field_kernel(s, sdf_ref, gain_ref, out_ref):
    hi, lo = split(sdf_ref[...].reshape(s.bxn * s.Yl, s.G).T)
    ghi, glo = split(gain_ref[...])
    wide = dot(hi, ghi) + dot(lo, ghi) + dot(hi, glo)
    for y in range(s.Yl):
        out_ref[0, y] = wide[:, y * s.L : (y + 1) * s.L]


def kernel_tiles(points):
    px, py, pz = points
    scale = 1.0 / B
    sub = lax.broadcasted_iota(jnp.int32, pz.shape, 0).astype(F32)
    gz = ((sub + 0.5) - pz) * scale
    gz = gz * gz
    gx = []
    gy = []
    for a in range(B):
        d = (px - (a + 0.5)) * scale
        gx.append(1.0 - d * d)
        d = (py - (a + 0.5)) * scale
        gy.append(d * d + gz)
    tiles = []
    for a in range(B):
        for b in range(B):
            t = jnp.maximum(gx[a] - gy[b], 0.0)
            tiles.append(t * t)
    return tiles


def by_distance(s, row, items):
    bit = 1
    while bit < s.nx:
        far = row & bit != 0
        items = [
            [jnp.where(far, b, a) for a, b in zip(items[e], items[e ^ bit])] for e in range(s.nx)
        ]
        bit *= 2
    return items


def store_spectrum(s, row, a, tiles, keep_ref, send_ref):
    groups = by_distance(s, row, [tiles[g * s.bxn : (g + 1) * s.bxn] for g in range(s.nx)])
    for e in range(s.nx):
        for b in range(s.bxn):
            (send_ref if e & 1 else keep_ref)[e // 2, a, b] = groups[e][b]


def grid_to_spectrum(s, rows_of, table):
    tiles = []
    for y in range(0, s.Yl, 2):
        both = jnp.concatenate([rows_of(y), rows_of(y + 1)], axis=1)
        hi, lo = split(both)
        res = dot(table, jnp.concatenate([hi, lo], axis=0))
        res = res[: s.K2] + res[s.K2 :]
        tiles += [res[:, : s.L], res[:, s.L :]]
    return block_turn(tiles, s.nx * s.bxn, s.cp)


def add_blocks(s, cap, id_ref, num_ref, in_ref, grid_ref):
    C = s.C
    group = lax.broadcasted_iota(jnp.int32, (s.L, 128), 0) // s.cp % s.bxn

    def per_source(src, carry):
        def per_pair(h, inner):
            results = []
            for i in range(2):
                j = h * 2 + i
                slot = src * cap + j
                points = [
                    jnp.broadcast_to(in_ref[src, pl.ds(cap * C + d * cap + j, 1), :], (8, 128))
                    - id_ref[3 + d, slot].astype(F32)
                    for d in range(3)
                ]
                weights = jnp.concatenate(kernel_tiles(points), axis=0)
                feats = in_ref[src, pl.ds(pl.multiple_of(j * C, 8), C), :]
                spread = []
                for g in range(s.nx):
                    spread += [feats[g * s.cp : (g + 1) * s.cp]] * s.bxn
                spread = jnp.where(group == id_ref[0, slot], jnp.concatenate(spread, axis=0), 0.0)
                whi, wlo = split(weights)
                fhi, flo = split(spread)
                left = jnp.concatenate([whi, wlo], axis=1)
                right = jnp.concatenate([fhi, fhi], axis=1)
                if s.L == 128:
                    under = jnp.concatenate([flo, jnp.zeros_like(flo)], axis=1)
                    res = dot(left, jnp.concatenate([right, under], axis=0), NT)
                    res = res[:, : s.L] + res[:, s.L :]
                else:
                    res = dot(left, right, NT) + dot(whi, flo, NT)
                results.append(res.reshape(B, B, B, s.L))
            for i in range(2):
                slot = src * cap + h * 2 + i
                ys = pl.ds(pl.multiple_of(id_ref[1, slot] * B, B), B)
                zs = pl.ds(pl.multiple_of(id_ref[2, slot] * B, B), B)
                grid_ref[:, ys, zs, :] = grid_ref[:, ys, zs, :] + results[i]
            return inner

        return lax.fori_loop(0, (num_ref[src] + 1) // 2, per_pair, carry)

    lax.fori_loop(0, s.ny, per_source, 0)


def encode_first_kernel(s, cap, id_ref, num_ref, in_ref, init_ref, grid_ref):
    for a in range(B):
        grid_ref[a] = init_ref[a]
    add_blocks(s, cap, id_ref, num_ref, in_ref, grid_ref)


def encode_last_kernel(
    s, cap, row_ref, id_ref, num_ref, in_ref, before_ref, table_ref, grid_ref, keep_ref, send_ref,
    sum_ref, held_ref, in_sem, out_sems
):
    fetch = pltpu.make_async_copy(before_ref, held_ref, in_sem)
    fetch.start()
    for a in range(B):
        sum_ref[a] = jnp.zeros(sum_ref.shape[1:], F32)
    add_blocks(s, cap, id_ref, num_ref, in_ref, sum_ref)
    fetch.wait()

    def transform(a, carry):
        held_ref[a] = held_ref[a] + sum_ref[a]
        pltpu.make_async_copy(held_ref.at[a], grid_ref.at[a], out_sems.at[a]).start()
        out = grid_to_spectrum(s, lambda y: held_ref[a, y], table_ref[...])
        store_spectrum(s, row_ref[0], a, out, keep_ref, send_ref)
        return carry

    lax.fori_loop(0, B, transform, 0)
    for a in range(B):
        pltpu.make_async_copy(held_ref.at[a], grid_ref.at[a], out_sems.at[a]).wait()


def mixed_rows(rows, whi, wlo):
    hi, lo = split(rows)
    width = whi.shape[1]
    if width == 128 and rows.shape[1] == 128:
        left = jnp.concatenate([hi, lo], axis=1)
        right = jnp.concatenate(
            [jnp.concatenate([whi, wlo], axis=1), jnp.concatenate([whi, jnp.zeros_like(wlo)], axis=1)], axis=0
        )
        res = dot(left, right)
        return res[:, :128] + res[:, 128:]
    return dot(hi, whi) + dot(lo, whi) + dot(hi, wlo)


def mix_kernel(s, grid_ref, mix_ref, bias_ref, out_ref):
    whi, wlo = split(mix_ref[...])
    for y in range(s.Yl):
        out_ref[0, y] = mixed_rows(grid_ref[0, y], whi, wlo) + bias_ref[...]


def readout_kernel(s, grid_ref, mix_ref, out_ref):
    whi, wlo = split(mix_ref[...])
    lane = lax.broadcasted_iota(jnp.int32, (B, s.LB), 1)
    for a in range(B):
        total = jnp.zeros((B, s.LB), F32)
        for by in range(s.byn):
            res = mixed_rows(grid_ref[0, by * B + a], whi, wlo)
            for bz in range(s.NB):
                mine = (lane // (s.bxn * s.byn) == bz) & (lane % s.byn == by)
                total = jnp.where(mine, res[bz * B : (bz + 1) * B], total)
        out_ref[0, a * B : (a + 1) * B, :] = total


def x_forward_kernel(s, keep_ref, recv_ref, table_ref, out_ref):
    M = s.M
    for i in range(s.ny):
        parts = []
        for k in range(s.KL):
            kz = i * s.KL + k
            parts.append(
                jnp.concatenate(
                    [
                        ref[0, pl.ds(ri * s.KZ + kz, s.Xl, stride=s.K2), :]
                        for ri in range(2)
                        for ref in (keep_ref, recv_ref)
                    ],
                    axis=0,
                )
            )
        hi, lo = split(jnp.concatenate(parts, axis=1))
        res = dot(table_ref[...], jnp.concatenate([hi, lo], axis=0))
        res = res[: 2 * M] + res[2 * M :]
        rows = []
        for ri in range(2):
            for k in range(s.KL):
                rows.append(res[ri * M : (ri + 1) * M, k * s.LY : (k + 1) * s.LY])
        out_ref[i] = jnp.concatenate(rows, axis=0).T


def y_spectrum(s, in_ref, table, u_ref, v_ref, cs):
    M = s.M
    both = jnp.concatenate([in_ref[pl.ds(c, s.G, stride=s.cp), :] for c in cs], axis=1)
    hi, lo = split(both)
    res = dot(table, jnp.concatenate([hi, lo], axis=0))
    res = res[: 2 * M] + res[2 * M :]
    out = []
    plus = half_signs(M, s.LK, 1.0)
    for i, c in enumerate(cs):
        part = res[:, i * s.LK : (i + 1) * s.LK]
        wave = part[:M] + plus * swap_halves(part[M:])
        out.append(wave * u_ref[c] + swap_halves(wave) * v_ref[c])
    return out


def y_kernel(s, in_ref, fwd_ref, inv_ref, u_ref, v_ref, out_ref):
    minus = half_signs(s.M, s.LK, -1.0)
    for c in range(0, s.cp, 2):
        prods = y_spectrum(s, in_ref, fwd_ref[...], u_ref, v_ref, (c, c + 1))
        both = jnp.concatenate(
            [jnp.concatenate([p, minus * swap_halves(p)], axis=0) for p in prods], axis=1
        )
        hi, lo = split(both)
        res = dot(inv_ref[...], jnp.concatenate([hi, lo, hi], axis=0))
        for i in range(2):
            out_ref[pl.ds(c + i, s.G, stride=s.cp), :] = res[:, i * s.LK : (i + 1) * s.LK]


def y_last_kernel(s, in_ref, fwd_ref, u_ref, v_ref, out_ref):
    total = jnp.zeros((s.M, s.LK), F32)
    for c in range(0, s.cp, 2):
        prods = y_spectrum(s, in_ref, fwd_ref[...], u_ref, v_ref, (c, c + 1))
        total = total + prods[0] + prods[1]
    M = s.M
    for r in range(2 * s.KL):
        part = total[:, r * M : (r + 1) * M]
        out_ref[r : r + 1, :] = jnp.concatenate([part[m : m + 1] for m in range(M)], axis=1)


def x_inverse_kernel(s, in_ref, table_ref, keep_ref, send_ref):
    for i in range(s.ny):
        hi, lo = split(in_ref[i])
        if s.LK == 128:
            res = dot(table_ref[...], jnp.concatenate([hi, lo, hi], axis=1), NT)
        else:
            t = table_ref[...]
            res = dot(t[:, : s.LK], hi, NT) + dot(t[:, : s.LK], lo, NT) + dot(t[:, 2 * s.LK :], hi, NT)
        for k in range(s.KL):
            for ri in range(2):
                at = (k * 2 + ri) * 2 * s.Xl
                places = pl.ds(ri * s.KZ + i * s.KL + k, s.Xl, stride=s.K2)
                keep_ref[places, :] = res[at : at + s.Xl]
                send_ref[places, :] = res[at + s.Xl : at + 2 * s.Xl]


def gelu(x):
    inner = math.sqrt(2.0 / math.pi) * (x + 0.044715 * (x * x * x))
    return 0.5 * x * (1.0 + jnp.tanh(inner))


def layer_kernel(s, row_ref, mixed_ref, inv_ref, fwd_ref, *refs):
    in_refs, (grid_ref, keep_ref, send_ref) = refs[: s.nx], refs[s.nx :]
    row = row_ref[0]
    groups = by_distance(s, row, [[ref[0, b] for b in range(s.bxn)] for ref in in_refs])
    tiles = block_turn([tile for group in groups for tile in group], s.Yl, s.cp)
    for y in range(0, s.Yl, 2):
        hi, lo = split(jnp.concatenate([tiles[y], tiles[y + 1]], axis=1))
        res = dot(inv_ref[...], jnp.concatenate([hi, lo, hi], axis=0))
        for i in range(2):
            grid_ref[0, y + i] = gelu(mixed_ref[0, y + i] + res[:, i * s.L : (i + 1) * s.L])
    out = grid_to_spectrum(s, lambda y: grid_ref[0, y], fwd_ref[...])
    store_spectrum(s, row, 0, out, keep_ref, send_ref)


def decode_kernel(s, caps, *refs):
    n = len(caps)
    id_refs, num_refs, in_refs = refs[:n], refs[n : 2 * n], refs[2 * n : 3 * n]
    base_ref, spec_ref, turn_ref, mix_ref, hi_ref, lo_ref, inv_ref, out_ref, s_ref = refs[3 * n :]
    modes = jnp.concatenate([spec_ref[i] for i in range(s.ny)], axis=0)
    real_row = lax.broadcasted_iota(jnp.int32, modes.shape, 0) // s.KL % 2 == 0

    def partner(x):
        return jnp.where(real_row, -pltpu.roll(x, s.K2 - s.KL, 0), pltpu.roll(x, s.KL, 0))

    modes = modes * turn_ref[0:1, :] + partner(modes) * turn_ref[1:2, :]
    mhi, mlo = split(jnp.concatenate([modes, partner(modes)], axis=1))
    wave = dot(jnp.concatenate([mhi, mlo], axis=0), hi_ref[...])
    wave = wave[: s.K2] + wave[s.K2 :] + dot(mhi, lo_ref[...])
    hi, lo = split(wave)
    field = dot(inv_ref[...], jnp.concatenate([hi, lo, hi], axis=0))
    width = s.bxn * s.byn
    per = 128 // width
    for q in range(field.shape[1] // 128):
        tiles = [field[z * B : (z + 1) * B, q * 128 : (q + 1) * 128] for z in range(s.NB)]
        for i, tile in enumerate(block_turn(tiles, per, width)):
            at = (q * per + i) * B
            s_ref[at : at + B, :] = tile + mix_ref[at : at + B, :] + base_ref[0]
    out_ref[...] = jnp.zeros(out_ref.shape, F32)
    cell = lax.broadcasted_iota(jnp.int32, (s.LB, 128), 0)

    first = 0
    for cap, id_ref, num_ref, pos_ref in zip(caps, id_refs, num_refs, in_refs):
        decode_blocks(s, cap, sum(caps), first, id_ref, num_ref, pos_ref, cell, s_ref, out_ref)
        first += cap


def decode_blocks(s, cap, all_caps, first, id_ref, num_ref, pos_ref, cell, s_ref, out_ref):
    def per_source(src, carry):
        def per_pair(h, inner):
            shi, slo = split(s_ref[...])
            picks = []
            for i in range(2):
                at = id_ref[6, src * cap + h * 2 + i]
                picks.append(jnp.where(cell == at, 1.0, 0.0).astype(BF))
            pick = jnp.concatenate(picks, axis=1)
            if s.LB == 128:
                vals = dot(jnp.concatenate([shi, slo], axis=1), jnp.concatenate([pick, pick], axis=0))
            else:
                vals = dot(shi, pick) + dot(slo, pick)
            for i in range(2):
                j = h * 2 + i
                slot = src * cap + j
                points = [
                    jnp.broadcast_to(pos_ref[src, pl.ds(d * cap + j, 1), :], (8, 128))
                    - id_ref[3 + d, slot].astype(F32)
                    for d in range(3)
                ]
                top = jnp.zeros((B, 128), F32)
                low = jnp.zeros((B, 128), F32)
                for n, tile in enumerate(kernel_tiles(points)):
                    top = top + tile * vals[n * B : (n + 1) * B, i * 128 : (i + 1) * 128]
                    low = low + tile
                top = jnp.sum(top, axis=0, keepdims=True)
                low = jnp.sum(low, axis=0, keepdims=True)
                out_ref[pl.ds(src * all_caps + first + j, 1), :] = top / jnp.where(low > 0.0, low, 1.0)
            return inner

        return lax.fori_loop(0, (num_ref[src] + 1) // 2, per_pair, carry)

    lax.fori_loop(0, s.ny, per_source, 0)


def per_device(
    positions,
    point_feat,
    area,
    block_brick,
    block_count,
    sdf,
    grid_gain,
    mix_w,
    mix_b,
    spec_w,
    readout_w,
):
    nx, ny = lax.axis_size("gx"), lax.axis_size("gy")
    row_x, row_y = lax.axis_index("gx"), lax.axis_index("gy")
    modes = math.isqrt(spec_w.shape[4])
    s = Sizes(nx, ny, sdf.shape[2], point_feat.shape[0], modes, spec_w.shape[2] * ny)
    t = {name: jnp.asarray(value) for name, value in make_tables(s).items()}
    shape = lambda *dims: jax.ShapeDtypeStruct(dims, F32)
    blocks = block_brick.shape[0]
    cap = blocks // ny
    PB = positions.shape[1] // blocks
    C, G, M, L = s.C, s.G, s.M, s.L
    large = cap * 5 // 16 * 2
    caps = (large, cap - large)

    *outgoing, slot_of = call(
        functools.partial(pack_kernel, s, caps),
        "pack",
        tuple(shape(ny, part * (C + 3), PB) for part in caps) + (jax.ShapeDtypeStruct((blocks,), jnp.int32),),
        [SM, SM, VM, VM, VM],
        (VM,) * len(caps) + (SM,),
        1e6,
        6e6,
        scratch=[pltpu.SMEM((ny,), jnp.int32)],
    )(block_brick, block_count, positions, point_feat, area.reshape(blocks, PB))
    early, late = (lax.all_to_all(part, "gy", split_axis=0, concat_axis=0, tiled=True) for part in outgoing)

    def placement(incoming, cap):
        in_pos = incoming[:, cap * C :, :]
        first = in_pos.reshape(ny, 3, cap, PB)[..., 0].transpose(1, 0, 2).reshape(3, ny * cap)
        counts = jnp.sum((first[0].reshape(ny, cap) >= 0.0).astype(jnp.int32), axis=1)
        brick = jnp.floor(first / B).astype(jnp.int32)
        start = jnp.stack([row_x * s.bxn, row_y * s.byn, jnp.zeros_like(row_x)])
        limit = jnp.array([s.bxn - 1, s.byn - 1, s.NB - 1], jnp.int32)
        local = jnp.clip(brick - start[:, None], 0, limit[:, None])
        corner = (local + start[:, None]) * B
        flat = local[2] * (s.bxn * s.byn) + local[0] * s.byn + local[1]
        owned = jnp.where(first[0:1] >= 0.0, local[0:1], -1)
        ids = jnp.concatenate([owned, local[1:], corner, flat[None], flat[None]], axis=0)
        return ids, counts, in_pos

    lane = jnp.arange(L)
    lane_bx = lane // s.cp % s.bxn
    same_bx = lane_bx[:, None] == lane_bx[None, :]
    gain_l = jnp.broadcast_to(grid_gain.reshape(nx, 1, s.cp), (nx, s.bxn, s.cp)).reshape(L)
    spread = (
        (jnp.arange(s.bxn)[:, None, None, None] == lane_bx[None, None, None, :])
        & (jnp.arange(s.Yl)[None, :, None, None] == jnp.arange(s.Yl)[None, None, :, None])
    )
    gains = jnp.where(spread, gain_l, 0.0).reshape(s.bxn * s.Yl, s.Yl * L)
    grid_shape = shape(B, s.Yl, G, L)
    grid_block = pl.BlockSpec((1, s.Yl, G, L), lambda a: (a, 0, 0, 0))
    whole = lambda array: pl.BlockSpec(array.shape, lambda a: (0,) * array.ndim)
    init = call(
        functools.partial(field_kernel, s),
        "field",
        grid_shape,
        [pl.BlockSpec((s.bxn, None, s.Yl, G), lambda a: (0, a, 0, 0)), whole(gains)],
        grid_block,
        3e9,
        1e7,
        grid=(B,),
    )(sdf.reshape(s.bxn, B, s.Yl, G), gains)

    on_lanes = lambda v: jnp.broadcast_to(v.reshape(nx, 1, s.cp), (nx, s.bxn, s.cp)).reshape(1, L)
    mixing = mix_w[0].T.reshape(nx, 1, s.cp, nx, 1, s.cp)
    mixing = jnp.broadcast_to(mixing, (nx, s.bxn, s.cp, nx, s.bxn, s.cp)).reshape(L, L)
    mixing = jnp.where(same_bx, mixing, 0.0)
    bias = on_lanes(mix_b[0])
    read_mix = jnp.sum(readout_w[:, None] * mix_w[1], axis=0)
    base = jnp.sum(readout_w * mix_b[1]).reshape(1)
    out_lane = jnp.arange(s.LB)
    reading = jnp.where(lane_bx[:, None] == out_lane[None, :] // s.byn % s.bxn, on_lanes(read_mix).reshape(L, 1), 0.0)
    mine = lax.dynamic_slice_in_dim(readout_w, row_x * s.cp, s.cp)

    def multipliers(w, scale):
        w = w.reshape(2, s.KL, s.cp, M, M)
        if scale is not None:
            w = w * scale[None, None, :, None, None]
        w = w.transpose(2, 4, 0, 1, 3)
        u = jnp.concatenate([w[:, :, 0:1], w[:, :, 0:1]], axis=2).reshape(s.cp, M, s.LK)
        v = jnp.concatenate([-w[:, :, 1:2], w[:, :, 1:2]], axis=2).reshape(s.cp, M, s.LK)
        return u, v

    u0, v0 = multipliers(spec_w[0], None)
    u1, v1 = multipliers(spec_w[1], mine)

    freq = jnp.asarray(s.freq, jnp.int32)
    turn = jnp.mod(freq[None, :] * (row_x * s.Xl) + freq[:, None] * (row_y * s.Yl), G).reshape(1, -1)
    angle = turn.astype(F32) * (2.0 * math.pi / G)
    turns = jnp.concatenate([jnp.cos(angle), jnp.sin(angle)], axis=0)
    x_fwd = lax.dynamic_index_in_dim(t["x_fwd"], row_x, 0, False)
    x_inv = lax.dynamic_index_in_dim(t["x_inv"], row_x, 0, False)
    row = row_x.astype(jnp.int32).reshape(1)
    prepared = (early, init, mixing, bias, base, reading, u0, v0, u1, v1, turns, x_fwd, x_inv, row)
    early, init, mixing, bias, base, reading, u0, v0, u1, v1, turns, x_fwd, x_inv, row = (
        lax.optimization_barrier(prepared)
    )
    ids_a, counts_a, pos_a = placement(early, caps[0])
    ids_b, counts_b, pos_b = placement(late, caps[1])

    half = s.nx // 2
    spec_shape = shape(half, B, s.bxn, s.K2, s.LY)
    before = call(
        functools.partial(encode_first_kernel, s, caps[0]),
        "encode_first",
        grid_shape,
        [SM, SM, VM, VM],
        VM,
        3e9,
        2e7,
    )(ids_a, counts_a, early, init)
    grid, keep, send = call(
        functools.partial(encode_last_kernel, s, caps[1]),
        "encode_last",
        (grid_shape, spec_shape, spec_shape),
        [SM, SM, SM, VM, pl.BlockSpec(memory_space=pl.ANY), VM],
        (pl.BlockSpec(memory_space=pl.ANY), VM, VM),
        4e9,
        2.2e7,
        scratch=[
            pltpu.VMEM(grid_shape.shape, F32),
            pltpu.VMEM(grid_shape.shape, F32),
            pltpu.SemaphoreType.DMA,
            pltpu.SemaphoreType.DMA((B,)),
        ],
    )(row, ids_b, counts_b, late, before, t["z_fwd"])

    def exchange(array, distance):
        return lax.ppermute(array, "gx", [(i, i ^ distance) for i in range(nx)])

    def to_modes(keep, send):
        recv = exchange(send, 1).reshape(half, s.Xl * s.K2, s.LY)
        keep = keep.reshape(half, s.Xl * s.K2, s.LY)

        def part(d):
            block = pl.BlockSpec((1, s.Xl * s.K2, s.LY), lambda i: (d, 0, 0))
            return call(
                functools.partial(x_forward_kernel, s),
                "x_forward",
                shape(ny, s.LY, s.LK),
                [block, block, pl.BlockSpec(x_fwd.shape, lambda i: (0, 0))],
                pl.BlockSpec((ny, s.LY, s.LK), lambda i: (0, 0, 0)),
                2e8,
                3e6,
                grid=(1,),
                room=16,
            )(keep, recv, x_fwd)

        others = [exchange(part(d), 2 * d) for d in range(1, half)]
        spec = part(0)
        for other in others:
            spec = spec + other
        spec = lax.all_to_all(spec, "gy", split_axis=0, concat_axis=0, tiled=True)
        return spec.reshape(G * s.cp, s.LK)

    spec = to_modes(keep, send)
    mixed = call(
        functools.partial(mix_kernel, s),
        "mix",
        grid_shape,
        [grid_block, whole(mixing), whole(bias)],
        grid_block,
        2e9,
        1.7e7,
        grid=(B,),
    )(grid, mixing, bias)
    spec = call(
        functools.partial(y_kernel, s), "y_both", shape(G * s.cp, s.LK), [VM] * 5, VM, 1e9, 2e6, room=16
    )(spec, t["y_fwd"], t["y_inv"], u0, v0)
    spec = lax.all_to_all(spec.reshape(ny, s.LY, s.LK), "gy", split_axis=0, concat_axis=0, tiled=True)
    near = [exchange(spec, 2 * d) for d in range(1, half)]
    mixed, *near = lax.optimization_barrier((mixed, *near))
    near = [spec] + near
    fields = []
    for item in near:
        own, other = call(
            functools.partial(x_inverse_kernel, s),
            "x_inverse",
            (shape(s.Xl * s.K2, s.LY),) * 2,
            [VM, VM],
            (VM, VM),
            3e8,
            3e6,
            room=16,
        )(item, x_inv)
        fields += [own, exchange(other, 1)]
    fields = [f.reshape(B, s.bxn, s.K2, s.LY) for f in fields]
    field_block = pl.BlockSpec((1, s.bxn, s.K2, s.LY), lambda a: (a, 0, 0, 0))
    spec_block = pl.BlockSpec((half, 1, s.bxn, s.K2, s.LY), lambda a: (0, a, 0, 0, 0))
    grid, keep, send = call(
        functools.partial(layer_kernel, s),
        "layer",
        (grid_shape, spec_shape, spec_shape),
        [SM, grid_block, whole(t["z_inv"]), whole(t["z_fwd"])] + [field_block] * nx,
        (grid_block, spec_block, spec_block),
        4e9,
        2.1e7,
        grid=(B,),
    )(row, mixed, t["z_inv"], t["z_fwd"], *fields)
    spec = to_modes(keep, send)
    read = call(
        functools.partial(readout_kernel, s),
        "readout",
        shape(B, B * B, s.LB),
        [grid_block, whole(reading)],
        pl.BlockSpec((1, B * B, s.LB), lambda a: (a, 0, 0)),
        2e9,
        9e6,
        grid=(B,),
    )(grid, reading)
    last = call(
        functools.partial(y_last_kernel, s), "y_last", shape(2 * s.KL, M * M), [VM] * 4, VM, 1e9, 1e6, room=16
    )(spec, t["y_fwd"], u1, v1)

    step = 1
    while step < nx:
        last = last + lax.ppermute(last, "gx", [(i, i ^ step) for i in range(nx)])
        step *= 2
    last = jnp.broadcast_to(last[None], (ny,) + last.shape)
    last = lax.all_to_all(last, "gy", split_axis=0, concat_axis=0, tiled=True)
    values = call(
        functools.partial(decode_kernel, s, caps),
        "decode",
        shape(ny * cap, PB),
        [SM] * 4 + [VM] * 2 + [SM] + [VM] * 6,
        VM,
        4e9,
        6e6,
        scratch=[pltpu.VMEM((B * B * B, s.LB), F32)],
        room=32,
    )(ids_a, ids_b, counts_a, counts_b, pos_a, pos_b, base, last, turns, read.reshape(B * B * B, s.LB), t["xy_hi"], t["xy_lo"], t["z_last"])
    returned = lax.all_to_all(values.reshape(ny, cap, PB), "gy", split_axis=0, concat_axis=0, tiled=True)
    choose = (slot_of[:, None] == jnp.arange(ny * cap, dtype=jnp.int32)[None, :]).astype(F32)
    pressure = jnp.dot(choose, returned.reshape(ny * cap, PB), precision=lax.Precision.HIGHEST)
    return pressure.reshape(blocks * PB)


def solution(mesh):
    placed = (
        P(None, ("gx", "gy")),
        P(None, ("gx", "gy")),
        P(("gx", "gy")),
        P(("gx", "gy")),
        P(("gx", "gy")),
        P("gx", "gy", None),
        P(),
        P(),
        P(),
        P(None, None, "gy", "gx", None),
        P(),
    )
    return jax.shard_map(
        per_device, mesh=mesh, in_specs=placed, out_specs=P(("gx", "gy")), check_vma=False
    )
```

```python
import functools
import math

import jax
import jax.numpy as jnp
import ml_dtypes
import numpy as np
from jax import lax
from jax.experimental import pallas as pl
from jax.experimental.pallas import tpu as pltpu
from jax.sharding import PartitionSpec as P

B = 8
BF = jnp.bfloat16
F32 = jnp.float32
VM = pl.BlockSpec(memory_space=pltpu.VMEM)
SM = pl.BlockSpec(memory_space=pltpu.SMEM)
MIB = 1024 * 1024


def split(x):
    hi = x.astype(BF)
    lo = (x - hi.astype(F32)).astype(BF)
    return hi, lo


def np_split(table):
    table = np.asarray(table, np.float64).astype(np.float32)
    hi = table.astype(ml_dtypes.bfloat16)
    lo = (table - hi.astype(np.float32)).astype(ml_dtypes.bfloat16)
    return hi, lo


def dot(a, b, contract=((1,), (0,))):
    return lax.dot_general(a, b, (contract, ((), ())), preferred_element_type=F32)


NT = ((1,), (1,))


def call(body, name, out_shape, in_specs, out_specs, flops, moved, grid=None, scratch=(), room=58):
    extra = {} if grid is None else {"grid": grid}
    return pl.pallas_call(
        body,
        name=name,
        out_shape=out_shape,
        in_specs=in_specs,
        out_specs=out_specs,
        scratch_shapes=list(scratch),
        compiler_params=pltpu.CompilerParams(vmem_limit_bytes=room * MIB),
        cost_estimate=pl.CostEstimate(flops=int(flops), bytes_accessed=int(moved), transcendentals=0),
        **extra,
    )


class Sizes:
    def __init__(self, nx, ny, grid, channels, modes, kz):
        self.nx, self.ny, self.G, self.C, self.M, self.KZ = nx, ny, grid, channels, modes, kz
        self.NB = grid // B
        self.bxn = self.NB // nx
        self.byn = self.NB // ny
        self.Xl = grid // nx
        self.Yl = grid // ny
        self.cp = channels // nx
        self.KL = kz // ny
        self.L = channels * self.bxn
        self.LY = self.Yl * self.cp
        self.LK = 2 * self.KL * modes
        self.K2 = 2 * kz
        self.LB = self.NB * self.bxn * self.byn
        self.freq = np.where(np.arange(modes) < modes // 2, np.arange(modes), np.arange(modes) - modes)


def trig(s, places, freqs):
    angle = (np.asarray(places)[:, None] * np.asarray(freqs)[None, :]) % s.G * (2.0 * np.pi / s.G)
    return np.cos(angle), np.sin(angle)


def stack_left(table):
    hi, lo = np_split(table)
    zero = np.zeros_like(lo)
    return np.concatenate([np.concatenate([hi, hi], 1), np.concatenate([lo, zero], 1)], 0)


def wide_left(table):
    hi, lo = np_split(table)
    return np.concatenate([hi, hi, lo], 1)


def make_tables(s):
    t = {}
    c, n = trig(s, np.arange(s.KZ), np.arange(s.G))
    t["z_fwd"] = stack_left(np.concatenate([c, -n], 0))
    back = np.where(np.arange(s.KZ) == 0, 1.0, 2.0)[None, :] / s.G
    c, n = trig(s, np.arange(s.G), np.arange(s.KZ))
    c, n = c * back, -n * back
    t["z_inv"] = wide_left(np.concatenate([c, n], 1))
    t["z_last"] = wide_left(np.stack([c.reshape(s.G, s.ny, s.KL), n.reshape(s.G, s.ny, s.KL)], 2).reshape(s.G, -1))
    local = np.arange(s.Xl).reshape(s.bxn, B).T.reshape(-1)
    fwd, inv = [], []
    for row in range(s.nx):
        places = np.concatenate([row * s.Xl + local, (row ^ 1) * s.Xl + local])
        c, n = trig(s, s.freq, places)
        fwd.append(stack_left(np.concatenate([np.concatenate([c, n], 1), np.concatenate([-n, c], 1)], 0)))
        c, n = c.T, n.T
        table = np.zeros((s.KL, 2, 2 * s.Xl, 2, s.KL, s.M))
        for k in range(s.KL):
            table[k, 0, :, 0, k], table[k, 0, :, 1, k] = c, -n
            table[k, 1, :, 0, k], table[k, 1, :, 1, k] = n, c
        inv.append(wide_left(table.reshape(4 * s.KL * s.Xl, s.LK) / s.G))
    t["x_fwd"] = np.stack(fwd)
    t["x_inv"] = np.stack(inv)
    c, n = trig(s, s.freq, np.arange(s.G))
    t["y_fwd"] = stack_left(np.concatenate([c, n], 0))
    t["y_inv"] = wide_left(np.concatenate([c.T, n.T], 1) / s.G)
    xs = (np.arange(s.bxn)[:, None] * B + np.arange(B)[None, :]).T.reshape(B, 1, s.bxn, 1)
    ys = (np.arange(s.byn)[:, None] * B + np.arange(B)[None, :]).T.reshape(1, B, 1, s.byn)
    full = (B, B, s.bxn, s.byn)
    xs, ys = np.broadcast_to(xs, full).reshape(-1), np.broadcast_to(ys, full).reshape(-1)
    turn = s.freq[None, :, None] * xs[None, None, :] + s.freq[:, None, None] * ys[None, None, :]
    angle = (turn % s.G).reshape(s.M * s.M, -1) * (2.0 * np.pi / s.G)
    t["xy_hi"], t["xy_lo"] = np_split(np.concatenate([np.cos(angle), np.sin(angle)], 0) / (s.G * s.G))
    return t


def block_turn(tiles, blocks, width):
    count = len(tiles)
    if count == blocks and count * width == 128:
        lane = lax.broadcasted_iota(jnp.int32, tiles[0].shape, 1) // width
        tiles = list(tiles)
        step = 1
        while step < count:
            upper = (lane & step) != 0
            for i in range(count):
                if i & step == 0:
                    a, b = tiles[i], tiles[i | step]
                    up = pltpu.roll(b, step * width, 1)
                    down = pltpu.roll(a, 128 - step * width, 1)
                    tiles[i] = jnp.where(upper, up, a)
                    tiles[i | step] = jnp.where(upper, b, down)
            step *= 2
        return tiles
    return [
        jnp.concatenate([tile[:, b * width : (b + 1) * width] for tile in tiles], axis=1)
        for b in range(blocks)
    ]


def swap_halves(x):
    half = x.shape[1] // 2
    if x.shape[1] == 128:
        return pltpu.roll(x, half, 1)
    return jnp.concatenate([x[:, half:], x[:, :half]], axis=1)


def half_signs(rows, width, first):
    lane = lax.broadcasted_iota(jnp.int32, (rows, width), 1)
    return jnp.where(lane < width // 2, first, -first).astype(F32)


def pack_kernel(s, caps, brick_ref, count_ref, pos_ref, feat_ref, area_ref, *refs):
    out_refs, (slot_ref, fill_ref) = refs[: len(caps)], refs[len(caps) :]
    blocks = brick_ref.shape[0]
    C = s.C
    for i in range(s.ny):
        fill_ref[i] = 0
        for out_ref in out_refs:
            out_ref[i] = jnp.full(out_ref.shape[1:], -1.0, F32)
    live = count_ref[0]

    def step(n, carry):
        @pl.when(n < live)
        def _():
            brick = brick_ref[n]
            dest = (brick // s.NB) % s.NB // s.byn
            order = fill_ref[dest]
            fill_ref[dest] = order + 1
            slot_ref[n] = dest * sum(caps) + order
            lanes = pl.ds(pl.multiple_of(n * 128, 128), 128)
            first = 0
            for cap, out_ref in zip(caps, out_refs):
                place = order - first

                @pl.when((place >= 0) & (place < cap))
                def _():
                    feats = feat_ref[:, lanes] * area_ref[pl.ds(n, 1), :]
                    out_ref[dest, pl.ds(pl.multiple_of(place * C, 8), C), :] = feats
                    points = pos_ref[:, lanes]
                    for d in range(3):
                        out_ref[dest, pl.ds(cap * C + d * cap + place, 1), :] = points[d : d + 1, :]

                first += cap

        @pl.when(n >= live)
        def _():
            slot_ref[n] = -1

        return carry

    lax.fori_loop(0, blocks, step, 0)


def field_kernel(s, sdf_ref, gain_ref, out_ref):
    hi, lo = split(sdf_ref[...].reshape(s.bxn * s.Yl, s.G).T)
    ghi, glo = split(gain_ref[...])
    wide = dot(hi, ghi) + dot(lo, ghi) + dot(hi, glo)
    for y in range(s.Yl):
        out_ref[0, y] = wide[:, y * s.L : (y + 1) * s.L]


def kernel_tiles(points):
    px, py, pz = points
    scale = 1.0 / B
    sub = lax.broadcasted_iota(jnp.int32, pz.shape, 0).astype(F32)
    gz = ((sub + 0.5) - pz) * scale
    gz = gz * gz
    gx = []
    gy = []
    for a in range(B):
        d = (px - (a + 0.5)) * scale
        gx.append(1.0 - d * d)
        d = (py - (a + 0.5)) * scale
        gy.append(d * d + gz)
    tiles = []
    for a in range(B):
        for b in range(B):
            t = jnp.maximum(gx[a] - gy[b], 0.0)
            tiles.append(t * t)
    return tiles


def by_distance(s, row, items):
    bit = 1
    while bit < s.nx:
        far = row & bit != 0
        items = [
            [jnp.where(far, b, a) for a, b in zip(items[e], items[e ^ bit])] for e in range(s.nx)
        ]
        bit *= 2
    return items


def store_spectrum(s, row, a, tiles, keep_ref, send_ref):
    groups = by_distance(s, row, [tiles[g * s.bxn : (g + 1) * s.bxn] for g in range(s.nx)])
    for e in range(s.nx):
        for b in range(s.bxn):
            (send_ref if e & 1 else keep_ref)[e // 2, a, b] = groups[e][b]


def grid_to_spectrum(s, rows_of, table):
    tiles = []
    for y in range(0, s.Yl, 2):
        both = jnp.concatenate([rows_of(y), rows_of(y + 1)], axis=1)
        hi, lo = split(both)
        res = dot(table, jnp.concatenate([hi, lo], axis=0))
        res = res[: s.K2] + res[s.K2 :]
        tiles += [res[:, : s.L], res[:, s.L :]]
    return block_turn(tiles, s.nx * s.bxn, s.cp)


def add_blocks(s, cap, id_ref, num_ref, in_ref, grid_ref):
    C = s.C
    group = lax.broadcasted_iota(jnp.int32, (s.L, 128), 0) // s.cp % s.bxn

    def per_source(src, carry):
        def per_pair(h, inner):
            results = []
            for i in range(2):
                j = h * 2 + i
                slot = src * cap + j
                points = [
                    jnp.broadcast_to(in_ref[src, pl.ds(cap * C + d * cap + j, 1), :], (8, 128))
                    - id_ref[3 + d, slot].astype(F32)
                    for d in range(3)
                ]
                weights = jnp.concatenate(kernel_tiles(points), axis=0)
                feats = in_ref[src, pl.ds(pl.multiple_of(j * C, 8), C), :]
                spread = []
                for g in range(s.nx):
                    spread += [feats[g * s.cp : (g + 1) * s.cp]] * s.bxn
                spread = jnp.where(group == id_ref[0, slot], jnp.concatenate(spread, axis=0), 0.0)
                whi, wlo = split(weights)
                fhi, flo = split(spread)
                left = jnp.concatenate([whi, wlo], axis=1)
                right = jnp.concatenate([fhi, fhi], axis=1)
                if s.L == 128:
                    under = jnp.concatenate([flo, jnp.zeros_like(flo)], axis=1)
                    res = dot(left, jnp.concatenate([right, under], axis=0), NT)
                    res = res[:, : s.L] + res[:, s.L :]
                else:
                    res = dot(left, right, NT) + dot(whi, flo, NT)
                results.append(res.reshape(B, B, B, s.L))
            for i in range(2):
                slot = src * cap + h * 2 + i
                ys = pl.ds(pl.multiple_of(id_ref[1, slot] * B, B), B)
                zs = pl.ds(pl.multiple_of(id_ref[2, slot] * B, B), B)
                grid_ref[:, ys, zs, :] = grid_ref[:, ys, zs, :] + results[i]
            return inner

        return lax.fori_loop(0, (num_ref[src] + 1) // 2, per_pair, carry)

    lax.fori_loop(0, s.ny, per_source, 0)


def encode_first_kernel(s, cap, id_ref, num_ref, in_ref, init_ref, grid_ref):
    for a in range(B):
        grid_ref[a] = init_ref[a]
    add_blocks(s, cap, id_ref, num_ref, in_ref, grid_ref)


def encode_last_kernel(
    s, cap, row_ref, id_ref, num_ref, in_ref, before_ref, table_ref, grid_ref, keep_ref, send_ref,
    sum_ref, held_ref, in_sem, out_sems
):
    fetch = pltpu.make_async_copy(before_ref, held_ref, in_sem)
    fetch.start()
    for a in range(B):
        sum_ref[a] = jnp.zeros(sum_ref.shape[1:], F32)
    add_blocks(s, cap, id_ref, num_ref, in_ref, sum_ref)
    fetch.wait()

    def transform(a, carry):
        held_ref[a] = held_ref[a] + sum_ref[a]
        pltpu.make_async_copy(held_ref.at[a], grid_ref.at[a], out_sems.at[a]).start()
        out = grid_to_spectrum(s, lambda y: held_ref[a, y], table_ref[...])
        store_spectrum(s, row_ref[0], a, out, keep_ref, send_ref)
        return carry

    lax.fori_loop(0, B, transform, 0)
    for a in range(B):
        pltpu.make_async_copy(held_ref.at[a], grid_ref.at[a], out_sems.at[a]).wait()


def mixed_rows(rows, whi, wlo):
    hi, lo = split(rows)
    width = whi.shape[1]
    if width == 128 and rows.shape[1] == 128:
        left = jnp.concatenate([hi, lo], axis=1)
        right = jnp.concatenate(
            [jnp.concatenate([whi, wlo], axis=1), jnp.concatenate([whi, jnp.zeros_like(wlo)], axis=1)], axis=0
        )
        res = dot(left, right)
        return res[:, :128] + res[:, 128:]
    return dot(hi, whi) + dot(lo, whi) + dot(hi, wlo)


def mix_kernel(s, grid_ref, mix_ref, bias_ref, out_ref):
    whi, wlo = split(mix_ref[...])
    for y in range(s.Yl):
        out_ref[0, y] = mixed_rows(grid_ref[0, y], whi, wlo) + bias_ref[...]


def readout_kernel(s, grid_ref, mix_ref, out_ref):
    whi, wlo = split(mix_ref[...])
    lane = lax.broadcasted_iota(jnp.int32, (B, s.LB), 1)
    for a in range(B):
        total = jnp.zeros((B, s.LB), F32)
        for by in range(s.byn):
            res = mixed_rows(grid_ref[0, by * B + a], whi, wlo)
            for bz in range(s.NB):
                mine = (lane // (s.bxn * s.byn) == bz) & (lane % s.byn == by)
                total = jnp.where(mine, res[bz * B : (bz + 1) * B], total)
        out_ref[0, a * B : (a + 1) * B, :] = total


def x_forward_kernel(s, keep_ref, recv_ref, table_ref, out_ref):
    M = s.M
    for i in range(s.ny):
        parts = []
        for k in range(s.KL):
            kz = i * s.KL + k
            parts.append(
                jnp.concatenate(
                    [
                        ref[0, pl.ds(ri * s.KZ + kz, s.Xl, stride=s.K2), :]
                        for ri in range(2)
                        for ref in (keep_ref, recv_ref)
                    ],
                    axis=0,
                )
            )
        hi, lo = split(jnp.concatenate(parts, axis=1))
        res = dot(table_ref[...], jnp.concatenate([hi, lo], axis=0))
        res = res[: 2 * M] + res[2 * M :]
        rows = []
        for ri in range(2):
            for k in range(s.KL):
                rows.append(res[ri * M : (ri + 1) * M, k * s.LY : (k + 1) * s.LY])
        out_ref[i] = jnp.concatenate(rows, axis=0).T


def y_spectrum(s, in_ref, table, u_ref, v_ref, cs):
    M = s.M
    both = jnp.concatenate([in_ref[pl.ds(c, s.G, stride=s.cp), :] for c in cs], axis=1)
    hi, lo = split(both)
    res = dot(table, jnp.concatenate([hi, lo], axis=0))
    res = res[: 2 * M] + res[2 * M :]
    out = []
    plus = half_signs(M, s.LK, 1.0)
    for i, c in enumerate(cs):
        part = res[:, i * s.LK : (i + 1) * s.LK]
        wave = part[:M] + plus * swap_halves(part[M:])
        out.append(wave * u_ref[c] + swap_halves(wave) * v_ref[c])
    return out


def y_kernel(s, in_ref, fwd_ref, inv_ref, u_ref, v_ref, out_ref):
    minus = half_signs(s.M, s.LK, -1.0)
    for c in range(0, s.cp, 2):
        prods = y_spectrum(s, in_ref, fwd_ref[...], u_ref, v_ref, (c, c + 1))
        both = jnp.concatenate(
            [jnp.concatenate([p, minus * swap_halves(p)], axis=0) for p in prods], axis=1
        )
        hi, lo = split(both)
        res = dot(inv_ref[...], jnp.concatenate([hi, lo, hi], axis=0))
        for i in range(2):
            out_ref[pl.ds(c + i, s.G, stride=s.cp), :] = res[:, i * s.LK : (i + 1) * s.LK]


def y_last_kernel(s, in_ref, fwd_ref, u_ref, v_ref, out_ref):
    total = jnp.zeros((s.M, s.LK), F32)
    for c in range(0, s.cp, 2):
        prods = y_spectrum(s, in_ref, fwd_ref[...], u_ref, v_ref, (c, c + 1))
        total = total + prods[0] + prods[1]
    M = s.M
    for r in range(2 * s.KL):
        part = total[:, r * M : (r + 1) * M]
        out_ref[r : r + 1, :] = jnp.concatenate([part[m : m + 1] for m in range(M)], axis=1)


def x_inverse_kernel(s, in_ref, table_ref, keep_ref, send_ref):
    for i in range(s.ny):
        hi, lo = split(in_ref[i])
        if s.LK == 128:
            res = dot(table_ref[...], jnp.concatenate([hi, lo, hi], axis=1), NT)
        else:
            t = table_ref[...]
            res = dot(t[:, : s.LK], hi, NT) + dot(t[:, : s.LK], lo, NT) + dot(t[:, 2 * s.LK :], hi, NT)
        for k in range(s.KL):
            for ri in range(2):
                at = (k * 2 + ri) * 2 * s.Xl
                places = pl.ds(ri * s.KZ + i * s.KL + k, s.Xl, stride=s.K2)
                keep_ref[places, :] = res[at : at + s.Xl]
                send_ref[places, :] = res[at + s.Xl : at + 2 * s.Xl]


def gelu(x):
    inner = math.sqrt(2.0 / math.pi) * (x + 0.044715 * (x * x * x))
    return 0.5 * x * (1.0 + jnp.tanh(inner))


def layer_kernel(s, row_ref, mixed_ref, inv_ref, fwd_ref, *refs):
    in_refs, (grid_ref, keep_ref, send_ref) = refs[: s.nx], refs[s.nx :]
    row = row_ref[0]
    groups = by_distance(s, row, [[ref[0, b] for b in range(s.bxn)] for ref in in_refs])
    tiles = block_turn([tile for group in groups for tile in group], s.Yl, s.cp)
    for y in range(0, s.Yl, 2):
        hi, lo = split(jnp.concatenate([tiles[y], tiles[y + 1]], axis=1))
        res = dot(inv_ref[...], jnp.concatenate([hi, lo, hi], axis=0))
        for i in range(2):
            grid_ref[0, y + i] = gelu(mixed_ref[0, y + i] + res[:, i * s.L : (i + 1) * s.L])
    out = grid_to_spectrum(s, lambda y: grid_ref[0, y], fwd_ref[...])
    store_spectrum(s, row, 0, out, keep_ref, send_ref)


def decode_kernel(s, caps, *refs):
    n = len(caps)
    id_refs, num_refs, in_refs = refs[:n], refs[n : 2 * n], refs[2 * n : 3 * n]
    col_ref, base_ref, turn_ref, mix_ref, hi_ref, lo_ref, inv_ref = refs[3 * n : 3 * n + 7]
    spec_refs, out_refs = refs[3 * n + 7 : 3 * n + 7 + s.ny], refs[3 * n + 7 + s.ny : 3 * n + 7 + 2 * s.ny]
    s_ref, modes_ref, out_ref = refs[3 * n + 7 + 2 * s.ny :]
    col = col_ref[0]
    for e in range(s.ny):
        for r in range(2 * s.KL):
            modes_ref[pl.ds((col ^ e) * 2 * s.KL + r, 1), :] = spec_refs[e][r : r + 1, :]
    modes = modes_ref[...]
    real_row = lax.broadcasted_iota(jnp.int32, modes.shape, 0) // s.KL % 2 == 0

    def partner(x):
        return jnp.where(real_row, -pltpu.roll(x, s.K2 - s.KL, 0), pltpu.roll(x, s.KL, 0))

    modes = modes * turn_ref[0:1, :] + partner(modes) * turn_ref[1:2, :]
    mhi, mlo = split(jnp.concatenate([modes, partner(modes)], axis=1))
    wave = dot(jnp.concatenate([mhi, mlo], axis=0), hi_ref[...])
    wave = wave[: s.K2] + wave[s.K2 :] + dot(mhi, lo_ref[...])
    hi, lo = split(wave)
    field = dot(inv_ref[...], jnp.concatenate([hi, lo, hi], axis=0))
    width = s.bxn * s.byn
    per = 128 // width
    for q in range(field.shape[1] // 128):
        tiles = [field[z * B : (z + 1) * B, q * 128 : (q + 1) * 128] for z in range(s.NB)]
        for i, tile in enumerate(block_turn(tiles, per, width)):
            at = (q * per + i) * B
            s_ref[at : at + B, :] = tile + mix_ref[at : at + B, :] + base_ref[0]
    out_ref[...] = jnp.zeros(out_ref.shape, F32)
    cell = lax.broadcasted_iota(jnp.int32, (s.LB, 128), 0)

    first = 0
    for cap, id_ref, num_ref, pos_ref in zip(caps, id_refs, num_refs, in_refs):
        decode_blocks(s, cap, sum(caps), first, id_ref, num_ref, pos_ref, cell, s_ref, out_ref)
        first += cap
    for e in range(s.ny):
        out_refs[e][...] = out_ref[pl.ds(pl.multiple_of((col ^ e) * sum(caps), 8), sum(caps)), :]


def return_kernel(s, cap, col_ref, slot_ref, *refs):
    in_refs, (out_ref, held_ref) = refs[: s.ny], refs[s.ny :]
    for e in range(s.ny):
        held_ref[pl.ds(pl.multiple_of((col_ref[0] ^ e) * cap, 8), cap), :] = in_refs[e][...]

    def step(n, carry):
        slot = slot_ref[n]
        line = held_ref[pl.ds(jnp.maximum(slot, 0), 1), :]
        out_ref[pl.ds(n, 1), :] = jnp.where(slot >= 0, line, 0.0)
        return carry

    lax.fori_loop(0, out_ref.shape[0], step, 0, unroll=4)


def decode_blocks(s, cap, all_caps, first, id_ref, num_ref, pos_ref, cell, s_ref, out_ref):
    def per_source(src, carry):
        def per_pair(h, inner):
            shi, slo = split(s_ref[...])
            picks = []
            for i in range(2):
                at = id_ref[6, src * cap + h * 2 + i]
                picks.append(jnp.where(cell == at, 1.0, 0.0).astype(BF))
            pick = jnp.concatenate(picks, axis=1)
            if s.LB == 128:
                vals = dot(jnp.concatenate([shi, slo], axis=1), jnp.concatenate([pick, pick], axis=0))
            else:
                vals = dot(shi, pick) + dot(slo, pick)
            for i in range(2):
                j = h * 2 + i
                slot = src * cap + j
                points = [
                    jnp.broadcast_to(pos_ref[src, pl.ds(d * cap + j, 1), :], (8, 128))
                    - id_ref[3 + d, slot].astype(F32)
                    for d in range(3)
                ]
                top = jnp.zeros((B, 128), F32)
                low = jnp.zeros((B, 128), F32)
                for n, tile in enumerate(kernel_tiles(points)):
                    top = top + tile * vals[n * B : (n + 1) * B, i * 128 : (i + 1) * 128]
                    low = low + tile
                top = jnp.sum(top, axis=0, keepdims=True)
                low = jnp.sum(low, axis=0, keepdims=True)
                out_ref[pl.ds(src * all_caps + first + j, 1), :] = top / jnp.where(low > 0.0, low, 1.0)
            return inner

        return lax.fori_loop(0, (num_ref[src] + 1) // 2, per_pair, carry)

    lax.fori_loop(0, s.ny, per_source, 0)


def per_device(
    positions,
    point_feat,
    area,
    block_brick,
    block_count,
    sdf,
    grid_gain,
    mix_w,
    mix_b,
    spec_w,
    readout_w,
):
    nx, ny = lax.axis_size("gx"), lax.axis_size("gy")
    row_x, row_y = lax.axis_index("gx"), lax.axis_index("gy")
    modes = math.isqrt(spec_w.shape[4])
    s = Sizes(nx, ny, sdf.shape[2], point_feat.shape[0], modes, spec_w.shape[2] * ny)
    t = {name: jnp.asarray(value) for name, value in make_tables(s).items()}
    shape = lambda *dims: jax.ShapeDtypeStruct(dims, F32)
    blocks = block_brick.shape[0]
    cap = blocks // ny
    PB = positions.shape[1] // blocks
    C, G, M, L = s.C, s.G, s.M, s.L
    large = cap * 5 // 16 * 2
    caps = (large, cap - large)

    *outgoing, slot_of = call(
        functools.partial(pack_kernel, s, caps),
        "pack",
        tuple(shape(ny, part * (C + 3), PB) for part in caps) + (jax.ShapeDtypeStruct((blocks,), jnp.int32),),
        [SM, SM, VM, VM, VM],
        (VM,) * len(caps) + (SM,),
        1e6,
        6e6,
        scratch=[pltpu.SMEM((ny,), jnp.int32)],
    )(block_brick, block_count, positions, point_feat, area.reshape(blocks, PB))
    early = lax.all_to_all(outgoing[0], "gy", split_axis=0, concat_axis=0, tiled=True)
    early, second = lax.optimization_barrier((early, outgoing[1]))
    late = lax.all_to_all(second, "gy", split_axis=0, concat_axis=0, tiled=True)

    def placement(incoming, cap):
        in_pos = incoming[:, cap * C :, :]
        first = in_pos.reshape(ny, 3, cap, PB)[..., 0].transpose(1, 0, 2).reshape(3, ny * cap)
        counts = jnp.sum((first[0].reshape(ny, cap) >= 0.0).astype(jnp.int32), axis=1)
        brick = jnp.floor(first / B).astype(jnp.int32)
        start = jnp.stack([row_x * s.bxn, row_y * s.byn, jnp.zeros_like(row_x)])
        limit = jnp.array([s.bxn - 1, s.byn - 1, s.NB - 1], jnp.int32)
        local = jnp.clip(brick - start[:, None], 0, limit[:, None])
        corner = (local + start[:, None]) * B
        flat = local[2] * (s.bxn * s.byn) + local[0] * s.byn + local[1]
        owned = jnp.where(first[0:1] >= 0.0, local[0:1], -1)
        ids = jnp.concatenate([owned, local[1:], corner, flat[None], flat[None]], axis=0)
        return ids, counts, in_pos

    lane = jnp.arange(L)
    lane_bx = lane // s.cp % s.bxn
    same_bx = lane_bx[:, None] == lane_bx[None, :]
    gain_l = jnp.broadcast_to(grid_gain.reshape(nx, 1, s.cp), (nx, s.bxn, s.cp)).reshape(L)
    spread = (
        (jnp.arange(s.bxn)[:, None, None, None] == lane_bx[None, None, None, :])
        & (jnp.arange(s.Yl)[None, :, None, None] == jnp.arange(s.Yl)[None, None, :, None])
    )
    gains = jnp.where(spread, gain_l, 0.0).reshape(s.bxn * s.Yl, s.Yl * L)
    grid_shape = shape(B, s.Yl, G, L)
    grid_block = pl.BlockSpec((1, s.Yl, G, L), lambda a: (a, 0, 0, 0))
    whole = lambda array: pl.BlockSpec(array.shape, lambda a: (0,) * array.ndim)
    init = call(
        functools.partial(field_kernel, s),
        "field",
        grid_shape,
        [pl.BlockSpec((s.bxn, None, s.Yl, G), lambda a: (0, a, 0, 0)), whole(gains)],
        grid_block,
        3e9,
        1e7,
        grid=(B,),
    )(sdf.reshape(s.bxn, B, s.Yl, G), gains)

    on_lanes = lambda v: jnp.broadcast_to(v.reshape(nx, 1, s.cp), (nx, s.bxn, s.cp)).reshape(1, L)
    mixing = mix_w[0].T.reshape(nx, 1, s.cp, nx, 1, s.cp)
    mixing = jnp.broadcast_to(mixing, (nx, s.bxn, s.cp, nx, s.bxn, s.cp)).reshape(L, L)
    mixing = jnp.where(same_bx, mixing, 0.0)
    bias = on_lanes(mix_b[0])
    read_mix = jnp.sum(readout_w[:, None] * mix_w[1], axis=0)
    base = jnp.sum(readout_w * mix_b[1]).reshape(1)
    out_lane = jnp.arange(s.LB)
    reading = jnp.where(lane_bx[:, None] == out_lane[None, :] // s.byn % s.bxn, on_lanes(read_mix).reshape(L, 1), 0.0)
    mine = lax.dynamic_slice_in_dim(readout_w, row_x * s.cp, s.cp)

    def multipliers(w, scale):
        w = w.reshape(2, s.KL, s.cp, M, M)
        if scale is not None:
            w = w * scale[None, None, :, None, None]
        w = w.transpose(2, 4, 0, 1, 3)
        u = jnp.concatenate([w[:, :, 0:1], w[:, :, 0:1]], axis=2).reshape(s.cp, M, s.LK)
        v = jnp.concatenate([-w[:, :, 1:2], w[:, :, 1:2]], axis=2).reshape(s.cp, M, s.LK)
        return u, v

    u0, v0 = multipliers(spec_w[0], None)
    u1, v1 = multipliers(spec_w[1], mine)

    freq = jnp.asarray(s.freq, jnp.int32)
    turn = jnp.mod(freq[None, :] * (row_x * s.Xl) + freq[:, None] * (row_y * s.Yl), G).reshape(1, -1)
    angle = turn.astype(F32) * (2.0 * math.pi / G)
    turns = jnp.concatenate([jnp.cos(angle), jnp.sin(angle)], axis=0)
    x_fwd = lax.dynamic_index_in_dim(t["x_fwd"], row_x, 0, False)
    x_inv = lax.dynamic_index_in_dim(t["x_inv"], row_x, 0, False)
    row = row_x.astype(jnp.int32).reshape(1)
    col = row_y.astype(jnp.int32).reshape(1)
    prepared = (early, init, mixing, bias, base, reading, u0, v0, u1, v1, turns, x_fwd, x_inv, row, col)
    early, init, mixing, bias, base, reading, u0, v0, u1, v1, turns, x_fwd, x_inv, row, col = (
        lax.optimization_barrier(prepared)
    )
    ids_a, counts_a, pos_a = placement(early, caps[0])
    ids_b, counts_b, pos_b = placement(late, caps[1])

    half = s.nx // 2
    spec_shape = shape(half, B, s.bxn, s.K2, s.LY)
    before = call(
        functools.partial(encode_first_kernel, s, caps[0]),
        "encode_first",
        grid_shape,
        [SM, SM, VM, VM],
        VM,
        3e9,
        2e7,
    )(ids_a, counts_a, early, init)
    grid, keep, send = call(
        functools.partial(encode_last_kernel, s, caps[1]),
        "encode_last",
        (grid_shape, spec_shape, spec_shape),
        [SM, SM, SM, VM, pl.BlockSpec(memory_space=pl.ANY), VM],
        (pl.BlockSpec(memory_space=pl.ANY), VM, VM),
        4e9,
        2.2e7,
        scratch=[
            pltpu.VMEM(grid_shape.shape, F32),
            pltpu.VMEM(grid_shape.shape, F32),
            pltpu.SemaphoreType.DMA,
            pltpu.SemaphoreType.DMA((B,)),
        ],
    )(row, ids_b, counts_b, late, before, t["z_fwd"])

    def exchange(array, distance):
        return lax.ppermute(array, "gx", [(i, i ^ distance) for i in range(nx)])

    def turned(array, distance):
        return lax.ppermute(array, "gy", [(i, i ^ distance) for i in range(ny)])

    def to_modes(keep, send, beside=None):
        recv = exchange(send, 1).reshape(half, s.Xl * s.K2, s.LY)
        keep = keep.reshape(half, s.Xl * s.K2, s.LY)

        def part(d):
            block = pl.BlockSpec((1, s.Xl * s.K2, s.LY), lambda i: (d, 0, 0))
            return call(
                functools.partial(x_forward_kernel, s),
                "x_forward",
                shape(ny, s.LY, s.LK),
                [block, block, pl.BlockSpec(x_fwd.shape, lambda i: (0, 0))],
                pl.BlockSpec((ny, s.LY, s.LK), lambda i: (0, 0, 0)),
                2e8,
                3e6,
                grid=(1,),
                room=16,
            )(keep, recv, x_fwd)

        others = [exchange(part(d), 2 * d) for d in range(1, half)]
        spec = part(0)
        if beside is not None:
            beside, *others = lax.optimization_barrier((beside(), *others))
        for other in others:
            spec = spec + other
        spec = lax.all_to_all(spec, "gy", split_axis=0, concat_axis=0, tiled=True)
        return spec.reshape(G * s.cp, s.LK), beside

    spec, unused = to_modes(keep, send)
    mixed = call(
        functools.partial(mix_kernel, s),
        "mix",
        grid_shape,
        [grid_block, whole(mixing), whole(bias)],
        grid_block,
        2e9,
        1.7e7,
        grid=(B,),
    )(grid, mixing, bias)
    spec = call(
        functools.partial(y_kernel, s), "y_both", shape(G * s.cp, s.LK), [VM] * 5, VM, 1e9, 2e6, room=16
    )(spec, t["y_fwd"], t["y_inv"], u0, v0)
    spec = lax.all_to_all(spec.reshape(ny, s.LY, s.LK), "gy", split_axis=0, concat_axis=0, tiled=True)
    near = [exchange(spec, 2 * d) for d in range(1, half)]
    mixed, *near = lax.optimization_barrier((mixed, *near))
    near = [spec] + near
    fields = []
    for item in near:
        own, other = call(
            functools.partial(x_inverse_kernel, s),
            "x_inverse",
            (shape(s.Xl * s.K2, s.LY),) * 2,
            [VM, VM],
            (VM, VM),
            3e8,
            3e6,
            room=16,
        )(item, x_inv)
        fields += [own, exchange(other, 1)]
    fields = [f.reshape(B, s.bxn, s.K2, s.LY) for f in fields]
    field_block = pl.BlockSpec((1, s.bxn, s.K2, s.LY), lambda a: (a, 0, 0, 0))
    spec_block = pl.BlockSpec((half, 1, s.bxn, s.K2, s.LY), lambda a: (0, a, 0, 0, 0))
    grid, keep, send = call(
        functools.partial(layer_kernel, s),
        "layer",
        (grid_shape, spec_shape, spec_shape),
        [SM, grid_block, whole(t["z_inv"]), whole(t["z_fwd"])] + [field_block] * nx,
        (grid_block, spec_block, spec_block),
        4e9,
        2.1e7,
        grid=(B,),
    )(row, mixed, t["z_inv"], t["z_fwd"], *fields)

    def readout():
        return call(
            functools.partial(readout_kernel, s),
            "readout",
            shape(B, B * B, s.LB),
            [grid_block, whole(reading)],
            pl.BlockSpec((1, B * B, s.LB), lambda a: (a, 0, 0)),
            2e9,
            9e6,
            grid=(B,),
        )(grid, reading)

    spec, read = to_modes(keep, send, readout)
    last = call(
        functools.partial(y_last_kernel, s), "y_last", shape(2 * s.KL, M * M), [VM] * 4, VM, 1e9, 1e6, room=16
    )(spec, t["y_fwd"], u1, v1)

    last = functools.reduce(jnp.add, [last] + [exchange(last, e) for e in range(1, nx)])
    pieces = [last] + [turned(last, e) for e in range(1, ny)]
    values = call(
        functools.partial(decode_kernel, s, caps),
        "decode",
        (shape(cap, PB),) * ny,
        [SM] * 4 + [VM] * 2 + [SM] * 2 + [VM] * (5 + ny),
        (VM,) * ny,
        4e9,
        6e6,
        scratch=[
            pltpu.VMEM((B * B * B, s.LB), F32),
            pltpu.VMEM((s.K2, M * M), F32),
            pltpu.VMEM((ny * cap, PB), F32),
        ],
        room=32,
    )(
        ids_a, ids_b, counts_a, counts_b, pos_a, pos_b, col, base, turns,
        read.reshape(B * B * B, s.LB), t["xy_hi"], t["xy_lo"], t["z_last"], *pieces,
    )
    values = [values[0]] + [turned(values[e], e) for e in range(1, ny)]
    pressure = call(
        functools.partial(return_kernel, s, cap),
        "return",
        shape(blocks, PB),
        [SM, SM] + [VM] * ny,
        VM,
        1e5,
        2e5,
        scratch=[pltpu.VMEM((ny * cap, PB), F32)],
        room=16,
    )(col, slot_of, *values)
    return pressure.reshape(blocks * PB)


def solution(mesh):
    placed = (
        P(None, ("gx", "gy")),
        P(None, ("gx", "gy")),
        P(("gx", "gy")),
        P(("gx", "gy")),
        P(("gx", "gy")),
        P("gx", "gy", None),
        P(),
        P(),
        P(),
        P(None, None, "gy", "gx", None),
        P(),
    )
    return jax.shard_map(
        per_device, mesh=mesh, in_specs=placed, out_specs=P(("gx", "gy")), check_vma=False
    )
```

```python
import functools
import math

import jax
import jax.numpy as jnp
import ml_dtypes
import numpy as np
from jax import lax
from jax.experimental import pallas as pl
from jax.experimental.pallas import tpu as pltpu
from jax.sharding import PartitionSpec as P

B = 8
BF = jnp.bfloat16
F32 = jnp.float32
VM = pl.BlockSpec(memory_space=pltpu.VMEM)
SM = pl.BlockSpec(memory_space=pltpu.SMEM)
MIB = 1024 * 1024


def split(x):
    hi = x.astype(BF)
    lo = (x - hi.astype(F32)).astype(BF)
    return hi, lo


def np_split(table):
    table = np.asarray(table, np.float64).astype(np.float32)
    hi = table.astype(ml_dtypes.bfloat16)
    lo = (table - hi.astype(np.float32)).astype(ml_dtypes.bfloat16)
    return hi, lo


def dot(a, b, contract=((1,), (0,))):
    return lax.dot_general(a, b, (contract, ((), ())), preferred_element_type=F32)


NT = ((1,), (1,))


def call(body, name, out_shape, in_specs, out_specs, flops, moved, grid=None, scratch=(), room=58):
    extra = {} if grid is None else {"grid": grid}
    return pl.pallas_call(
        body,
        name=name,
        out_shape=out_shape,
        in_specs=in_specs,
        out_specs=out_specs,
        scratch_shapes=list(scratch),
        compiler_params=pltpu.CompilerParams(vmem_limit_bytes=room * MIB),
        cost_estimate=pl.CostEstimate(flops=int(flops), bytes_accessed=int(moved), transcendentals=0),
        **extra,
    )


class Sizes:
    def __init__(self, nx, ny, grid, channels, modes, kz):
        self.nx, self.ny, self.G, self.C, self.M, self.KZ = nx, ny, grid, channels, modes, kz
        self.NB = grid // B
        self.bxn = self.NB // nx
        self.byn = self.NB // ny
        self.Xl = grid // nx
        self.Yl = grid // ny
        self.cp = channels // nx
        self.KL = kz // ny
        self.L = channels * self.bxn
        self.LY = self.Yl * self.cp
        self.LK = 2 * self.KL * modes
        self.K2 = 2 * kz
        self.LB = self.NB * self.bxn * self.byn
        self.freq = np.where(np.arange(modes) < modes // 2, np.arange(modes), np.arange(modes) - modes)


def trig(s, places, freqs):
    angle = (np.asarray(places)[:, None] * np.asarray(freqs)[None, :]) % s.G * (2.0 * np.pi / s.G)
    return np.cos(angle), np.sin(angle)


def stack_left(table):
    hi, lo = np_split(table)
    zero = np.zeros_like(lo)
    return np.concatenate([np.concatenate([hi, hi], 1), np.concatenate([lo, zero], 1)], 0)


def wide_left(table):
    hi, lo = np_split(table)
    return np.concatenate([hi, hi, lo], 1)


def make_tables(s):
    t = {}
    c, n = trig(s, np.arange(s.KZ), np.arange(s.G))
    t["z_fwd"] = stack_left(np.concatenate([c, -n], 0))
    back = np.where(np.arange(s.KZ) == 0, 1.0, 2.0)[None, :] / s.G
    c, n = trig(s, np.arange(s.G), np.arange(s.KZ))
    c, n = c * back, -n * back
    t["z_inv"] = wide_left(np.concatenate([c, n], 1))
    t["z_last"] = wide_left(np.stack([c.reshape(s.G, s.ny, s.KL), n.reshape(s.G, s.ny, s.KL)], 2).reshape(s.G, -1))
    local = np.arange(s.Xl).reshape(s.bxn, B).T.reshape(-1)
    fwd, inv = [], []
    for row in range(s.nx):
        places = np.concatenate([row * s.Xl + local, (row ^ 1) * s.Xl + local])
        c, n = trig(s, s.freq, places)
        fwd.append(stack_left(np.concatenate([np.concatenate([c, n], 1), np.concatenate([-n, c], 1)], 0)))
        c, n = c.T, n.T
        table = np.zeros((s.KL, 2, 2 * s.Xl, 2, s.KL, s.M))
        for k in range(s.KL):
            table[k, 0, :, 0, k], table[k, 0, :, 1, k] = c, -n
            table[k, 1, :, 0, k], table[k, 1, :, 1, k] = n, c
        inv.append(wide_left(table.reshape(4 * s.KL * s.Xl, s.LK) / s.G))
    t["x_fwd"] = np.stack(fwd)
    t["x_inv"] = np.stack(inv)
    c, n = trig(s, s.freq, np.arange(s.G))
    t["y_fwd"] = stack_left(np.concatenate([c, n], 0))
    t["y_inv"] = wide_left(np.concatenate([c.T, n.T], 1) / s.G)
    xs = (np.arange(s.bxn)[:, None] * B + np.arange(B)[None, :]).T.reshape(B, 1, s.bxn, 1)
    ys = (np.arange(s.byn)[:, None] * B + np.arange(B)[None, :]).T.reshape(1, B, 1, s.byn)
    full = (B, B, s.bxn, s.byn)
    xs, ys = np.broadcast_to(xs, full).reshape(-1), np.broadcast_to(ys, full).reshape(-1)
    turn = s.freq[None, :, None] * xs[None, None, :] + s.freq[:, None, None] * ys[None, None, :]
    angle = (turn % s.G).reshape(s.M * s.M, -1) * (2.0 * np.pi / s.G)
    t["xy_hi"], t["xy_lo"] = np_split(np.concatenate([np.cos(angle), np.sin(angle)], 0) / (s.G * s.G))
    return t


def block_turn(tiles, blocks, width):
    count = len(tiles)
    if count == blocks and count * width == 128:
        lane = lax.broadcasted_iota(jnp.int32, tiles[0].shape, 1) // width
        tiles = list(tiles)
        step = 1
        while step < count:
            upper = (lane & step) != 0
            for i in range(count):
                if i & step == 0:
                    a, b = tiles[i], tiles[i | step]
                    up = pltpu.roll(b, step * width, 1)
                    down = pltpu.roll(a, 128 - step * width, 1)
                    tiles[i] = jnp.where(upper, up, a)
                    tiles[i | step] = jnp.where(upper, b, down)
            step *= 2
        return tiles
    return [
        jnp.concatenate([tile[:, b * width : (b + 1) * width] for tile in tiles], axis=1)
        for b in range(blocks)
    ]


def swap_halves(x):
    half = x.shape[1] // 2
    if x.shape[1] == 128:
        return pltpu.roll(x, half, 1)
    return jnp.concatenate([x[:, half:], x[:, :half]], axis=1)


def half_signs(rows, width, first):
    lane = lax.broadcasted_iota(jnp.int32, (rows, width), 1)
    return jnp.where(lane < width // 2, first, -first).astype(F32)


def pack_kernel(s, caps, brick_ref, count_ref, pos_ref, feat_ref, area_ref, *refs):
    out_refs, (slot_ref, fill_ref) = refs[: len(caps)], refs[len(caps) :]
    blocks = brick_ref.shape[0]
    C = s.C
    for i in range(s.ny):
        fill_ref[i] = 0
        for out_ref in out_refs:
            out_ref[i] = jnp.full(out_ref.shape[1:], -1.0, F32)
    live = count_ref[0]

    def step(n, carry):
        @pl.when(n < live)
        def _():
            brick = brick_ref[n]
            dest = (brick // s.NB) % s.NB // s.byn
            order = fill_ref[dest]
            fill_ref[dest] = order + 1
            slot_ref[n] = dest * sum(caps) + order
            lanes = pl.ds(pl.multiple_of(n * 128, 128), 128)
            first = 0
            for cap, out_ref in zip(caps, out_refs):
                place = order - first

                @pl.when((place >= 0) & (place < cap))
                def _():
                    feats = feat_ref[:, lanes] * area_ref[pl.ds(n, 1), :]
                    out_ref[dest, pl.ds(pl.multiple_of(place * C, 8), C), :] = feats
                    points = pos_ref[:, lanes]
                    for d in range(3):
                        out_ref[dest, pl.ds(cap * C + d * cap + place, 1), :] = points[d : d + 1, :]

                first += cap

        @pl.when(n >= live)
        def _():
            slot_ref[n] = -1

        return carry

    lax.fori_loop(0, blocks, step, 0)


def field_kernel(s, sdf_ref, gain_ref, out_ref):
    hi, lo = split(sdf_ref[...].reshape(s.bxn * s.Yl, s.G).T)
    ghi, glo = split(gain_ref[...])
    wide = dot(hi, ghi) + dot(lo, ghi) + dot(hi, glo)
    for y in range(s.Yl):
        out_ref[0, y] = wide[:, y * s.L : (y + 1) * s.L]


def kernel_tiles(points):
    px, py, pz = points
    scale = 1.0 / B
    sub = lax.broadcasted_iota(jnp.int32, pz.shape, 0).astype(F32)
    gz = ((sub + 0.5) - pz) * scale
    gz = gz * gz
    gx = []
    gy = []
    for a in range(B):
        d = (px - (a + 0.5)) * scale
        gx.append(1.0 - d * d)
        d = (py - (a + 0.5)) * scale
        gy.append(d * d + gz)
    tiles = []
    for a in range(B):
        for b in range(B):
            t = jnp.maximum(gx[a] - gy[b], 0.0)
            tiles.append(t * t)
    return tiles


def by_distance(s, row, items):
    bit = 1
    while bit < s.nx:
        far = row & bit != 0
        items = [
            [jnp.where(far, b, a) for a, b in zip(items[e], items[e ^ bit])] for e in range(s.nx)
        ]
        bit *= 2
    return items


def store_spectrum(s, row, a, tiles, keep_ref, send_ref):
    groups = by_distance(s, row, [tiles[g * s.bxn : (g + 1) * s.bxn] for g in range(s.nx)])
    for e in range(s.nx):
        for b in range(s.bxn):
            (send_ref if e & 1 else keep_ref)[e // 2, a, b] = groups[e][b]


def grid_to_spectrum(s, rows_of, table):
    tiles = []
    for y in range(0, s.Yl, 2):
        both = jnp.concatenate([rows_of(y), rows_of(y + 1)], axis=1)
        hi, lo = split(both)
        res = dot(table, jnp.concatenate([hi, lo], axis=0))
        res = res[: s.K2] + res[s.K2 :]
        tiles += [res[:, : s.L], res[:, s.L :]]
    return block_turn(tiles, s.nx * s.bxn, s.cp)


def add_blocks(s, cap, id_ref, num_ref, in_ref, grid_ref):
    C = s.C
    group = lax.broadcasted_iota(jnp.int32, (s.L, 128), 0) // s.cp % s.bxn

    def per_source(src, carry):
        def per_pair(h, inner):
            results = []
            for i in range(2):
                j = h * 2 + i
                slot = src * cap + j
                points = [
                    jnp.broadcast_to(in_ref[src, pl.ds(cap * C + d * cap + j, 1), :], (8, 128))
                    - id_ref[3 + d, slot].astype(F32)
                    for d in range(3)
                ]
                weights = jnp.concatenate(kernel_tiles(points), axis=0)
                feats = in_ref[src, pl.ds(pl.multiple_of(j * C, 8), C), :]
                spread = []
                for g in range(s.nx):
                    spread += [feats[g * s.cp : (g + 1) * s.cp]] * s.bxn
                spread = jnp.where(group == id_ref[0, slot], jnp.concatenate(spread, axis=0), 0.0)
                whi, wlo = split(weights)
                fhi, flo = split(spread)
                left = jnp.concatenate([whi, wlo], axis=1)
                right = jnp.concatenate([fhi, fhi], axis=1)
                if s.L == 128:
                    under = jnp.concatenate([flo, jnp.zeros_like(flo)], axis=1)
                    res = dot(left, jnp.concatenate([right, under], axis=0), NT)
                    res = res[:, : s.L] + res[:, s.L :]
                else:
                    res = dot(left, right, NT) + dot(whi, flo, NT)
                results.append(res.reshape(B, B, B, s.L))
            for i in range(2):
                slot = src * cap + h * 2 + i
                ys = pl.ds(pl.multiple_of(id_ref[1, slot] * B, B), B)
                zs = pl.ds(pl.multiple_of(id_ref[2, slot] * B, B), B)
                grid_ref[:, ys, zs, :] = grid_ref[:, ys, zs, :] + results[i]
            return inner

        return lax.fori_loop(0, (num_ref[src] + 1) // 2, per_pair, carry)

    lax.fori_loop(0, s.ny, per_source, 0)


def encode_first_kernel(s, cap, id_ref, num_ref, in_ref, init_ref, grid_ref):
    for a in range(B):
        grid_ref[a] = init_ref[a]
    add_blocks(s, cap, id_ref, num_ref, in_ref, grid_ref)


def encode_last_kernel(
    s, cap, row_ref, id_ref, num_ref, in_ref, before_ref, table_ref, grid_ref, keep_ref, send_ref,
    sum_ref, held_ref, in_sem, out_sems
):
    fetch = pltpu.make_async_copy(before_ref, held_ref, in_sem)
    fetch.start()
    for a in range(B):
        sum_ref[a] = jnp.zeros(sum_ref.shape[1:], F32)
    add_blocks(s, cap, id_ref, num_ref, in_ref, sum_ref)
    fetch.wait()

    def transform(a, carry):
        held_ref[a] = held_ref[a] + sum_ref[a]
        pltpu.make_async_copy(held_ref.at[a], grid_ref.at[a], out_sems.at[a]).start()
        out = grid_to_spectrum(s, lambda y: held_ref[a, y], table_ref[...])
        store_spectrum(s, row_ref[0], a, out, keep_ref, send_ref)
        return carry

    lax.fori_loop(0, B, transform, 0)
    for a in range(B):
        pltpu.make_async_copy(held_ref.at[a], grid_ref.at[a], out_sems.at[a]).wait()


def mixed_rows(rows, whi, wlo):
    hi, lo = split(rows)
    width = whi.shape[1]
    if width == 128 and rows.shape[1] == 128:
        left = jnp.concatenate([hi, lo], axis=1)
        right = jnp.concatenate(
            [jnp.concatenate([whi, wlo], axis=1), jnp.concatenate([whi, jnp.zeros_like(wlo)], axis=1)], axis=0
        )
        res = dot(left, right)
        return res[:, :128] + res[:, 128:]
    return dot(hi, whi) + dot(lo, whi) + dot(hi, wlo)


def mix_kernel(s, grid_ref, mix_ref, bias_ref, out_ref):
    whi, wlo = split(mix_ref[...])
    for y in range(s.Yl):
        out_ref[0, y] = mixed_rows(grid_ref[0, y], whi, wlo) + bias_ref[...]


def readout_kernel(s, grid_ref, mix_ref, out_ref):
    whi, wlo = split(mix_ref[...])
    lane = lax.broadcasted_iota(jnp.int32, (B, s.LB), 1)
    for a in range(B):
        total = jnp.zeros((B, s.LB), F32)
        for by in range(s.byn):
            res = mixed_rows(grid_ref[0, by * B + a], whi, wlo)
            for bz in range(s.NB):
                mine = (lane // (s.bxn * s.byn) == bz) & (lane % s.byn == by)
                total = jnp.where(mine, res[bz * B : (bz + 1) * B], total)
        out_ref[0, a * B : (a + 1) * B, :] = total


def x_forward_kernel(s, keep_ref, recv_ref, table_ref, out_ref):
    M = s.M
    for i in range(s.ny):
        parts = []
        for k in range(s.KL):
            kz = i * s.KL + k
            parts.append(
                jnp.concatenate(
                    [
                        ref[0, pl.ds(ri * s.KZ + kz, s.Xl, stride=s.K2), :]
                        for ri in range(2)
                        for ref in (keep_ref, recv_ref)
                    ],
                    axis=0,
                )
            )
        hi, lo = split(jnp.concatenate(parts, axis=1))
        res = dot(table_ref[...], jnp.concatenate([hi, lo], axis=0))
        res = res[: 2 * M] + res[2 * M :]
        rows = []
        for ri in range(2):
            for k in range(s.KL):
                rows.append(res[ri * M : (ri + 1) * M, k * s.LY : (k + 1) * s.LY])
        out_ref[i] = jnp.concatenate(rows, axis=0).T


def y_spectrum(s, in_ref, table, u_ref, v_ref, cs):
    M = s.M
    both = jnp.concatenate([in_ref[pl.ds(c, s.G, stride=s.cp), :] for c in cs], axis=1)
    hi, lo = split(both)
    res = dot(table, jnp.concatenate([hi, lo], axis=0))
    res = res[: 2 * M] + res[2 * M :]
    out = []
    plus = half_signs(M, s.LK, 1.0)
    for i, c in enumerate(cs):
        part = res[:, i * s.LK : (i + 1) * s.LK]
        wave = part[:M] + plus * swap_halves(part[M:])
        out.append(wave * u_ref[c] + swap_halves(wave) * v_ref[c])
    return out


def y_kernel(s, in_ref, fwd_ref, inv_ref, u_ref, v_ref, out_ref):
    minus = half_signs(s.M, s.LK, -1.0)
    for c in range(0, s.cp, 2):
        prods = y_spectrum(s, in_ref, fwd_ref[...], u_ref, v_ref, (c, c + 1))
        both = jnp.concatenate(
            [jnp.concatenate([p, minus * swap_halves(p)], axis=0) for p in prods], axis=1
        )
        hi, lo = split(both)
        res = dot(inv_ref[...], jnp.concatenate([hi, lo, hi], axis=0))
        for i in range(2):
            out_ref[pl.ds(c + i, s.G, stride=s.cp), :] = res[:, i * s.LK : (i + 1) * s.LK]


def y_last_kernel(s, in_ref, fwd_ref, u_ref, v_ref, out_ref):
    total = jnp.zeros((s.M, s.LK), F32)
    for c in range(0, s.cp, 2):
        prods = y_spectrum(s, in_ref, fwd_ref[...], u_ref, v_ref, (c, c + 1))
        total = total + prods[0] + prods[1]
    M = s.M
    for r in range(2 * s.KL):
        part = total[:, r * M : (r + 1) * M]
        out_ref[r : r + 1, :] = jnp.concatenate([part[m : m + 1] for m in range(M)], axis=1)


def x_inverse_kernel(s, in_ref, table_ref, keep_ref, send_ref):
    for i in range(s.ny):
        hi, lo = split(in_ref[i])
        if s.LK == 128:
            res = dot(table_ref[...], jnp.concatenate([hi, lo, hi], axis=1), NT)
        else:
            t = table_ref[...]
            res = dot(t[:, : s.LK], hi, NT) + dot(t[:, : s.LK], lo, NT) + dot(t[:, 2 * s.LK :], hi, NT)
        for k in range(s.KL):
            for ri in range(2):
                at = (k * 2 + ri) * 2 * s.Xl
                places = pl.ds(ri * s.KZ + i * s.KL + k, s.Xl, stride=s.K2)
                keep_ref[places, :] = res[at : at + s.Xl]
                send_ref[places, :] = res[at + s.Xl : at + 2 * s.Xl]


def gelu(x):
    inner = math.sqrt(2.0 / math.pi) * (x + 0.044715 * (x * x * x))
    return 0.5 * x * (1.0 + jnp.tanh(inner))


def layer_kernel(s, row_ref, mixed_ref, inv_ref, fwd_ref, *refs):
    in_refs, (grid_ref, keep_ref, send_ref) = refs[: s.nx], refs[s.nx :]
    row = row_ref[0]
    groups = by_distance(s, row, [[ref[0, b] for b in range(s.bxn)] for ref in in_refs])
    tiles = block_turn([tile for group in groups for tile in group], s.Yl, s.cp)
    for y in range(0, s.Yl, 2):
        hi, lo = split(jnp.concatenate([tiles[y], tiles[y + 1]], axis=1))
        res = dot(inv_ref[...], jnp.concatenate([hi, lo, hi], axis=0))
        for i in range(2):
            grid_ref[0, y + i] = gelu(mixed_ref[0, y + i] + res[:, i * s.L : (i + 1) * s.L])
    out = grid_to_spectrum(s, lambda y: grid_ref[0, y], fwd_ref[...])
    store_spectrum(s, row, 0, out, keep_ref, send_ref)


def decode_kernel(
    s, id_ref, base_ref, point_ref, spec_ref, turn_ref, mix_ref, hi_ref, lo_ref, inv_ref, out_ref, s_ref, list_ref
):
    modes = jnp.concatenate([spec_ref[i] for i in range(s.ny)], axis=0)
    real_row = lax.broadcasted_iota(jnp.int32, modes.shape, 0) // s.KL % 2 == 0

    def partner(x):
        return jnp.where(real_row, -pltpu.roll(x, s.K2 - s.KL, 0), pltpu.roll(x, s.KL, 0))

    modes = modes * turn_ref[0:1, :] + partner(modes) * turn_ref[1:2, :]
    mhi, mlo = split(jnp.concatenate([modes, partner(modes)], axis=1))
    wave = dot(jnp.concatenate([mhi, mlo], axis=0), hi_ref[...])
    wave = wave[: s.K2] + wave[s.K2 :] + dot(mhi, lo_ref[...])
    hi, lo = split(wave)
    field = dot(inv_ref[...], jnp.concatenate([hi, lo, hi], axis=0))
    width = s.bxn * s.byn
    per = 128 // width
    fields = []
    for q in range(field.shape[1] // 128):
        tiles = [field[z * B : (z + 1) * B, q * 128 : (q + 1) * 128] for z in range(s.NB)]
        for i, tile in enumerate(block_turn(tiles, per, width)):
            at = (q * per + i) * B
            fields.append(tile + mix_ref[at : at + B, :] + base_ref[0])
    out_ref[...] = jnp.zeros(out_ref.shape, F32)
    cell = lax.broadcasted_iota(jnp.int32, (s.LB, 128), 0)

    shi, slo = split(jnp.concatenate(fields, axis=0))
    s_ref[0], s_ref[1] = shi, slo
    slots = point_ref.shape[1]
    step = 4

    def collect(n, live):
        list_ref[live] = n
        return live + id_ref[1, n]

    live = lax.fori_loop(0, slots, collect, 0, unroll=8)
    for i in range(step):
        list_ref[live + i] = 0

    def per_group(h, carry):
        at = [list_ref[h * step + i] for i in range(step)]
        pick = jnp.concatenate([jnp.where(cell == id_ref[0, q], 1.0, 0.0).astype(BF) for q in at], axis=1)
        if s.LB == 128:
            vals = dot(jnp.concatenate([s_ref[0], s_ref[1]], axis=1), jnp.concatenate([pick, pick], axis=0))
        else:
            vals = dot(s_ref[0], pick) + dot(s_ref[1], pick)
        for i, q in enumerate(at):
            points = [jnp.broadcast_to(point_ref[d, pl.ds(q, 1), :], (8, 128)) for d in range(3)]
            top = jnp.zeros((B, 128), F32)
            low = jnp.zeros((B, 128), F32)
            for n, tile in enumerate(kernel_tiles(points)):
                top = top + tile * vals[n * B : (n + 1) * B, i * 128 : (i + 1) * 128]
                low = low + tile
            top = jnp.sum(top, axis=0, keepdims=True)
            low = jnp.sum(low, axis=0, keepdims=True)
            out_ref[pl.ds(id_ref[2, q], 1), :] = top / jnp.where(low > 0.0, low, 1.0)
        return carry

    lax.fori_loop(0, (live + step - 1) // step, per_group, 0)


def return_kernel(s, slot_ref, in_ref, out_ref):
    def step(n, carry):
        slot = slot_ref[n]
        line = in_ref[pl.ds(jnp.maximum(slot, 0), 1), :]
        out_ref[pl.ds(n, 1), :] = jnp.where(slot >= 0, line, 0.0)
        return carry

    lax.fori_loop(0, out_ref.shape[0], step, 0, unroll=8)


def per_device(
    positions,
    point_feat,
    area,
    block_brick,
    block_count,
    sdf,
    grid_gain,
    mix_w,
    mix_b,
    spec_w,
    readout_w,
):
    nx, ny = lax.axis_size("gx"), lax.axis_size("gy")
    row_x, row_y = lax.axis_index("gx"), lax.axis_index("gy")
    modes = math.isqrt(spec_w.shape[4])
    s = Sizes(nx, ny, sdf.shape[2], point_feat.shape[0], modes, spec_w.shape[2] * ny)
    t = {name: jnp.asarray(value) for name, value in make_tables(s).items()}
    shape = lambda *dims: jax.ShapeDtypeStruct(dims, F32)
    blocks = block_brick.shape[0]
    cap = blocks // ny
    PB = positions.shape[1] // blocks
    C, G, M, L = s.C, s.G, s.M, s.L
    large = cap * 5 // 16 * 2
    caps = (large, cap - large)

    *outgoing, slot_of = call(
        functools.partial(pack_kernel, s, caps),
        "pack",
        tuple(shape(ny, part * (C + 3), PB) for part in caps) + (jax.ShapeDtypeStruct((blocks,), jnp.int32),),
        [SM, SM, VM, VM, VM],
        (VM,) * len(caps) + (SM,),
        1e6,
        6e6,
        scratch=[pltpu.SMEM((ny,), jnp.int32)],
    )(block_brick, block_count, positions, point_feat, area.reshape(blocks, PB))
    early = lax.all_to_all(outgoing[0], "gy", split_axis=0, concat_axis=0, tiled=True)

    def placement(incoming, cap):
        in_pos = incoming[:, cap * C :, :]
        first = in_pos.reshape(ny, 3, cap, PB)[..., 0].transpose(1, 0, 2).reshape(3, ny * cap)
        counts = jnp.sum((first[0].reshape(ny, cap) >= 0.0).astype(jnp.int32), axis=1)
        brick = jnp.floor(first / B).astype(jnp.int32)
        start = jnp.stack([row_x * s.bxn, row_y * s.byn, jnp.zeros_like(row_x)])
        limit = jnp.array([s.bxn - 1, s.byn - 1, s.NB - 1], jnp.int32)
        local = jnp.clip(brick - start[:, None], 0, limit[:, None])
        corner = (local + start[:, None]) * B
        flat = local[2] * (s.bxn * s.byn) + local[0] * s.byn + local[1]
        owned = jnp.where(first[0:1] >= 0.0, local[0:1], -1)
        ids = jnp.concatenate([owned, local[1:], corner, flat[None], flat[None]], axis=0)
        return ids, counts, in_pos

    lane = jnp.arange(L)
    lane_bx = lane // s.cp % s.bxn
    same_bx = lane_bx[:, None] == lane_bx[None, :]
    gain_l = jnp.broadcast_to(grid_gain.reshape(nx, 1, s.cp), (nx, s.bxn, s.cp)).reshape(L)
    spread = (
        (jnp.arange(s.bxn)[:, None, None, None] == lane_bx[None, None, None, :])
        & (jnp.arange(s.Yl)[None, :, None, None] == jnp.arange(s.Yl)[None, None, :, None])
    )
    gains = jnp.where(spread, gain_l, 0.0).reshape(s.bxn * s.Yl, s.Yl * L)
    grid_shape = shape(B, s.Yl, G, L)
    grid_block = pl.BlockSpec((1, s.Yl, G, L), lambda a: (a, 0, 0, 0))
    whole = lambda array: pl.BlockSpec(array.shape, lambda a: (0,) * array.ndim)
    init = call(
        functools.partial(field_kernel, s),
        "field",
        grid_shape,
        [pl.BlockSpec((s.bxn, None, s.Yl, G), lambda a: (0, a, 0, 0)), whole(gains)],
        grid_block,
        3e9,
        1e7,
        grid=(B,),
    )(sdf.reshape(s.bxn, B, s.Yl, G), gains)

    on_lanes = lambda v: jnp.broadcast_to(v.reshape(nx, 1, s.cp), (nx, s.bxn, s.cp)).reshape(1, L)
    mixing = mix_w[0].T.reshape(nx, 1, s.cp, nx, 1, s.cp)
    mixing = jnp.broadcast_to(mixing, (nx, s.bxn, s.cp, nx, s.bxn, s.cp)).reshape(L, L)
    mixing = jnp.where(same_bx, mixing, 0.0)
    bias = on_lanes(mix_b[0])
    read_mix = jnp.sum(readout_w[:, None] * mix_w[1], axis=0)
    base = jnp.sum(readout_w * mix_b[1]).reshape(1)
    out_lane = jnp.arange(s.LB)
    reading = jnp.where(lane_bx[:, None] == out_lane[None, :] // s.byn % s.bxn, on_lanes(read_mix).reshape(L, 1), 0.0)
    mine = lax.dynamic_slice_in_dim(readout_w, row_x * s.cp, s.cp)

    def multipliers(w, scale):
        w = w.reshape(2, s.KL, s.cp, M, M)
        if scale is not None:
            w = w * scale[None, None, :, None, None]
        w = w.transpose(2, 4, 0, 1, 3)
        u = jnp.concatenate([w[:, :, 0:1], w[:, :, 0:1]], axis=2).reshape(s.cp, M, s.LK)
        v = jnp.concatenate([-w[:, :, 1:2], w[:, :, 1:2]], axis=2).reshape(s.cp, M, s.LK)
        return u, v

    u0, v0 = multipliers(spec_w[0], None)
    u1, v1 = multipliers(spec_w[1], mine)

    freq = jnp.asarray(s.freq, jnp.int32)
    turn = jnp.mod(freq[None, :] * (row_x * s.Xl) + freq[:, None] * (row_y * s.Yl), G).reshape(1, -1)
    angle = turn.astype(F32) * (2.0 * math.pi / G)
    turns = jnp.concatenate([jnp.cos(angle), jnp.sin(angle)], axis=0)
    x_fwd = lax.dynamic_index_in_dim(t["x_fwd"], row_x, 0, False)
    x_inv = lax.dynamic_index_in_dim(t["x_inv"], row_x, 0, False)
    row = row_x.astype(jnp.int32).reshape(1)
    prepared = (early, outgoing[1], init, mixing, bias, base, reading, u0, v0, u1, v1, turns, x_fwd, x_inv, row)
    early, second, init, mixing, bias, base, reading, u0, v0, u1, v1, turns, x_fwd, x_inv, row = (
        lax.optimization_barrier(prepared)
    )
    late = lax.all_to_all(second, "gy", split_axis=0, concat_axis=0, tiled=True)
    ids_a, counts_a, pos_a = placement(early, caps[0])
    ids_b, counts_b, pos_b = placement(late, caps[1])

    half = s.nx // 2
    spec_shape = shape(half, B, s.bxn, s.K2, s.LY)
    before = call(
        functools.partial(encode_first_kernel, s, caps[0]),
        "encode_first",
        grid_shape,
        [SM, SM, VM, VM],
        VM,
        3e9,
        2e7,
    )(ids_a, counts_a, early, init)
    grid, keep, send = call(
        functools.partial(encode_last_kernel, s, caps[1]),
        "encode_last",
        (grid_shape, spec_shape, spec_shape),
        [SM, SM, SM, VM, pl.BlockSpec(memory_space=pl.ANY), VM],
        (pl.BlockSpec(memory_space=pl.ANY), VM, VM),
        4e9,
        2.2e7,
        scratch=[
            pltpu.VMEM(grid_shape.shape, F32),
            pltpu.VMEM(grid_shape.shape, F32),
            pltpu.SemaphoreType.DMA,
            pltpu.SemaphoreType.DMA((B,)),
        ],
    )(row, ids_b, counts_b, late, before, t["z_fwd"])

    def exchange(array, distance):
        return lax.ppermute(array, "gx", [(i, i ^ distance) for i in range(nx)])

    def to_modes(keep, send, beside=None):
        recv = exchange(send, 1).reshape(half, s.Xl * s.K2, s.LY)
        keep = keep.reshape(half, s.Xl * s.K2, s.LY)

        def part(d):
            block = pl.BlockSpec((1, s.Xl * s.K2, s.LY), lambda i: (d, 0, 0))
            return call(
                functools.partial(x_forward_kernel, s),
                "x_forward",
                shape(ny, s.LY, s.LK),
                [block, block, pl.BlockSpec(x_fwd.shape, lambda i: (0, 0))],
                pl.BlockSpec((ny, s.LY, s.LK), lambda i: (0, 0, 0)),
                2e8,
                3e6,
                grid=(1,),
                room=16,
            )(keep, recv, x_fwd)

        others = [exchange(part(d), 2 * d) for d in range(1, half)]
        spec = part(0)
        if beside is not None:
            beside, *others = lax.optimization_barrier((beside(), *others))
        for other in others:
            spec = spec + other
        spec = lax.all_to_all(spec, "gy", split_axis=0, concat_axis=0, tiled=True)
        return spec.reshape(G * s.cp, s.LK), beside

    spec, unused = to_modes(keep, send)
    mixed = call(
        functools.partial(mix_kernel, s),
        "mix",
        grid_shape,
        [grid_block, whole(mixing), whole(bias)],
        grid_block,
        2e9,
        1.7e7,
        grid=(B,),
    )(grid, mixing, bias)
    spec = call(
        functools.partial(y_kernel, s), "y_both", shape(G * s.cp, s.LK), [VM] * 5, VM, 1e9, 2e6, room=16
    )(spec, t["y_fwd"], t["y_inv"], u0, v0)
    spec = lax.all_to_all(spec.reshape(ny, s.LY, s.LK), "gy", split_axis=0, concat_axis=0, tiled=True)
    near = [exchange(spec, 2 * d) for d in range(1, half)]
    mixed, *near = lax.optimization_barrier((mixed, *near))
    near = [spec] + near
    fields = []
    for item in near:
        own, other = call(
            functools.partial(x_inverse_kernel, s),
            "x_inverse",
            (shape(s.Xl * s.K2, s.LY),) * 2,
            [VM, VM],
            (VM, VM),
            3e8,
            3e6,
            room=16,
        )(item, x_inv)
        fields += [own, exchange(other, 1)]
    fields = [f.reshape(B, s.bxn, s.K2, s.LY) for f in fields]
    field_block = pl.BlockSpec((1, s.bxn, s.K2, s.LY), lambda a: (a, 0, 0, 0))
    spec_block = pl.BlockSpec((half, 1, s.bxn, s.K2, s.LY), lambda a: (0, a, 0, 0, 0))
    grid, keep, send = call(
        functools.partial(layer_kernel, s),
        "layer",
        (grid_shape, spec_shape, spec_shape),
        [SM, grid_block, whole(t["z_inv"]), whole(t["z_fwd"])] + [field_block] * nx,
        (grid_block, spec_block, spec_block),
        4e9,
        2.1e7,
        grid=(B,),
    )(row, mixed, t["z_inv"], t["z_fwd"], *fields)

    def readout():
        return call(
            functools.partial(readout_kernel, s),
            "readout",
            shape(B, B * B, s.LB),
            [grid_block, whole(reading)],
            pl.BlockSpec((1, B * B, s.LB), lambda a: (a, 0, 0)),
            2e9,
            9e6,
            grid=(B,),
        )(grid, reading), decode_places()

    def decode_places():
        points, bricks, live, places = [], [], [], []
        first = 0
        for part, ids, pos in ((caps[0], ids_a, pos_a), (caps[1], ids_b, pos_b)):
            pos = pos.reshape(ny, 3, part, PB).transpose(1, 0, 2, 3).reshape(3, ny * part, PB)
            points.append(pos - ids[3:6].astype(F32)[:, :, None])
            bricks.append(ids[6])
            live.append((ids[0] >= 0).astype(jnp.int32))
            places.append((jnp.arange(ny)[:, None] * cap + first + jnp.arange(part)[None, :]).reshape(-1))
            first += part
        where = [jnp.concatenate(v).astype(jnp.int32) for v in (bricks, live, places)]
        return jnp.concatenate(points, axis=1), jnp.stack(where)

    spec, (read, (points, where)) = to_modes(keep, send, readout)
    last = call(
        functools.partial(y_last_kernel, s), "y_last", shape(2 * s.KL, M * M), [VM] * 4, VM, 1e9, 1e6, room=16
    )(spec, t["y_fwd"], u1, v1)

    last = functools.reduce(jnp.add, [last] + [exchange(last, e) for e in range(1, nx)])
    last = jnp.broadcast_to(last[None], (ny,) + last.shape)
    last = lax.all_to_all(last, "gy", split_axis=0, concat_axis=0, tiled=True)
    values = call(
        functools.partial(decode_kernel, s),
        "decode",
        shape(ny * cap, PB),
        [SM, SM] + [VM] * 7,
        VM,
        4e9,
        6e6,
        scratch=[pltpu.VMEM((2, B * B * B, s.LB), BF), pltpu.SMEM((ny * cap + 8,), jnp.int32)],
        room=32,
    )(where, base, points, last, turns, read.reshape(B * B * B, s.LB), t["xy_hi"], t["xy_lo"], t["z_last"])
    returned = lax.all_to_all(values.reshape(ny, cap, PB), "gy", split_axis=0, concat_axis=0, tiled=True)
    pressure = call(
        functools.partial(return_kernel, s), "return", shape(blocks, PB), [SM, VM], VM, 1e5, 2e5, room=16
    )(slot_of, returned.reshape(ny * cap, PB))
    return pressure.reshape(blocks * PB)


def solution(mesh):
    placed = (
        P(None, ("gx", "gy")),
        P(None, ("gx", "gy")),
        P(("gx", "gy")),
        P(("gx", "gy")),
        P(("gx", "gy")),
        P("gx", "gy", None),
        P(),
        P(),
        P(),
        P(None, None, "gy", "gx", None),
        P(),
    )
    return jax.shard_map(
        per_device, mesh=mesh, in_specs=placed, out_specs=P(("gx", "gy")), check_vma=False
    )
```

```python
import functools
import math

import jax
import jax.numpy as jnp
import ml_dtypes
import numpy as np
from jax import lax
from jax.experimental import pallas as pl
from jax.experimental.pallas import tpu as pltpu
from jax.sharding import PartitionSpec as P

B = 8
BF = jnp.bfloat16
F32 = jnp.float32
VM = pl.BlockSpec(memory_space=pltpu.VMEM)
SM = pl.BlockSpec(memory_space=pltpu.SMEM)
MIB = 1024 * 1024


def split(x):
    hi = x.astype(BF)
    lo = (x - hi.astype(F32)).astype(BF)
    return hi, lo


def np_split(table):
    table = np.asarray(table, np.float64).astype(np.float32)
    hi = table.astype(ml_dtypes.bfloat16)
    lo = (table - hi.astype(np.float32)).astype(ml_dtypes.bfloat16)
    return hi, lo


def dot(a, b, contract=((1,), (0,))):
    return lax.dot_general(a, b, (contract, ((), ())), preferred_element_type=F32)


NT = ((1,), (1,))


def call(body, name, out_shape, in_specs, out_specs, flops, moved, grid=None, scratch=(), room=58):
    extra = {} if grid is None else {"grid": grid}
    return pl.pallas_call(
        body,
        name=name,
        out_shape=out_shape,
        in_specs=in_specs,
        out_specs=out_specs,
        scratch_shapes=list(scratch),
        compiler_params=pltpu.CompilerParams(vmem_limit_bytes=room * MIB),
        cost_estimate=pl.CostEstimate(flops=int(flops), bytes_accessed=int(moved), transcendentals=0),
        **extra,
    )


class Sizes:
    def __init__(self, nx, ny, grid, channels, modes, kz):
        self.nx, self.ny, self.G, self.C, self.M, self.KZ = nx, ny, grid, channels, modes, kz
        self.NB = grid // B
        self.bxn = self.NB // nx
        self.byn = self.NB // ny
        self.Xl = grid // nx
        self.Yl = grid // ny
        self.cp = channels // nx
        self.KL = kz // ny
        self.L = channels * self.bxn
        self.LY = self.Yl * self.cp
        self.LK = 2 * self.KL * modes
        self.K2 = 2 * kz
        self.LB = self.NB * self.bxn * self.byn
        self.freq = np.where(np.arange(modes) < modes // 2, np.arange(modes), np.arange(modes) - modes)


def trig(s, places, freqs):
    angle = (np.asarray(places)[:, None] * np.asarray(freqs)[None, :]) % s.G * (2.0 * np.pi / s.G)
    return np.cos(angle), np.sin(angle)


def stack_left(table):
    hi, lo = np_split(table)
    zero = np.zeros_like(lo)
    return np.concatenate([np.concatenate([hi, hi], 1), np.concatenate([lo, zero], 1)], 0)


def wide_left(table):
    hi, lo = np_split(table)
    return np.concatenate([hi, hi, lo], 1)


def make_tables(s):
    t = {}
    c, n = trig(s, np.arange(s.KZ), np.arange(s.G))
    t["z_fwd"] = stack_left(np.concatenate([c, -n], 0))
    back = np.where(np.arange(s.KZ) == 0, 1.0, 2.0)[None, :] / s.G
    c, n = trig(s, np.arange(s.G), np.arange(s.KZ))
    c, n = c * back, -n * back
    t["z_inv"] = wide_left(np.concatenate([c, n], 1))
    t["z_last"] = wide_left(np.stack([c.reshape(s.G, s.ny, s.KL), n.reshape(s.G, s.ny, s.KL)], 2).reshape(s.G, -1))
    local = np.arange(s.Xl).reshape(s.bxn, B).T.reshape(-1)
    fwd, inv = [], []
    for row in range(s.nx):
        places = np.concatenate([row * s.Xl + local, (row ^ 1) * s.Xl + local])
        c, n = trig(s, s.freq, places)
        fwd.append(stack_left(np.concatenate([np.concatenate([c, n], 1), np.concatenate([-n, c], 1)], 0)))
        c, n = c.T, n.T
        table = np.zeros((s.KL, 2, 2 * s.Xl, 2, s.KL, s.M))
        for k in range(s.KL):
            table[k, 0, :, 0, k], table[k, 0, :, 1, k] = c, -n
            table[k, 1, :, 0, k], table[k, 1, :, 1, k] = n, c
        inv.append(wide_left(table.reshape(4 * s.KL * s.Xl, s.LK) / s.G))
    t["x_fwd"] = np.stack(fwd)
    t["x_inv"] = np.stack(inv)
    c, n = trig(s, s.freq, np.arange(s.G))
    t["y_fwd"] = stack_left(np.concatenate([c, n], 0))
    t["y_inv"] = wide_left(np.concatenate([c.T, n.T], 1) / s.G)
    xs = (np.arange(s.bxn)[:, None] * B + np.arange(B)[None, :]).T.reshape(B, 1, s.bxn, 1)
    ys = (np.arange(s.byn)[:, None] * B + np.arange(B)[None, :]).T.reshape(1, B, 1, s.byn)
    full = (B, B, s.bxn, s.byn)
    xs, ys = np.broadcast_to(xs, full).reshape(-1), np.broadcast_to(ys, full).reshape(-1)
    turn = s.freq[None, :, None] * xs[None, None, :] + s.freq[:, None, None] * ys[None, None, :]
    angle = (turn % s.G).reshape(s.M * s.M, -1) * (2.0 * np.pi / s.G)
    t["xy_hi"], t["xy_lo"] = np_split(np.concatenate([np.cos(angle), np.sin(angle)], 0) / (s.G * s.G))
    return t


def block_turn(tiles, blocks, width):
    count = len(tiles)
    if count == blocks and count * width == 128:
        lane = lax.broadcasted_iota(jnp.int32, tiles[0].shape, 1) // width
        tiles = list(tiles)
        step = 1
        while step < count:
            upper = (lane & step) != 0
            for i in range(count):
                if i & step == 0:
                    a, b = tiles[i], tiles[i | step]
                    up = pltpu.roll(b, step * width, 1)
                    down = pltpu.roll(a, 128 - step * width, 1)
                    tiles[i] = jnp.where(upper, up, a)
                    tiles[i | step] = jnp.where(upper, b, down)
            step *= 2
        return tiles
    return [
        jnp.concatenate([tile[:, b * width : (b + 1) * width] for tile in tiles], axis=1)
        for b in range(blocks)
    ]


def swap_halves(x):
    half = x.shape[1] // 2
    if x.shape[1] == 128:
        return pltpu.roll(x, half, 1)
    return jnp.concatenate([x[:, half:], x[:, :half]], axis=1)


def half_signs(rows, width, first):
    lane = lax.broadcasted_iota(jnp.int32, (rows, width), 1)
    return jnp.where(lane < width // 2, first, -first).astype(F32)


def pack_kernel(s, caps, brick_ref, count_ref, pos_ref, feat_ref, area_ref, *refs):
    out_refs, (slot_ref, fill_ref, feat_out, pos_out) = refs[: len(caps)], refs[len(caps) :]
    blocks = brick_ref.shape[0]
    C, cap = s.C, sum(caps)
    for i in range(s.ny):
        fill_ref[i] = 0
        pos_out[i] = jnp.full(pos_out.shape[1:], -1.0, F32)
        feat_out[i] = jnp.zeros(feat_out.shape[1:], F32)
    fill_ref[s.ny] = 0
    live = count_ref[0]

    def place(n, carry):
        alive = n < live
        dest = jnp.where(alive, (brick_ref[n] // s.NB) % s.NB // s.byn, s.ny)
        order = jnp.where(alive, fill_ref[dest], 0)
        fill_ref[dest] = order + 1
        slot_ref[n] = jnp.where(alive, dest * cap + order, -1)
        lanes = pl.ds(pl.multiple_of(n * 128, 128), 128)
        feats = feat_ref[:, lanes] * area_ref[pl.ds(n, 1), :]
        feat_out[dest, pl.ds(pl.multiple_of(order * C, 8), C), :] = feats
        points = pos_ref[:, lanes]
        for d in range(3):
            pos_out[dest, d, pl.ds(order, 1), :] = points[d : d + 1, :]
        return carry

    lax.fori_loop(0, blocks, place, 0, unroll=8)
    first = 0
    for part, out_ref in zip(caps, out_refs):
        for i in range(s.ny):
            out_ref[i, : part * C] = feat_out[i, first * C : (first + part) * C]
            for d in range(3):
                at = part * C + d * part
                out_ref[i, at : at + part] = pos_out[i, d, first : first + part]
        first += part


def field_kernel(s, sdf_ref, gain_ref, out_ref):
    hi, lo = split(sdf_ref[...].reshape(s.bxn * s.Yl, s.G).T)
    ghi, glo = split(gain_ref[...])
    wide = dot(hi, ghi) + dot(lo, ghi) + dot(hi, glo)
    for y in range(s.Yl):
        out_ref[0, y] = wide[:, y * s.L : (y + 1) * s.L]


def kernel_tiles(points):
    px, py, pz = points
    scale = 1.0 / B
    sub = lax.broadcasted_iota(jnp.int32, pz.shape, 0).astype(F32)
    gz = ((sub + 0.5) - pz) * scale
    gz = gz * gz
    gx = []
    gy = []
    for a in range(B):
        d = (px - (a + 0.5)) * scale
        gx.append(1.0 - d * d)
        d = (py - (a + 0.5)) * scale
        gy.append(d * d + gz)
    tiles = []
    for a in range(B):
        for b in range(B):
            t = jnp.maximum(gx[a] - gy[b], 0.0)
            tiles.append(t * t)
    return tiles


def by_distance(s, row, items):
    bit = 1
    while bit < s.nx:
        far = row & bit != 0
        items = [
            [jnp.where(far, b, a) for a, b in zip(items[e], items[e ^ bit])] for e in range(s.nx)
        ]
        bit *= 2
    return items


def store_spectrum(s, row, a, tiles, keep_ref, send_ref):
    groups = by_distance(s, row, [tiles[g * s.bxn : (g + 1) * s.bxn] for g in range(s.nx)])
    for e in range(s.nx):
        for b in range(s.bxn):
            (send_ref if e & 1 else keep_ref)[e // 2, a, b] = groups[e][b]


def grid_to_spectrum(s, rows_of, table):
    tiles = []
    for y in range(0, s.Yl, 4):
        hi, lo = split(jnp.concatenate([rows_of(y + i) for i in range(4)], axis=1))
        res = dot(table, jnp.concatenate([hi, lo], axis=0))
        res = res[: s.K2] + res[s.K2 :]
        tiles += [res[:, i * s.L : (i + 1) * s.L] for i in range(4)]
    return block_turn(tiles, s.nx * s.bxn, s.cp)


def live_list(alive, slots, step, list_ref):
    def collect(n, live):
        list_ref[live] = n
        return live + alive(n)

    live = lax.fori_loop(0, slots, collect, 0, unroll=8)
    for i in range(step):
        list_ref[live + i] = 0
    return live


def add_blocks(s, cap, id_ref, in_ref, grid_ref, list_ref):
    C = s.C
    step = 4
    group = lax.broadcasted_iota(jnp.int32, (s.L, 128), 0) // s.cp % s.bxn
    live = live_list(lambda n: jnp.where(id_ref[0, n] >= 0, 1, 0), s.ny * cap, step, list_ref)

    def per_group(h, carry):
        results = []
        slots = [list_ref[h * step + i] for i in range(step)]
        for i, slot in enumerate(slots):
            src, j = slot // cap, slot % cap
            points = [
                jnp.broadcast_to(in_ref[src, pl.ds(cap * C + d * cap + j, 1), :], (8, 128))
                - id_ref[3 + d, slot].astype(F32)
                for d in range(3)
            ]
            weights = jnp.concatenate(kernel_tiles(points), axis=0)
            feats = in_ref[src, pl.ds(pl.multiple_of(j * C, 8), C), :]
            spread = []
            for g in range(s.nx):
                spread += [feats[g * s.cp : (g + 1) * s.cp]] * s.bxn
            mine = jnp.where(h * step + i < live, id_ref[0, slot], -1)
            spread = jnp.where(group == mine, jnp.concatenate(spread, axis=0), 0.0)
            whi, wlo = split(weights)
            fhi, flo = split(spread)
            left = jnp.concatenate([whi, wlo], axis=1)
            right = jnp.concatenate([fhi, fhi], axis=1)
            if s.L == 128:
                under = jnp.concatenate([flo, jnp.zeros_like(flo)], axis=1)
                res = dot(left, jnp.concatenate([right, under], axis=0), NT)
                res = res[:, : s.L] + res[:, s.L :]
            else:
                res = dot(left, right, NT) + dot(whi, flo, NT)
            results.append(res.reshape(B, B, B, s.L))
        for slot, res in zip(slots, results):
            ys = pl.ds(pl.multiple_of(id_ref[1, slot] * B, B), B)
            zs = pl.ds(pl.multiple_of(id_ref[2, slot] * B, B), B)
            grid_ref[:, ys, zs, :] = grid_ref[:, ys, zs, :] + res
        return carry

    lax.fori_loop(0, (live + step - 1) // step, per_group, 0)


def encode_first_kernel(s, cap, id_ref, in_ref, init_ref, grid_ref, list_ref):
    for a in range(B):
        grid_ref[a] = init_ref[a]
    add_blocks(s, cap, id_ref, in_ref, grid_ref, list_ref)


def encode_last_kernel(
    s, cap, row_ref, id_ref, in_ref, before_ref, table_ref, grid_ref, keep_ref, send_ref,
    list_ref, sum_ref, held_ref, in_sem, out_sems
):
    fetch = pltpu.make_async_copy(before_ref, held_ref, in_sem)
    fetch.start()
    for a in range(B):
        sum_ref[a] = jnp.zeros(sum_ref.shape[1:], F32)
    add_blocks(s, cap, id_ref, in_ref, sum_ref, list_ref)
    fetch.wait()

    def transform(a, carry):
        held_ref[a] = held_ref[a] + sum_ref[a]
        pltpu.make_async_copy(held_ref.at[a], grid_ref.at[a], out_sems.at[a]).start()
        out = grid_to_spectrum(s, lambda y: held_ref[a, y], table_ref[...])
        store_spectrum(s, row_ref[0], a, out, keep_ref, send_ref)
        return carry

    lax.fori_loop(0, B, transform, 0)
    for a in range(B):
        pltpu.make_async_copy(held_ref.at[a], grid_ref.at[a], out_sems.at[a]).wait()


def mixed_rows(rows, whi, wlo):
    hi, lo = split(rows)
    width = whi.shape[1]
    if width == 128 and rows.shape[1] == 128:
        left = jnp.concatenate([hi, lo], axis=1)
        right = jnp.concatenate(
            [jnp.concatenate([whi, wlo], axis=1), jnp.concatenate([whi, jnp.zeros_like(wlo)], axis=1)], axis=0
        )
        res = dot(left, right)
        return res[:, :128] + res[:, 128:]
    return dot(hi, whi) + dot(lo, whi) + dot(hi, wlo)


def mix_kernel(s, grid_ref, mix_ref, bias_ref, out_ref):
    whi, wlo = split(mix_ref[...])
    for y in range(s.Yl):
        out_ref[0, y] = mixed_rows(grid_ref[0, y], whi, wlo) + bias_ref[...]


def readout_kernel(s, grid_ref, mix_ref, out_ref):
    whi, wlo = split(mix_ref[...])
    lane = lax.broadcasted_iota(jnp.int32, (B, s.LB), 1)
    for a in range(B):
        total = jnp.zeros((B, s.LB), F32)
        for by in range(s.byn):
            res = mixed_rows(grid_ref[0, by * B + a], whi, wlo)
            for bz in range(s.NB):
                mine = (lane // (s.bxn * s.byn) == bz) & (lane % s.byn == by)
                total = jnp.where(mine, res[bz * B : (bz + 1) * B], total)
        out_ref[0, a * B : (a + 1) * B, :] = total


def x_forward_kernel(s, keep_ref, recv_ref, table_ref, out_ref):
    M = s.M
    for i in range(s.ny):
        parts = []
        for k in range(s.KL):
            kz = i * s.KL + k
            parts.append(
                jnp.concatenate(
                    [
                        ref[0, pl.ds(ri * s.KZ + kz, s.Xl, stride=s.K2), :]
                        for ri in range(2)
                        for ref in (keep_ref, recv_ref)
                    ],
                    axis=0,
                )
            )
        hi, lo = split(jnp.concatenate(parts, axis=1))
        res = dot(table_ref[...], jnp.concatenate([hi, lo], axis=0))
        res = res[: 2 * M] + res[2 * M :]
        rows = []
        for ri in range(2):
            for k in range(s.KL):
                rows.append(res[ri * M : (ri + 1) * M, k * s.LY : (k + 1) * s.LY])
        out_ref[i] = jnp.concatenate(rows, axis=0).T


def y_spectrum(s, in_ref, table, u_ref, v_ref, cs):
    M = s.M
    both = jnp.concatenate([in_ref[pl.ds(c, s.G, stride=s.cp), :] for c in cs], axis=1)
    hi, lo = split(both)
    res = dot(table, jnp.concatenate([hi, lo], axis=0))
    res = res[: 2 * M] + res[2 * M :]
    out = []
    plus = half_signs(M, s.LK, 1.0)
    for i, c in enumerate(cs):
        part = res[:, i * s.LK : (i + 1) * s.LK]
        wave = part[:M] + plus * swap_halves(part[M:])
        out.append(wave * u_ref[c] + swap_halves(wave) * v_ref[c])
    return out


def y_kernel(s, in_ref, fwd_ref, inv_ref, u_ref, v_ref, out_ref):
    minus = half_signs(s.M, s.LK, -1.0)
    for c in range(0, s.cp, 2):
        prods = y_spectrum(s, in_ref, fwd_ref[...], u_ref, v_ref, (c, c + 1))
        both = jnp.concatenate(
            [jnp.concatenate([p, minus * swap_halves(p)], axis=0) for p in prods], axis=1
        )
        hi, lo = split(both)
        res = dot(inv_ref[...], jnp.concatenate([hi, lo, hi], axis=0))
        for i in range(2):
            out_ref[pl.ds(c + i, s.G, stride=s.cp), :] = res[:, i * s.LK : (i + 1) * s.LK]


def y_last_kernel(s, in_ref, fwd_ref, u_ref, v_ref, out_ref):
    total = jnp.zeros((s.M, s.LK), F32)
    for c in range(0, s.cp, 2):
        prods = y_spectrum(s, in_ref, fwd_ref[...], u_ref, v_ref, (c, c + 1))
        total = total + prods[0] + prods[1]
    M = s.M
    for r in range(2 * s.KL):
        part = total[:, r * M : (r + 1) * M]
        out_ref[r : r + 1, :] = jnp.concatenate([part[m : m + 1] for m in range(M)], axis=1)


def x_inverse_kernel(s, in_ref, table_ref, keep_ref, send_ref):
    for i in range(s.ny):
        hi, lo = split(in_ref[i])
        if s.LK == 128:
            res = dot(table_ref[...], jnp.concatenate([hi, lo, hi], axis=1), NT)
        else:
            t = table_ref[...]
            res = dot(t[:, : s.LK], hi, NT) + dot(t[:, : s.LK], lo, NT) + dot(t[:, 2 * s.LK :], hi, NT)
        for k in range(s.KL):
            for ri in range(2):
                at = (k * 2 + ri) * 2 * s.Xl
                places = pl.ds(ri * s.KZ + i * s.KL + k, s.Xl, stride=s.K2)
                keep_ref[places, :] = res[at : at + s.Xl]
                send_ref[places, :] = res[at + s.Xl : at + 2 * s.Xl]


def gelu(x):
    inner = math.sqrt(2.0 / math.pi) * (x + 0.044715 * (x * x * x))
    return 0.5 * x * (1.0 + jnp.tanh(inner))


def layer_kernel(s, row_ref, mixed_ref, inv_ref, fwd_ref, *refs):
    in_refs, (grid_ref, keep_ref, send_ref) = refs[: s.nx], refs[s.nx :]
    row = row_ref[0]
    groups = by_distance(s, row, [[ref[0, b] for b in range(s.bxn)] for ref in in_refs])
    tiles = block_turn([tile for group in groups for tile in group], s.Yl, s.cp)
    for y in range(0, s.Yl, 4):
        hi, lo = split(jnp.concatenate(tiles[y : y + 4], axis=1))
        res = dot(inv_ref[...], jnp.concatenate([hi, lo, hi], axis=0))
        for i in range(4):
            grid_ref[0, y + i] = gelu(mixed_ref[0, y + i] + res[:, i * s.L : (i + 1) * s.L])
    out = grid_to_spectrum(s, lambda y: grid_ref[0, y], fwd_ref[...])
    store_spectrum(s, row, 0, out, keep_ref, send_ref)


def decode_kernel(
    s, id_ref, base_ref, point_ref, spec_ref, turn_ref, mix_ref, hi_ref, lo_ref, inv_ref, out_ref, s_ref, list_ref
):
    modes = jnp.concatenate([spec_ref[i] for i in range(s.ny)], axis=0)
    real_row = lax.broadcasted_iota(jnp.int32, modes.shape, 0) // s.KL % 2 == 0

    def partner(x):
        return jnp.where(real_row, -pltpu.roll(x, s.K2 - s.KL, 0), pltpu.roll(x, s.KL, 0))

    modes = modes * turn_ref[0:1, :] + partner(modes) * turn_ref[1:2, :]
    mhi, mlo = split(jnp.concatenate([modes, partner(modes)], axis=1))
    wave = dot(jnp.concatenate([mhi, mlo], axis=0), hi_ref[...])
    wave = wave[: s.K2] + wave[s.K2 :] + dot(mhi, lo_ref[...])
    hi, lo = split(wave)
    field = dot(inv_ref[...], jnp.concatenate([hi, lo, hi], axis=0))
    width = s.bxn * s.byn
    per = 128 // width
    fields = []
    for q in range(field.shape[1] // 128):
        tiles = [field[z * B : (z + 1) * B, q * 128 : (q + 1) * 128] for z in range(s.NB)]
        for i, tile in enumerate(block_turn(tiles, per, width)):
            at = (q * per + i) * B
            fields.append(tile + mix_ref[at : at + B, :] + base_ref[0])
    out_ref[...] = jnp.zeros(out_ref.shape, F32)
    cell = lax.broadcasted_iota(jnp.int32, (s.LB, 128), 0)

    shi, slo = split(jnp.concatenate(fields, axis=0))
    s_ref[0], s_ref[1] = shi, slo
    slots = point_ref.shape[1]
    step = 4

    live = live_list(lambda n: id_ref[1, n], slots, step, list_ref)

    def per_group(h, carry):
        at = [list_ref[h * step + i] for i in range(step)]
        pick = jnp.concatenate([jnp.where(cell == id_ref[0, q], 1.0, 0.0).astype(BF) for q in at], axis=1)
        if s.LB == 128:
            vals = dot(jnp.concatenate([s_ref[0], s_ref[1]], axis=1), jnp.concatenate([pick, pick], axis=0))
        else:
            vals = dot(s_ref[0], pick) + dot(s_ref[1], pick)
        for i, q in enumerate(at):
            points = [jnp.broadcast_to(point_ref[d, pl.ds(q, 1), :], (8, 128)) for d in range(3)]
            top = jnp.zeros((B, 128), F32)
            low = jnp.zeros((B, 128), F32)
            for n, tile in enumerate(kernel_tiles(points)):
                top = top + tile * vals[n * B : (n + 1) * B, i * 128 : (i + 1) * 128]
                low = low + tile
            top = jnp.sum(top, axis=0, keepdims=True)
            low = jnp.sum(low, axis=0, keepdims=True)
            out_ref[pl.ds(id_ref[2, q], 1), :] = top / jnp.where(low > 0.0, low, 1.0)
        return carry

    lax.fori_loop(0, (live + step - 1) // step, per_group, 0)


def per_device(
    positions,
    point_feat,
    area,
    block_brick,
    block_count,
    sdf,
    grid_gain,
    mix_w,
    mix_b,
    spec_w,
    readout_w,
):
    nx, ny = lax.axis_size("gx"), lax.axis_size("gy")
    row_x, row_y = lax.axis_index("gx"), lax.axis_index("gy")
    modes = math.isqrt(spec_w.shape[4])
    s = Sizes(nx, ny, sdf.shape[2], point_feat.shape[0], modes, spec_w.shape[2] * ny)
    t = {name: jnp.asarray(value) for name, value in make_tables(s).items()}
    shape = lambda *dims: jax.ShapeDtypeStruct(dims, F32)
    blocks = block_brick.shape[0]
    cap = blocks // ny
    PB = positions.shape[1] // blocks
    C, G, M, L = s.C, s.G, s.M, s.L
    large = cap * 5 // 16 * 2
    caps = (large, cap - large)

    *outgoing, slot_of = call(
        functools.partial(pack_kernel, s, caps),
        "pack",
        tuple(shape(ny, part * (C + 3), PB) for part in caps) + (jax.ShapeDtypeStruct((blocks,), jnp.int32),),
        [SM, SM, VM, VM, VM],
        (VM,) * len(caps) + (SM,),
        1e6,
        6e6,
        scratch=[
            pltpu.SMEM((ny + 1,), jnp.int32),
            pltpu.VMEM((ny + 1, cap * C, PB), F32),
            pltpu.VMEM((ny + 1, 3, cap, PB), F32),
        ],
    )(block_brick, block_count, positions, point_feat, area.reshape(blocks, PB))
    early = lax.all_to_all(outgoing[0], "gy", split_axis=0, concat_axis=0, tiled=True)

    def placement(incoming, cap):
        in_pos = incoming[:, cap * C :, :]
        first = in_pos.reshape(ny, 3, cap, PB)[..., 0].transpose(1, 0, 2).reshape(3, ny * cap)
        brick = jnp.floor(first / B).astype(jnp.int32)
        start = jnp.stack([row_x * s.bxn, row_y * s.byn, jnp.zeros_like(row_x)])
        limit = jnp.array([s.bxn - 1, s.byn - 1, s.NB - 1], jnp.int32)
        local = jnp.clip(brick - start[:, None], 0, limit[:, None])
        corner = (local + start[:, None]) * B
        flat = local[2] * (s.bxn * s.byn) + local[0] * s.byn + local[1]
        owned = jnp.where(first[0:1] >= 0.0, local[0:1], -1)
        ids = jnp.concatenate([owned, local[1:], corner, flat[None], flat[None]], axis=0)
        return ids, in_pos

    lane = jnp.arange(L)
    lane_bx = lane // s.cp % s.bxn
    same_bx = lane_bx[:, None] == lane_bx[None, :]
    gain_l = jnp.broadcast_to(grid_gain.reshape(nx, 1, s.cp), (nx, s.bxn, s.cp)).reshape(L)
    spread = (
        (jnp.arange(s.bxn)[:, None, None, None] == lane_bx[None, None, None, :])
        & (jnp.arange(s.Yl)[None, :, None, None] == jnp.arange(s.Yl)[None, None, :, None])
    )
    gains = jnp.where(spread, gain_l, 0.0).reshape(s.bxn * s.Yl, s.Yl * L)
    grid_shape = shape(B, s.Yl, G, L)
    grid_block = pl.BlockSpec((1, s.Yl, G, L), lambda a: (a, 0, 0, 0))
    whole = lambda array: pl.BlockSpec(array.shape, lambda a: (0,) * array.ndim)
    init = call(
        functools.partial(field_kernel, s),
        "field",
        grid_shape,
        [pl.BlockSpec((s.bxn, None, s.Yl, G), lambda a: (0, a, 0, 0)), whole(gains)],
        grid_block,
        3e9,
        1e7,
        grid=(B,),
    )(sdf.reshape(s.bxn, B, s.Yl, G), gains)

    on_lanes = lambda v: jnp.broadcast_to(v.reshape(nx, 1, s.cp), (nx, s.bxn, s.cp)).reshape(1, L)
    mixing = mix_w[0].T.reshape(nx, 1, s.cp, nx, 1, s.cp)
    mixing = jnp.broadcast_to(mixing, (nx, s.bxn, s.cp, nx, s.bxn, s.cp)).reshape(L, L)
    mixing = jnp.where(same_bx, mixing, 0.0)
    bias = on_lanes(mix_b[0])
    read_mix = jnp.sum(readout_w[:, None] * mix_w[1], axis=0)
    base = jnp.sum(readout_w * mix_b[1]).reshape(1)
    out_lane = jnp.arange(s.LB)
    reading = jnp.where(lane_bx[:, None] == out_lane[None, :] // s.byn % s.bxn, on_lanes(read_mix).reshape(L, 1), 0.0)
    mine = lax.dynamic_slice_in_dim(readout_w, row_x * s.cp, s.cp)

    def multipliers(w, scale):
        w = w.reshape(2, s.KL, s.cp, M, M)
        if scale is not None:
            w = w * scale[None, None, :, None, None]
        w = w.transpose(2, 4, 0, 1, 3)
        u = jnp.concatenate([w[:, :, 0:1], w[:, :, 0:1]], axis=2).reshape(s.cp, M, s.LK)
        v = jnp.concatenate([-w[:, :, 1:2], w[:, :, 1:2]], axis=2).reshape(s.cp, M, s.LK)
        return u, v

    u0, v0 = multipliers(spec_w[0], None)
    u1, v1 = multipliers(spec_w[1], mine)

    freq = jnp.asarray(s.freq, jnp.int32)
    turn = jnp.mod(freq[None, :] * (row_x * s.Xl) + freq[:, None] * (row_y * s.Yl), G).reshape(1, -1)
    angle = turn.astype(F32) * (2.0 * math.pi / G)
    turns = jnp.concatenate([jnp.cos(angle), jnp.sin(angle)], axis=0)
    x_fwd = lax.dynamic_index_in_dim(t["x_fwd"], row_x, 0, False)
    x_inv = lax.dynamic_index_in_dim(t["x_inv"], row_x, 0, False)
    row = row_x.astype(jnp.int32).reshape(1)
    prepared = (early, outgoing[1], init, mixing, bias, base, reading, u0, v0, u1, v1, turns, x_fwd, x_inv, row)
    early, second, init, mixing, bias, base, reading, u0, v0, u1, v1, turns, x_fwd, x_inv, row = (
        lax.optimization_barrier(prepared)
    )
    late = lax.all_to_all(second, "gy", split_axis=0, concat_axis=0, tiled=True)
    ids_a, pos_a = placement(early, caps[0])
    ids_b, pos_b = placement(late, caps[1])

    half = s.nx // 2
    spec_shape = shape(half, B, s.bxn, s.K2, s.LY)
    before = call(
        functools.partial(encode_first_kernel, s, caps[0]),
        "encode_first",
        grid_shape,
        [SM, VM, VM],
        VM,
        3e9,
        2e7,
        scratch=[pltpu.SMEM((ny * caps[0] + 8,), jnp.int32)],
    )(ids_a, early, init)
    grid, keep, send = call(
        functools.partial(encode_last_kernel, s, caps[1]),
        "encode_last",
        (grid_shape, spec_shape, spec_shape),
        [SM, SM, VM, pl.BlockSpec(memory_space=pl.ANY), VM],
        (pl.BlockSpec(memory_space=pl.ANY), VM, VM),
        4e9,
        2.2e7,
        scratch=[
            pltpu.SMEM((ny * caps[1] + 8,), jnp.int32),
            pltpu.VMEM(grid_shape.shape, F32),
            pltpu.VMEM(grid_shape.shape, F32),
            pltpu.SemaphoreType.DMA,
            pltpu.SemaphoreType.DMA((B,)),
        ],
    )(row, ids_b, late, before, t["z_fwd"])

    def exchange(array, distance):
        return lax.ppermute(array, "gx", [(i, i ^ distance) for i in range(nx)])

    def to_modes(keep, send, beside=None):
        recv = exchange(send, 1).reshape(half, s.Xl * s.K2, s.LY)
        keep = keep.reshape(half, s.Xl * s.K2, s.LY)

        def part(d):
            block = pl.BlockSpec((1, s.Xl * s.K2, s.LY), lambda i: (d, 0, 0))
            return call(
                functools.partial(x_forward_kernel, s),
                "x_forward",
                shape(ny, s.LY, s.LK),
                [block, block, pl.BlockSpec(x_fwd.shape, lambda i: (0, 0))],
                pl.BlockSpec((ny, s.LY, s.LK), lambda i: (0, 0, 0)),
                2e8,
                3e6,
                grid=(1,),
                room=16,
            )(keep, recv, x_fwd)

        others = [exchange(part(d), 2 * d) for d in range(1, half)]
        spec = part(0)
        if beside is not None:
            beside, *others = lax.optimization_barrier((beside(), *others))
        for other in others:
            spec = spec + other
        spec = lax.all_to_all(spec, "gy", split_axis=0, concat_axis=0, tiled=True)
        return spec.reshape(G * s.cp, s.LK), beside

    spec, unused = to_modes(keep, send)
    mixed = call(
        functools.partial(mix_kernel, s),
        "mix",
        grid_shape,
        [grid_block, whole(mixing), whole(bias)],
        grid_block,
        2e9,
        1.7e7,
        grid=(B,),
    )(grid, mixing, bias)
    spec = call(
        functools.partial(y_kernel, s), "y_both", shape(G * s.cp, s.LK), [VM] * 5, VM, 1e9, 2e6, room=16
    )(spec, t["y_fwd"], t["y_inv"], u0, v0)
    spec = lax.all_to_all(spec.reshape(ny, s.LY, s.LK), "gy", split_axis=0, concat_axis=0, tiled=True)
    near = [exchange(spec, 2 * d) for d in range(1, half)]
    mixed, *near = lax.optimization_barrier((mixed, *near))
    near = [spec] + near
    fields = []
    for item in near:
        own, other = call(
            functools.partial(x_inverse_kernel, s),
            "x_inverse",
            (shape(s.Xl * s.K2, s.LY),) * 2,
            [VM, VM],
            (VM, VM),
            3e8,
            3e6,
            room=16,
        )(item, x_inv)
        fields += [own, exchange(other, 1)]
    fields = [f.reshape(B, s.bxn, s.K2, s.LY) for f in fields]
    field_block = pl.BlockSpec((1, s.bxn, s.K2, s.LY), lambda a: (a, 0, 0, 0))
    spec_block = pl.BlockSpec((half, 1, s.bxn, s.K2, s.LY), lambda a: (0, a, 0, 0, 0))
    grid, keep, send = call(
        functools.partial(layer_kernel, s),
        "layer",
        (grid_shape, spec_shape, spec_shape),
        [SM, grid_block, whole(t["z_inv"]), whole(t["z_fwd"])] + [field_block] * nx,
        (grid_block, spec_block, spec_block),
        4e9,
        2.1e7,
        grid=(B,),
    )(row, mixed, t["z_inv"], t["z_fwd"], *fields)

    def readout():
        return call(
            functools.partial(readout_kernel, s),
            "readout",
            shape(B, B * B, s.LB),
            [grid_block, whole(reading)],
            pl.BlockSpec((1, B * B, s.LB), lambda a: (a, 0, 0)),
            2e9,
            9e6,
            grid=(B,),
        )(grid, reading), decode_places()

    def decode_places():
        points, bricks, live, places = [], [], [], []
        first = 0
        for part, ids, pos in ((caps[0], ids_a, pos_a), (caps[1], ids_b, pos_b)):
            pos = pos.reshape(ny, 3, part, PB).transpose(1, 0, 2, 3).reshape(3, ny * part, PB)
            points.append(pos - ids[3:6].astype(F32)[:, :, None])
            bricks.append(ids[6])
            live.append((ids[0] >= 0).astype(jnp.int32))
            places.append((jnp.arange(ny)[:, None] * cap + first + jnp.arange(part)[None, :]).reshape(-1))
            first += part
        where = [jnp.concatenate(v).astype(jnp.int32) for v in (bricks, live, places)]
        return jnp.concatenate(points, axis=1), jnp.stack(where)

    spec, (read, (points, where)) = to_modes(keep, send, readout)
    last = call(
        functools.partial(y_last_kernel, s), "y_last", shape(2 * s.KL, M * M), [VM] * 4, VM, 1e9, 1e6, room=16
    )(spec, t["y_fwd"], u1, v1)

    last = functools.reduce(jnp.add, [last] + [exchange(last, e) for e in range(1, nx)])
    last = jnp.broadcast_to(last[None], (ny,) + last.shape)
    last = lax.all_to_all(last, "gy", split_axis=0, concat_axis=0, tiled=True)
    values = call(
        functools.partial(decode_kernel, s),
        "decode",
        shape(ny * cap, PB),
        [SM, SM] + [VM] * 7,
        VM,
        4e9,
        6e6,
        scratch=[pltpu.VMEM((2, B * B * B, s.LB), BF), pltpu.SMEM((ny * cap + 8,), jnp.int32)],
        room=32,
    )(where, base, points, last, turns, read.reshape(B * B * B, s.LB), t["xy_hi"], t["xy_lo"], t["z_last"])
    returned = lax.all_to_all(values.reshape(ny, cap, PB), "gy", split_axis=0, concat_axis=0, tiled=True)
    choose = (slot_of[:, None] == jnp.arange(ny * cap, dtype=jnp.int32)[None, :]).astype(F32)
    pressure = jnp.dot(choose, returned.reshape(ny * cap, PB), precision=lax.Precision.HIGHEST)
    return pressure.reshape(blocks * PB)


def solution(mesh):
    placed = (
        P(None, ("gx", "gy")),
        P(None, ("gx", "gy")),
        P(("gx", "gy")),
        P(("gx", "gy")),
        P(("gx", "gy")),
        P("gx", "gy", None),
        P(),
        P(),
        P(),
        P(None, None, "gy", "gx", None),
        P(),
    )
    return jax.shard_map(
        per_device, mesh=mesh, in_specs=placed, out_specs=P(("gx", "gy")), check_vma=False
    )
```

```python
import functools
import math

import jax
import jax.numpy as jnp
import ml_dtypes
import numpy as np
from jax import lax
from jax.experimental import pallas as pl
from jax.experimental.pallas import tpu as pltpu
from jax.sharding import PartitionSpec as P

B = 8
BF = jnp.bfloat16
F32 = jnp.float32
VM = pl.BlockSpec(memory_space=pltpu.VMEM)
SM = pl.BlockSpec(memory_space=pltpu.SMEM)
MIB = 1024 * 1024


def split(x):
    hi = x.astype(BF)
    lo = (x - hi.astype(F32)).astype(BF)
    return hi, lo


def np_split(table):
    table = np.asarray(table, np.float64).astype(np.float32)
    hi = table.astype(ml_dtypes.bfloat16)
    lo = (table - hi.astype(np.float32)).astype(ml_dtypes.bfloat16)
    return hi, lo


def dot(a, b, contract=((1,), (0,))):
    return lax.dot_general(a, b, (contract, ((), ())), preferred_element_type=F32)


NT = ((1,), (1,))


def call(body, name, out_shape, in_specs, out_specs, flops, moved, grid=None, scratch=(), room=58):
    extra = {} if grid is None else {"grid": grid}
    return pl.pallas_call(
        body,
        name=name,
        out_shape=out_shape,
        in_specs=in_specs,
        out_specs=out_specs,
        scratch_shapes=list(scratch),
        compiler_params=pltpu.CompilerParams(vmem_limit_bytes=room * MIB),
        cost_estimate=pl.CostEstimate(flops=int(flops), bytes_accessed=int(moved), transcendentals=0),
        **extra,
    )


class Sizes:
    def __init__(self, nx, ny, grid, channels, modes, kz):
        self.nx, self.ny, self.G, self.C, self.M, self.KZ = nx, ny, grid, channels, modes, kz
        self.NB = grid // B
        self.bxn = self.NB // nx
        self.byn = self.NB // ny
        self.Xl = grid // nx
        self.Yl = grid // ny
        self.cp = channels // nx
        self.KL = kz // ny
        self.L = channels * self.bxn
        self.LY = self.Yl * self.cp
        self.LK = 2 * self.KL * modes
        self.K2 = 2 * kz
        self.LB = self.NB * self.bxn * self.byn
        self.freq = np.where(np.arange(modes) < modes // 2, np.arange(modes), np.arange(modes) - modes)


def trig(s, places, freqs):
    angle = (np.asarray(places)[:, None] * np.asarray(freqs)[None, :]) % s.G * (2.0 * np.pi / s.G)
    return np.cos(angle), np.sin(angle)


def stack_left(table):
    hi, lo = np_split(table)
    zero = np.zeros_like(lo)
    return np.concatenate([np.concatenate([hi, hi], 1), np.concatenate([lo, zero], 1)], 0)


def wide_left(table):
    hi, lo = np_split(table)
    return np.concatenate([hi, hi, lo], 1)


def make_tables(s):
    t = {}
    c, n = trig(s, np.arange(s.KZ), np.arange(s.G))
    t["z_fwd"] = stack_left(np.concatenate([c, -n], 0))
    back = np.where(np.arange(s.KZ) == 0, 1.0, 2.0)[None, :] / s.G
    c, n = trig(s, np.arange(s.G), np.arange(s.KZ))
    c, n = c * back, -n * back
    t["z_inv"] = wide_left(np.concatenate([c, n], 1))
    t["z_last"] = wide_left(np.stack([c.reshape(s.G, s.ny, s.KL), n.reshape(s.G, s.ny, s.KL)], 2).reshape(s.G, -1))
    local = np.arange(s.Xl).reshape(s.bxn, B).T.reshape(-1)
    fwd, inv = [], []
    for row in range(s.nx):
        places = np.concatenate([row * s.Xl + local, (row ^ 1) * s.Xl + local])
        c, n = trig(s, s.freq, places)
        fwd.append(stack_left(np.concatenate([np.concatenate([c, n], 1), np.concatenate([-n, c], 1)], 0)))
        c, n = c.T, n.T
        table = np.zeros((s.KL, 2, 2 * s.Xl, 2, s.KL, s.M))
        for k in range(s.KL):
            table[k, 0, :, 0, k], table[k, 0, :, 1, k] = c, -n
            table[k, 1, :, 0, k], table[k, 1, :, 1, k] = n, c
        inv.append(wide_left(table.reshape(4 * s.KL * s.Xl, s.LK) / s.G))
    t["x_fwd"] = np.stack(fwd)
    t["x_inv"] = np.stack(inv)
    c, n = trig(s, s.freq, np.arange(s.G))
    t["y_fwd"] = stack_left(np.concatenate([c, n], 0))
    t["y_inv"] = wide_left(np.concatenate([c.T, n.T], 1) / s.G)
    xs = (np.arange(s.bxn)[:, None] * B + np.arange(B)[None, :]).T.reshape(B, 1, s.bxn, 1)
    ys = (np.arange(s.byn)[:, None] * B + np.arange(B)[None, :]).T.reshape(1, B, 1, s.byn)
    full = (B, B, s.bxn, s.byn)
    xs, ys = np.broadcast_to(xs, full).reshape(-1), np.broadcast_to(ys, full).reshape(-1)
    turn = s.freq[None, :, None] * xs[None, None, :] + s.freq[:, None, None] * ys[None, None, :]
    angle = (turn % s.G).reshape(s.M * s.M, -1) * (2.0 * np.pi / s.G)
    t["xy_hi"], t["xy_lo"] = np_split(np.concatenate([np.cos(angle), np.sin(angle)], 0) / (s.G * s.G))
    return t


def block_turn(tiles, blocks, width):
    count = len(tiles)
    if count == blocks and count * width == 128:
        lane = lax.broadcasted_iota(jnp.int32, tiles[0].shape, 1) // width
        tiles = list(tiles)
        step = 1
        while step < count:
            upper = (lane & step) != 0
            for i in range(count):
                if i & step == 0:
                    a, b = tiles[i], tiles[i | step]
                    up = pltpu.roll(b, step * width, 1)
                    down = pltpu.roll(a, 128 - step * width, 1)
                    tiles[i] = jnp.where(upper, up, a)
                    tiles[i | step] = jnp.where(upper, b, down)
            step *= 2
        return tiles
    return [
        jnp.concatenate([tile[:, b * width : (b + 1) * width] for tile in tiles], axis=1)
        for b in range(blocks)
    ]


def swap_halves(x):
    half = x.shape[1] // 2
    if x.shape[1] == 128:
        return pltpu.roll(x, half, 1)
    return jnp.concatenate([x[:, half:], x[:, :half]], axis=1)


def half_signs(rows, width, first):
    lane = lax.broadcasted_iota(jnp.int32, (rows, width), 1)
    return jnp.where(lane < width // 2, first, -first).astype(F32)


def pack_kernel(s, caps, brick_ref, count_ref, pos_ref, feat_ref, area_ref, *refs):
    out_refs, (slot_ref, fill_ref, feat_out, pos_out) = refs[: len(caps)], refs[len(caps) :]
    blocks = brick_ref.shape[0]
    C, cap = s.C, sum(caps)
    for i in range(s.ny):
        fill_ref[i] = 0
        pos_out[i] = jnp.full(pos_out.shape[1:], -1.0, F32)
    fill_ref[s.ny] = 0
    live = count_ref[0]

    def place(n, carry):
        alive = n < live
        dest = jnp.where(alive, (brick_ref[n] // s.NB) % s.NB // s.byn, s.ny)
        order = jnp.where(alive, fill_ref[dest], 0)
        fill_ref[dest] = order + 1
        slot_ref[n] = jnp.where(alive, dest * cap + order, -1)
        lanes = pl.ds(pl.multiple_of(n * 128, 128), 128)
        feats = feat_ref[:, lanes] * area_ref[pl.ds(n, 1), :]
        feat_out[dest, pl.ds(pl.multiple_of(order * C, 8), C), :] = feats
        points = pos_ref[:, lanes]
        for d in range(3):
            pos_out[dest, d, pl.ds(order, 1), :] = points[d : d + 1, :]
        return carry

    lax.fori_loop(0, blocks, place, 0, unroll=8)
    early_ref, late_ref = out_refs
    at = caps[0] * C
    for i in range(s.ny):
        early_ref[i, :at] = feat_out[i, :at]
        late_ref[i] = feat_out[i, at:]
        for d in range(3):
            early_ref[i, at + d * cap : at + (d + 1) * cap] = pos_out[i, d]


def field_kernel(s, sdf_ref, gain_ref, out_ref):
    hi, lo = split(sdf_ref[...].reshape(s.bxn * s.Yl, s.G).T)
    ghi, glo = split(gain_ref[...])
    wide = dot(hi, ghi) + dot(lo, ghi) + dot(hi, glo)
    for y in range(s.Yl):
        out_ref[0, y] = wide[:, y * s.L : (y + 1) * s.L]


def kernel_tiles(points):
    px, py, pz = points
    scale = 1.0 / B
    sub = lax.broadcasted_iota(jnp.int32, pz.shape, 0).astype(F32)
    gz = ((sub + 0.5) - pz) * scale
    gz = gz * gz
    gx = []
    gy = []
    for a in range(B):
        d = (px - (a + 0.5)) * scale
        gx.append(1.0 - d * d)
        d = (py - (a + 0.5)) * scale
        gy.append(d * d + gz)
    tiles = []
    for a in range(B):
        for b in range(B):
            t = jnp.maximum(gx[a] - gy[b], 0.0)
            tiles.append(t * t)
    return tiles


def by_distance(s, row, items):
    bit = 1
    while bit < s.nx:
        far = row & bit != 0
        items = [
            [jnp.where(far, b, a) for a, b in zip(items[e], items[e ^ bit])] for e in range(s.nx)
        ]
        bit *= 2
    return items


def store_spectrum(s, row, a, tiles, keep_ref, send_ref):
    groups = by_distance(s, row, [tiles[g * s.bxn : (g + 1) * s.bxn] for g in range(s.nx)])
    for e in range(s.nx):
        for b in range(s.bxn):
            (send_ref if e & 1 else keep_ref)[e // 2, a, b] = groups[e][b]


def grid_to_spectrum(s, rows_of, table):
    tiles = []
    for y in range(0, s.Yl, 4):
        hi, lo = split(jnp.concatenate([rows_of(y + i) for i in range(4)], axis=1))
        res = dot(table, jnp.concatenate([hi, lo], axis=0))
        res = res[: s.K2] + res[s.K2 :]
        tiles += [res[:, i * s.L : (i + 1) * s.L] for i in range(4)]
    return block_turn(tiles, s.nx * s.bxn, s.cp)


def live_list(alive, slots, step, list_ref):
    def collect(n, live):
        list_ref[live] = n
        return live + alive(n)

    live = lax.fori_loop(0, slots, collect, 0, unroll=8)
    for i in range(step):
        list_ref[live + i] = 0
    return live


def add_blocks(s, caps, turn, id_ref, in_ref, pos_ref, at, grid_ref, list_ref):
    C = s.C
    cap = sum(caps)
    step = 4
    group = lax.broadcasted_iota(jnp.int32, (s.L, 128), 0) // s.cp % s.bxn
    live = live_list(lambda n: jnp.where(id_ref[7, n] == turn, 1, 0), s.ny * cap, step, list_ref)

    def per_group(h, carry):
        results = []
        slots = [list_ref[h * step + i] for i in range(step)]
        for i, slot in enumerate(slots):
            src, j = slot // cap, slot % cap
            points = [
                jnp.broadcast_to(pos_ref[src, pl.ds(at + d * cap + j, 1), :], (8, 128))
                - id_ref[3 + d, slot].astype(F32)
                for d in range(3)
            ]
            weights = jnp.concatenate(kernel_tiles(points), axis=0)
            place = jnp.clip(j - turn * caps[0], 0, caps[turn] - 1)
            feats = in_ref[src, pl.ds(pl.multiple_of(place * C, 8), C), :]
            spread = []
            for g in range(s.nx):
                spread += [feats[g * s.cp : (g + 1) * s.cp]] * s.bxn
            mine = jnp.where(h * step + i < live, id_ref[0, slot], -1)
            spread = jnp.where(group == mine, jnp.concatenate(spread, axis=0), 0.0)
            whi, wlo = split(weights)
            fhi, flo = split(spread)
            left = jnp.concatenate([whi, wlo], axis=1)
            right = jnp.concatenate([fhi, fhi], axis=1)
            if s.L == 128:
                under = jnp.concatenate([flo, jnp.zeros_like(flo)], axis=1)
                res = dot(left, jnp.concatenate([right, under], axis=0), NT)
                res = res[:, : s.L] + res[:, s.L :]
            else:
                res = dot(left, right, NT) + dot(whi, flo, NT)
            results.append(res.reshape(B, B, B, s.L))
        for slot, res in zip(slots, results):
            ys = pl.ds(pl.multiple_of(id_ref[1, slot] * B, B), B)
            zs = pl.ds(pl.multiple_of(id_ref[2, slot] * B, B), B)
            grid_ref[:, ys, zs, :] = grid_ref[:, ys, zs, :] + res
        return carry

    lax.fori_loop(0, (live + step - 1) // step, per_group, 0)


def encode_first_kernel(s, caps, id_ref, in_ref, init_ref, grid_ref, list_ref):
    for a in range(B):
        grid_ref[a] = init_ref[a]
    add_blocks(s, caps, 0, id_ref, in_ref, in_ref, caps[0] * s.C, grid_ref, list_ref)


def encode_last_kernel(
    s, caps, row_ref, id_ref, in_ref, pos_ref, before_ref, table_ref, grid_ref, keep_ref, send_ref,
    list_ref, sum_ref, held_ref, in_sem, out_sems
):
    fetch = pltpu.make_async_copy(before_ref, held_ref, in_sem)
    fetch.start()
    for a in range(B):
        sum_ref[a] = jnp.zeros(sum_ref.shape[1:], F32)
    add_blocks(s, caps, 1, id_ref, in_ref, pos_ref, 0, sum_ref, list_ref)
    fetch.wait()

    def transform(a, carry):
        held_ref[a] = held_ref[a] + sum_ref[a]
        pltpu.make_async_copy(held_ref.at[a], grid_ref.at[a], out_sems.at[a]).start()
        out = grid_to_spectrum(s, lambda y: held_ref[a, y], table_ref[...])
        store_spectrum(s, row_ref[0], a, out, keep_ref, send_ref)
        return carry

    lax.fori_loop(0, B, transform, 0)
    for a in range(B):
        pltpu.make_async_copy(held_ref.at[a], grid_ref.at[a], out_sems.at[a]).wait()


def mixed_rows(rows, whi, wlo):
    hi, lo = split(rows)
    width = whi.shape[1]
    if width == 128 and rows.shape[1] == 128:
        left = jnp.concatenate([hi, lo], axis=1)
        right = jnp.concatenate(
            [jnp.concatenate([whi, wlo], axis=1), jnp.concatenate([whi, jnp.zeros_like(wlo)], axis=1)], axis=0
        )
        res = dot(left, right)
        return res[:, :128] + res[:, 128:]
    return dot(hi, whi) + dot(lo, whi) + dot(hi, wlo)


def mix_kernel(s, grid_ref, mix_ref, bias_ref, out_ref):
    whi, wlo = split(mix_ref[...])
    for y in range(s.Yl):
        out_ref[0, y] = mixed_rows(grid_ref[0, y], whi, wlo) + bias_ref[...]


def readout_kernel(s, grid_ref, mix_ref, out_ref):
    whi, wlo = split(mix_ref[...])
    lane = lax.broadcasted_iota(jnp.int32, (B, s.LB), 1)
    for a in range(B):
        total = jnp.zeros((B, s.LB), F32)
        for by in range(s.byn):
            res = mixed_rows(grid_ref[0, by * B + a], whi, wlo)
            for bz in range(s.NB):
                mine = (lane // (s.bxn * s.byn) == bz) & (lane % s.byn == by)
                total = jnp.where(mine, res[bz * B : (bz + 1) * B], total)
        out_ref[0, a * B : (a + 1) * B, :] = total


def x_forward_kernel(s, keep_ref, recv_ref, table_ref, out_ref):
    M = s.M
    for i in range(s.ny):
        parts = []
        for k in range(s.KL):
            kz = i * s.KL + k
            parts.append(
                jnp.concatenate(
                    [
                        ref[0, pl.ds(ri * s.KZ + kz, s.Xl, stride=s.K2), :]
                        for ri in range(2)
                        for ref in (keep_ref, recv_ref)
                    ],
                    axis=0,
                )
            )
        hi, lo = split(jnp.concatenate(parts, axis=1))
        res = dot(table_ref[...], jnp.concatenate([hi, lo], axis=0))
        res = res[: 2 * M] + res[2 * M :]
        rows = []
        for ri in range(2):
            for k in range(s.KL):
                rows.append(res[ri * M : (ri + 1) * M, k * s.LY : (k + 1) * s.LY])
        out_ref[i] = jnp.concatenate(rows, axis=0).T


def y_spectrum(s, in_ref, table, u_ref, v_ref, cs):
    M = s.M
    both = jnp.concatenate([in_ref[pl.ds(c, s.G, stride=s.cp), :] for c in cs], axis=1)
    hi, lo = split(both)
    res = dot(table, jnp.concatenate([hi, lo], axis=0))
    res = res[: 2 * M] + res[2 * M :]
    out = []
    plus = half_signs(M, s.LK, 1.0)
    for i, c in enumerate(cs):
        part = res[:, i * s.LK : (i + 1) * s.LK]
        wave = part[:M] + plus * swap_halves(part[M:])
        out.append(wave * u_ref[c] + swap_halves(wave) * v_ref[c])
    return out


def y_kernel(s, in_ref, fwd_ref, inv_ref, u_ref, v_ref, out_ref):
    minus = half_signs(s.M, s.LK, -1.0)
    for c in range(0, s.cp, 2):
        prods = y_spectrum(s, in_ref, fwd_ref[...], u_ref, v_ref, (c, c + 1))
        both = jnp.concatenate(
            [jnp.concatenate([p, minus * swap_halves(p)], axis=0) for p in prods], axis=1
        )
        hi, lo = split(both)
        res = dot(inv_ref[...], jnp.concatenate([hi, lo, hi], axis=0))
        for i in range(2):
            out_ref[pl.ds(c + i, s.G, stride=s.cp), :] = res[:, i * s.LK : (i + 1) * s.LK]


def y_last_kernel(s, in_ref, fwd_ref, u_ref, v_ref, out_ref):
    total = jnp.zeros((s.M, s.LK), F32)
    for c in range(0, s.cp, 2):
        prods = y_spectrum(s, in_ref, fwd_ref[...], u_ref, v_ref, (c, c + 1))
        total = total + prods[0] + prods[1]
    M = s.M
    for r in range(2 * s.KL):
        part = total[:, r * M : (r + 1) * M]
        out_ref[r : r + 1, :] = jnp.concatenate([part[m : m + 1] for m in range(M)], axis=1)


def x_inverse_kernel(s, in_ref, table_ref, keep_ref, send_ref):
    for i in range(s.ny):
        hi, lo = split(in_ref[i])
        if s.LK == 128:
            res = dot(table_ref[...], jnp.concatenate([hi, lo, hi], axis=1), NT)
        else:
            t = table_ref[...]
            res = dot(t[:, : s.LK], hi, NT) + dot(t[:, : s.LK], lo, NT) + dot(t[:, 2 * s.LK :], hi, NT)
        for k in range(s.KL):
            for ri in range(2):
                at = (k * 2 + ri) * 2 * s.Xl
                places = pl.ds(ri * s.KZ + i * s.KL + k, s.Xl, stride=s.K2)
                keep_ref[places, :] = res[at : at + s.Xl]
                send_ref[places, :] = res[at + s.Xl : at + 2 * s.Xl]


def gelu(x):
    inner = math.sqrt(2.0 / math.pi) * (x + 0.044715 * (x * x * x))
    return 0.5 * x * (1.0 + jnp.tanh(inner))


def layer_kernel(s, row_ref, mixed_ref, inv_ref, fwd_ref, *refs):
    in_refs, (grid_ref, keep_ref, send_ref) = refs[: s.nx], refs[s.nx :]
    row = row_ref[0]
    groups = by_distance(s, row, [[ref[0, b] for b in range(s.bxn)] for ref in in_refs])
    tiles = block_turn([tile for group in groups for tile in group], s.Yl, s.cp)
    for y in range(0, s.Yl, 4):
        hi, lo = split(jnp.concatenate(tiles[y : y + 4], axis=1))
        res = dot(inv_ref[...], jnp.concatenate([hi, lo, hi], axis=0))
        for i in range(4):
            grid_ref[0, y + i] = gelu(mixed_ref[0, y + i] + res[:, i * s.L : (i + 1) * s.L])
    out = grid_to_spectrum(s, lambda y: grid_ref[0, y], fwd_ref[...])
    store_spectrum(s, row, 0, out, keep_ref, send_ref)


def decode_kernel(
    s, id_ref, base_ref, point_ref, spec_ref, turn_ref, mix_ref, hi_ref, lo_ref, inv_ref, out_ref, s_ref, list_ref
):
    modes = jnp.concatenate([spec_ref[i] for i in range(s.ny)], axis=0)
    real_row = lax.broadcasted_iota(jnp.int32, modes.shape, 0) // s.KL % 2 == 0

    def partner(x):
        return jnp.where(real_row, -pltpu.roll(x, s.K2 - s.KL, 0), pltpu.roll(x, s.KL, 0))

    modes = modes * turn_ref[0:1, :] + partner(modes) * turn_ref[1:2, :]
    mhi, mlo = split(jnp.concatenate([modes, partner(modes)], axis=1))
    wave = dot(jnp.concatenate([mhi, mlo], axis=0), hi_ref[...])
    wave = wave[: s.K2] + wave[s.K2 :] + dot(mhi, lo_ref[...])
    hi, lo = split(wave)
    field = dot(inv_ref[...], jnp.concatenate([hi, lo, hi], axis=0))
    width = s.bxn * s.byn
    per = 128 // width
    fields = []
    for q in range(field.shape[1] // 128):
        tiles = [field[z * B : (z + 1) * B, q * 128 : (q + 1) * 128] for z in range(s.NB)]
        for i, tile in enumerate(block_turn(tiles, per, width)):
            at = (q * per + i) * B
            fields.append(tile + mix_ref[at : at + B, :] + base_ref[0])
    out_ref[...] = jnp.zeros(out_ref.shape, F32)
    cell = lax.broadcasted_iota(jnp.int32, (s.LB, 128), 0)

    shi, slo = split(jnp.concatenate(fields, axis=0))
    s_ref[0], s_ref[1] = shi, slo
    slots = point_ref.shape[1]
    step = 8

    live = live_list(lambda n: id_ref[1, n], slots, step, list_ref)

    def per_group(h, carry):
        at = [list_ref[h * step + i] for i in range(step)]
        pick = jnp.concatenate([jnp.where(cell == id_ref[0, q], 1.0, 0.0).astype(BF) for q in at], axis=1)
        if s.LB == 128:
            vals = dot(jnp.concatenate([s_ref[0], s_ref[1]], axis=1), jnp.concatenate([pick, pick], axis=0))
        else:
            vals = dot(s_ref[0], pick) + dot(s_ref[1], pick)
        for i, q in enumerate(at):
            points = [jnp.broadcast_to(point_ref[d, pl.ds(q, 1), :], (8, 128)) for d in range(3)]
            top = jnp.zeros((B, 128), F32)
            low = jnp.zeros((B, 128), F32)
            for n, tile in enumerate(kernel_tiles(points)):
                top = top + tile * vals[n * B : (n + 1) * B, i * 128 : (i + 1) * 128]
                low = low + tile
            top = jnp.sum(top, axis=0, keepdims=True)
            low = jnp.sum(low, axis=0, keepdims=True)
            out_ref[pl.ds(id_ref[2, q], 1), :] = top / jnp.where(low > 0.0, low, 1.0)
        return carry

    lax.fori_loop(0, (live + step - 1) // step, per_group, 0)


def per_device(
    positions,
    point_feat,
    area,
    block_brick,
    block_count,
    sdf,
    grid_gain,
    mix_w,
    mix_b,
    spec_w,
    readout_w,
):
    nx, ny = lax.axis_size("gx"), lax.axis_size("gy")
    row_x, row_y = lax.axis_index("gx"), lax.axis_index("gy")
    modes = math.isqrt(spec_w.shape[4])
    s = Sizes(nx, ny, sdf.shape[2], point_feat.shape[0], modes, spec_w.shape[2] * ny)
    t = {name: jnp.asarray(value) for name, value in make_tables(s).items()}
    shape = lambda *dims: jax.ShapeDtypeStruct(dims, F32)
    blocks = block_brick.shape[0]
    cap = blocks // ny
    PB = positions.shape[1] // blocks
    C, G, M, L = s.C, s.G, s.M, s.L
    large = cap * 5 // 16 * 2
    caps = (large, cap - large)

    *outgoing, slot_of = call(
        functools.partial(pack_kernel, s, caps),
        "pack",
        (
            shape(ny, caps[0] * C + 3 * cap, PB),
            shape(ny, caps[1] * C, PB),
            jax.ShapeDtypeStruct((blocks,), jnp.int32),
        ),
        [SM, SM, VM, VM, VM],
        (VM, VM, SM),
        1e6,
        6e6,
        scratch=[
            pltpu.SMEM((ny + 1,), jnp.int32),
            pltpu.VMEM((ny + 1, cap * C, PB), F32),
            pltpu.VMEM((ny + 1, 3, cap, PB), F32),
        ],
    )(block_brick, block_count, positions, point_feat, area.reshape(blocks, PB))
    early = lax.all_to_all(outgoing[0], "gy", split_axis=0, concat_axis=0, tiled=True)

    def placement(incoming):
        in_pos = incoming[:, caps[0] * C :, :]
        first = in_pos.reshape(ny, 3, cap, PB)[..., 0].transpose(1, 0, 2).reshape(3, ny * cap)
        brick = jnp.floor(first / B).astype(jnp.int32)
        start = jnp.stack([row_x * s.bxn, row_y * s.byn, jnp.zeros_like(row_x)])
        limit = jnp.array([s.bxn - 1, s.byn - 1, s.NB - 1], jnp.int32)
        local = jnp.clip(brick - start[:, None], 0, limit[:, None])
        corner = (local + start[:, None]) * B
        flat = local[2] * (s.bxn * s.byn) + local[0] * s.byn + local[1]
        owned = jnp.where(first[0:1] >= 0.0, local[0:1], -1)
        turn = jnp.where(jnp.arange(ny * cap) % cap < caps[0], 0, 1).astype(jnp.int32)
        turn = jnp.where(first[0] >= 0.0, turn, -1)
        ids = jnp.concatenate([owned, local[1:], corner, flat[None], turn[None]], axis=0)
        return ids, in_pos

    lane = jnp.arange(L)
    lane_bx = lane // s.cp % s.bxn
    same_bx = lane_bx[:, None] == lane_bx[None, :]
    gain_l = jnp.broadcast_to(grid_gain.reshape(nx, 1, s.cp), (nx, s.bxn, s.cp)).reshape(L)
    spread = (
        (jnp.arange(s.bxn)[:, None, None, None] == lane_bx[None, None, None, :])
        & (jnp.arange(s.Yl)[None, :, None, None] == jnp.arange(s.Yl)[None, None, :, None])
    )
    gains = jnp.where(spread, gain_l, 0.0).reshape(s.bxn * s.Yl, s.Yl * L)
    grid_shape = shape(B, s.Yl, G, L)
    grid_block = pl.BlockSpec((1, s.Yl, G, L), lambda a: (a, 0, 0, 0))
    whole = lambda array: pl.BlockSpec(array.shape, lambda a: (0,) * array.ndim)
    init = call(
        functools.partial(field_kernel, s),
        "field",
        grid_shape,
        [pl.BlockSpec((s.bxn, None, s.Yl, G), lambda a: (0, a, 0, 0)), whole(gains)],
        grid_block,
        3e9,
        1e7,
        grid=(B,),
    )(sdf.reshape(s.bxn, B, s.Yl, G), gains)

    on_lanes = lambda v: jnp.broadcast_to(v.reshape(nx, 1, s.cp), (nx, s.bxn, s.cp)).reshape(1, L)
    mixing = mix_w[0].T.reshape(nx, 1, s.cp, nx, 1, s.cp)
    mixing = jnp.broadcast_to(mixing, (nx, s.bxn, s.cp, nx, s.bxn, s.cp)).reshape(L, L)
    mixing = jnp.where(same_bx, mixing, 0.0)
    bias = on_lanes(mix_b[0])
    read_mix = jnp.sum(readout_w[:, None] * mix_w[1], axis=0)
    base = jnp.sum(readout_w * mix_b[1]).reshape(1)
    out_lane = jnp.arange(s.LB)
    reading = jnp.where(lane_bx[:, None] == out_lane[None, :] // s.byn % s.bxn, on_lanes(read_mix).reshape(L, 1), 0.0)
    mine = lax.dynamic_slice_in_dim(readout_w, row_x * s.cp, s.cp)

    def multipliers(w, scale):
        w = w.reshape(2, s.KL, s.cp, M, M)
        if scale is not None:
            w = w * scale[None, None, :, None, None]
        w = w.transpose(2, 4, 0, 1, 3)
        u = jnp.concatenate([w[:, :, 0:1], w[:, :, 0:1]], axis=2).reshape(s.cp, M, s.LK)
        v = jnp.concatenate([-w[:, :, 1:2], w[:, :, 1:2]], axis=2).reshape(s.cp, M, s.LK)
        return u, v

    u0, v0 = multipliers(spec_w[0], None)
    u1, v1 = multipliers(spec_w[1], mine)

    freq = jnp.asarray(s.freq, jnp.int32)
    turn = jnp.mod(freq[None, :] * (row_x * s.Xl) + freq[:, None] * (row_y * s.Yl), G).reshape(1, -1)
    angle = turn.astype(F32) * (2.0 * math.pi / G)
    turns = jnp.concatenate([jnp.cos(angle), jnp.sin(angle)], axis=0)
    x_fwd = lax.dynamic_index_in_dim(t["x_fwd"], row_x, 0, False)
    x_inv = lax.dynamic_index_in_dim(t["x_inv"], row_x, 0, False)
    row = row_x.astype(jnp.int32).reshape(1)
    prepared = (early, outgoing[1], init, mixing, bias, base, reading, u0, v0, u1, v1, turns, x_fwd, x_inv, row)
    early, second, init, mixing, bias, base, reading, u0, v0, u1, v1, turns, x_fwd, x_inv, row = (
        lax.optimization_barrier(prepared)
    )
    late = lax.all_to_all(second, "gy", split_axis=0, concat_axis=0, tiled=True)
    ids, in_pos = placement(early)

    half = s.nx // 2
    spec_shape = shape(half, B, s.bxn, s.K2, s.LY)
    before = call(
        functools.partial(encode_first_kernel, s, caps),
        "encode_first",
        grid_shape,
        [SM, VM, VM],
        VM,
        3e9,
        2e7,
        scratch=[pltpu.SMEM((ny * cap + 8,), jnp.int32)],
    )(ids, early, init)
    grid, keep, send = call(
        functools.partial(encode_last_kernel, s, caps),
        "encode_last",
        (grid_shape, spec_shape, spec_shape),
        [SM, SM, VM, VM, pl.BlockSpec(memory_space=pl.ANY), VM],
        (pl.BlockSpec(memory_space=pl.ANY), VM, VM),
        4e9,
        2.2e7,
        scratch=[
            pltpu.SMEM((ny * cap + 8,), jnp.int32),
            pltpu.VMEM(grid_shape.shape, F32),
            pltpu.VMEM(grid_shape.shape, F32),
            pltpu.SemaphoreType.DMA,
            pltpu.SemaphoreType.DMA((B,)),
        ],
    )(row, ids, late, in_pos, before, t["z_fwd"])

    def exchange(array, distance):
        return lax.ppermute(array, "gx", [(i, i ^ distance) for i in range(nx)])

    def to_modes(keep, send, beside=None):
        recv = exchange(send, 1).reshape(half, s.Xl * s.K2, s.LY)
        keep = keep.reshape(half, s.Xl * s.K2, s.LY)

        def part(d):
            block = pl.BlockSpec((1, s.Xl * s.K2, s.LY), lambda i: (d, 0, 0))
            return call(
                functools.partial(x_forward_kernel, s),
                "x_forward",
                shape(ny, s.LY, s.LK),
                [block, block, pl.BlockSpec(x_fwd.shape, lambda i: (0, 0))],
                pl.BlockSpec((ny, s.LY, s.LK), lambda i: (0, 0, 0)),
                2e8,
                3e6,
                grid=(1,),
                room=16,
            )(keep, recv, x_fwd)

        others = [exchange(part(d), 2 * d) for d in range(1, half)]
        spec = part(0)
        if beside is not None:
            beside, *others = lax.optimization_barrier((beside(), *others))
        for other in others:
            spec = spec + other
        spec = lax.all_to_all(spec, "gy", split_axis=0, concat_axis=0, tiled=True)
        return spec.reshape(G * s.cp, s.LK), beside

    spec, unused = to_modes(keep, send)
    mixed = call(
        functools.partial(mix_kernel, s),
        "mix",
        grid_shape,
        [grid_block, whole(mixing), whole(bias)],
        grid_block,
        2e9,
        1.7e7,
        grid=(B,),
    )(grid, mixing, bias)
    spec = call(
        functools.partial(y_kernel, s), "y_both", shape(G * s.cp, s.LK), [VM] * 5, VM, 1e9, 2e6, room=16
    )(spec, t["y_fwd"], t["y_inv"], u0, v0)
    spec = lax.all_to_all(spec.reshape(ny, s.LY, s.LK), "gy", split_axis=0, concat_axis=0, tiled=True)
    near = [exchange(spec, 2 * d) for d in range(1, half)]
    mixed, *near = lax.optimization_barrier((mixed, *near))
    near = [spec] + near
    fields = []
    for item in near:
        own, other = call(
            functools.partial(x_inverse_kernel, s),
            "x_inverse",
            (shape(s.Xl * s.K2, s.LY),) * 2,
            [VM, VM],
            (VM, VM),
            3e8,
            3e6,
            room=16,
        )(item, x_inv)
        fields += [own, exchange(other, 1)]
    fields = [f.reshape(B, s.bxn, s.K2, s.LY) for f in fields]
    field_block = pl.BlockSpec((1, s.bxn, s.K2, s.LY), lambda a: (a, 0, 0, 0))
    spec_block = pl.BlockSpec((half, 1, s.bxn, s.K2, s.LY), lambda a: (0, a, 0, 0, 0))
    grid, keep, send = call(
        functools.partial(layer_kernel, s),
        "layer",
        (grid_shape, spec_shape, spec_shape),
        [SM, grid_block, whole(t["z_inv"]), whole(t["z_fwd"])] + [field_block] * nx,
        (grid_block, spec_block, spec_block),
        4e9,
        2.1e7,
        grid=(B,),
        room=63,
    )(row, mixed, t["z_inv"], t["z_fwd"], *fields)

    def readout():
        return call(
            functools.partial(readout_kernel, s),
            "readout",
            shape(B, B * B, s.LB),
            [grid_block, whole(reading)],
            pl.BlockSpec((1, B * B, s.LB), lambda a: (a, 0, 0)),
            2e9,
            9e6,
            grid=(B,),
        )(grid, reading), decode_places()

    def decode_places():
        points = in_pos.reshape(ny, 3, cap, PB).transpose(1, 0, 2, 3).reshape(3, ny * cap, PB)
        live = (ids[7] >= 0).astype(jnp.int32)
        where = jnp.stack([ids[6], live, jnp.arange(ny * cap, dtype=jnp.int32)])
        return points - ids[3:6].astype(F32)[:, :, None], where

    spec, (read, (points, where)) = to_modes(keep, send, readout)
    last = call(
        functools.partial(y_last_kernel, s), "y_last", shape(2 * s.KL, M * M), [VM] * 4, VM, 1e9, 1e6, room=16
    )(spec, t["y_fwd"], u1, v1)

    last = functools.reduce(jnp.add, [last] + [exchange(last, e) for e in range(1, nx)])
    last = jnp.broadcast_to(last[None], (ny,) + last.shape)
    last = lax.all_to_all(last, "gy", split_axis=0, concat_axis=0, tiled=True)
    values = call(
        functools.partial(decode_kernel, s),
        "decode",
        shape(ny * cap, PB),
        [SM, SM] + [VM] * 7,
        VM,
        4e9,
        6e6,
        scratch=[pltpu.VMEM((2, B * B * B, s.LB), BF), pltpu.SMEM((ny * cap + 8,), jnp.int32)],
        room=32,
    )(where, base, points, last, turns, read.reshape(B * B * B, s.LB), t["xy_hi"], t["xy_lo"], t["z_last"])
    returned = lax.all_to_all(values.reshape(ny, cap, PB), "gy", split_axis=0, concat_axis=0, tiled=True)
    choose = (slot_of[:, None] == jnp.arange(ny * cap, dtype=jnp.int32)[None, :]).astype(F32)
    pressure = jnp.dot(choose, returned.reshape(ny * cap, PB), precision=lax.Precision.HIGHEST)
    return pressure.reshape(blocks * PB)


def solution(mesh):
    placed = (
        P(None, ("gx", "gy")),
        P(None, ("gx", "gy")),
        P(("gx", "gy")),
        P(("gx", "gy")),
        P(("gx", "gy")),
        P("gx", "gy", None),
        P(),
        P(),
        P(),
        P(None, None, "gy", "gx", None),
        P(),
    )
    return jax.shard_map(
        per_device, mesh=mesh, in_specs=placed, out_specs=P(("gx", "gy")), check_vma=False
    )
```

```python
import functools
import math

import jax
import jax.numpy as jnp
import ml_dtypes
import numpy as np
from jax import lax
from jax.experimental import pallas as pl
from jax.experimental.pallas import tpu as pltpu
from jax.sharding import PartitionSpec as P

B = 8
BF = jnp.bfloat16
F32 = jnp.float32
VM = pl.BlockSpec(memory_space=pltpu.VMEM)
SM = pl.BlockSpec(memory_space=pltpu.SMEM)
ANY = pl.BlockSpec(memory_space=pl.ANY)
MIB = 1024 * 1024


def split(x):
    hi = x.astype(BF)
    lo = (x - hi.astype(F32)).astype(BF)
    return hi, lo


def np_split(table):
    table = np.asarray(table, np.float64).astype(np.float32)
    hi = table.astype(ml_dtypes.bfloat16)
    lo = (table - hi.astype(np.float32)).astype(ml_dtypes.bfloat16)
    return hi, lo


def dot(a, b, contract=((1,), (0,))):
    return lax.dot_general(a, b, (contract, ((), ())), preferred_element_type=F32)


NT = ((1,), (1,))


def call(body, name, out_shape, in_specs, out_specs, flops, moved, grid=None, scratch=(), room=58):
    extra = {} if grid is None else {"grid": grid}
    return pl.pallas_call(
        body,
        name=name,
        out_shape=out_shape,
        in_specs=in_specs,
        out_specs=out_specs,
        scratch_shapes=list(scratch),
        compiler_params=pltpu.CompilerParams(vmem_limit_bytes=room * MIB),
        cost_estimate=pl.CostEstimate(flops=int(flops), bytes_accessed=int(moved), transcendentals=0),
        **extra,
    )


class Sizes:
    def __init__(self, nx, ny, grid, channels, modes, kz):
        self.nx, self.ny, self.G, self.C, self.M, self.KZ = nx, ny, grid, channels, modes, kz
        self.NB = grid // B
        self.bxn = self.NB // nx
        self.byn = self.NB // ny
        self.Xl = grid // nx
        self.Yl = grid // ny
        self.cp = channels // nx
        self.KL = kz // ny
        self.L = channels * self.bxn
        self.LY = self.Yl * self.cp
        self.LK = 2 * self.KL * modes
        self.K2 = 2 * kz
        self.LB = self.NB * self.bxn * self.byn
        self.freq = np.where(np.arange(modes) < modes // 2, np.arange(modes), np.arange(modes) - modes)


def trig(s, places, freqs):
    angle = (np.asarray(places)[:, None] * np.asarray(freqs)[None, :]) % s.G * (2.0 * np.pi / s.G)
    return np.cos(angle), np.sin(angle)


def stack_left(table):
    hi, lo = np_split(table)
    zero = np.zeros_like(lo)
    return np.concatenate([np.concatenate([hi, hi], 1), np.concatenate([lo, zero], 1)], 0)


def wide_left(table):
    hi, lo = np_split(table)
    return np.concatenate([hi, hi, lo], 1)


def make_tables(s):
    t = {}
    c, n = trig(s, np.arange(s.KZ), np.arange(s.G))
    t["z_fwd"] = stack_left(np.concatenate([c, -n], 0))
    back = np.where(np.arange(s.KZ) == 0, 1.0, 2.0)[None, :] / s.G
    c, n = trig(s, np.arange(s.G), np.arange(s.KZ))
    c, n = c * back, -n * back
    t["z_inv"] = wide_left(np.concatenate([c, n], 1))
    t["z_last"] = wide_left(np.stack([c.reshape(s.G, s.ny, s.KL), n.reshape(s.G, s.ny, s.KL)], 2).reshape(s.G, -1))
    local = np.arange(s.Xl).reshape(s.bxn, B).T.reshape(-1)
    fwd, inv = [], []
    for row in range(s.nx):
        places = np.concatenate([row * s.Xl + local, (row ^ 1) * s.Xl + local])
        c, n = trig(s, s.freq, places)
        fwd.append(stack_left(np.concatenate([np.concatenate([c, n], 1), np.concatenate([-n, c], 1)], 0)))
        c, n = c.T, n.T
        table = np.zeros((s.KL, 2, 2 * s.Xl, 2, s.KL, s.M))
        for k in range(s.KL):
            table[k, 0, :, 0, k], table[k, 0, :, 1, k] = c, -n
            table[k, 1, :, 0, k], table[k, 1, :, 1, k] = n, c
        inv.append(wide_left(table.reshape(4 * s.KL * s.Xl, s.LK) / s.G))
    t["x_fwd"] = np.stack(fwd)
    t["x_inv"] = np.stack(inv)
    c, n = trig(s, s.freq, np.arange(s.G))
    t["y_fwd"] = stack_left(np.concatenate([c, n], 0))
    t["y_inv"] = wide_left(np.concatenate([c.T, n.T], 1) / s.G)
    xs = (np.arange(s.bxn)[:, None] * B + np.arange(B)[None, :]).T.reshape(B, 1, s.bxn, 1)
    ys = (np.arange(s.byn)[:, None] * B + np.arange(B)[None, :]).T.reshape(1, B, 1, s.byn)
    full = (B, B, s.bxn, s.byn)
    xs, ys = np.broadcast_to(xs, full).reshape(-1), np.broadcast_to(ys, full).reshape(-1)
    turn = s.freq[None, :, None] * xs[None, None, :] + s.freq[:, None, None] * ys[None, None, :]
    angle = (turn % s.G).reshape(s.M * s.M, -1) * (2.0 * np.pi / s.G)
    t["xy_hi"], t["xy_lo"] = np_split(np.concatenate([np.cos(angle), np.sin(angle)], 0) / (s.G * s.G))
    return t


def block_turn(tiles, blocks, width):
    count = len(tiles)
    if count == blocks and count * width == 128:
        lane = lax.broadcasted_iota(jnp.int32, tiles[0].shape, 1) // width
        tiles = list(tiles)
        step = 1
        while step < count:
            upper = (lane & step) != 0
            for i in range(count):
                if i & step == 0:
                    a, b = tiles[i], tiles[i | step]
                    up = pltpu.roll(b, step * width, 1)
                    down = pltpu.roll(a, 128 - step * width, 1)
                    tiles[i] = jnp.where(upper, up, a)
                    tiles[i | step] = jnp.where(upper, b, down)
            step *= 2
        return tiles
    return [
        jnp.concatenate([tile[:, b * width : (b + 1) * width] for tile in tiles], axis=1)
        for b in range(blocks)
    ]


def swap_halves(x):
    half = x.shape[1] // 2
    if x.shape[1] == 128:
        return pltpu.roll(x, half, 1)
    return jnp.concatenate([x[:, half:], x[:, :half]], axis=1)


def half_signs(rows, width, first):
    lane = lax.broadcasted_iota(jnp.int32, (rows, width), 1)
    return jnp.where(lane < width // 2, first, -first).astype(F32)


def pack_kernel(
    s, caps, brick_ref, count_ref, pos_ref, feat_hbm, area_ref, early_ref, late_ref, slot_ref,
    fill_ref, feat_ref, feat_out, pos_out, in_sems, out_sems
):
    blocks = brick_ref.shape[0]
    pieces = in_sems.shape[0]
    fetches = []
    for i in range(pieces):
        lanes = pl.ds(i * (blocks // pieces) * 128, blocks // pieces * 128)
        fetches.append(pltpu.make_async_copy(feat_hbm.at[:, lanes], feat_ref.at[:, lanes], in_sems.at[i]))
        fetches[-1].start()
    C, cap = s.C, sum(caps)
    for i in range(s.ny):
        fill_ref[i] = 0
        pos_out[i] = jnp.full(pos_out.shape[1:], -1.0, F32)
    fill_ref[s.ny] = 0
    live = count_ref[0]

    def place(n, carry):
        alive = n < live
        dest = jnp.where(alive, (brick_ref[n] // s.NB) % s.NB // s.byn, s.ny)
        order = jnp.where(alive, fill_ref[dest], 0)
        fill_ref[dest] = order + 1
        slot_ref[n] = jnp.where(alive, dest * cap + order, -1)
        lanes = pl.ds(pl.multiple_of(n * 128, 128), 128)
        feats = feat_ref[:, lanes] * area_ref[pl.ds(n, 1), :]
        feat_out[dest, pl.ds(pl.multiple_of(order * C, 8), C), :] = feats
        points = pos_ref[:, lanes]
        for d in range(3):
            pos_out[dest, d, pl.ds(order, 1), :] = points[d : d + 1, :]
        return carry

    for i, fetch in enumerate(fetches):
        fetch.wait()
        lax.fori_loop(i * (blocks // pieces), (i + 1) * (blocks // pieces), place, 0, unroll=8)
    at = caps[0] * C
    copies = []
    for i in range(s.ny):
        pairs = [(feat_out.at[i, pl.ds(0, at)], early_ref.at[i, pl.ds(0, at)])]
        pairs.append((feat_out.at[i, pl.ds(at, caps[1] * C)], late_ref.at[i]))
        for d in range(3):
            pairs.append((pos_out.at[i, d], early_ref.at[i, pl.ds(at + d * cap, cap)]))
        for k, (src, dst) in enumerate(pairs):
            copies.append(pltpu.make_async_copy(src, dst, out_sems.at[i, k]))
            copies[-1].start()
    for copy in copies:
        copy.wait()


def field_kernel(s, sdf_ref, gain_ref, out_ref):
    hi, lo = split(sdf_ref[...].reshape(s.bxn * s.Yl, s.G).T)
    ghi, glo = split(gain_ref[...])
    wide = dot(hi, ghi) + dot(lo, ghi) + dot(hi, glo)
    for y in range(s.Yl):
        out_ref[0, y] = wide[:, y * s.L : (y + 1) * s.L]


def kernel_tiles(points):
    px, py, pz = points
    scale = 1.0 / B
    sub = lax.broadcasted_iota(jnp.int32, pz.shape, 0).astype(F32)
    gz = ((sub + 0.5) - pz) * scale
    gz = gz * gz
    gx = []
    gy = []
    for a in range(B):
        d = (px - (a + 0.5)) * scale
        gx.append(1.0 - d * d)
        d = (py - (a + 0.5)) * scale
        gy.append(d * d + gz)
    tiles = []
    for a in range(B):
        for b in range(B):
            t = jnp.maximum(gx[a] - gy[b], 0.0)
            tiles.append(t * t)
    return tiles


def by_distance(s, row, items):
    bit = 1
    while bit < s.nx:
        far = row & bit != 0
        items = [
            [jnp.where(far, b, a) for a, b in zip(items[e], items[e ^ bit])] for e in range(s.nx)
        ]
        bit *= 2
    return items


def store_spectrum(s, row, a, tiles, keep_ref, send_ref):
    groups = by_distance(s, row, [tiles[g * s.bxn : (g + 1) * s.bxn] for g in range(s.nx)])
    for e in range(s.nx):
        for b in range(s.bxn):
            (send_ref if e & 1 else keep_ref)[e // 2, a, b] = groups[e][b]


def grid_to_spectrum(s, rows_of, table):
    tiles = []
    for y in range(0, s.Yl, 4):
        hi, lo = split(jnp.concatenate([rows_of(y + i) for i in range(4)], axis=1))
        res = dot(table, jnp.concatenate([hi, lo], axis=0))
        res = res[: s.K2] + res[s.K2 :]
        tiles += [res[:, i * s.L : (i + 1) * s.L] for i in range(4)]
    return block_turn(tiles, s.nx * s.bxn, s.cp)


def live_list(alive, slots, step, list_ref):
    def collect(n, live):
        list_ref[live] = n
        return live + alive(n)

    live = lax.fori_loop(0, slots, collect, 0, unroll=8)
    for i in range(step):
        list_ref[live + i] = 0
    return live


def add_blocks(s, caps, turn, id_ref, in_ref, pos_ref, at, grid_ref, list_ref):
    C = s.C
    cap = sum(caps)
    step = 4
    group = lax.broadcasted_iota(jnp.int32, (s.L, 128), 0) // s.cp % s.bxn
    live = live_list(lambda n: jnp.where(id_ref[7, n] == turn, 1, 0), s.ny * cap, step, list_ref)

    def per_group(h, carry):
        results = []
        slots = [list_ref[h * step + i] for i in range(step)]
        for i, slot in enumerate(slots):
            src, j = slot // cap, slot % cap
            points = [
                jnp.broadcast_to(pos_ref[src, pl.ds(at + d * cap + j, 1), :], (8, 128))
                - id_ref[3 + d, slot].astype(F32)
                for d in range(3)
            ]
            weights = jnp.concatenate(kernel_tiles(points), axis=0)
            place = jnp.clip(j - turn * caps[0], 0, caps[turn] - 1)
            feats = in_ref[src, pl.ds(pl.multiple_of(place * C, 8), C), :]
            spread = []
            for g in range(s.nx):
                spread += [feats[g * s.cp : (g + 1) * s.cp]] * s.bxn
            mine = jnp.where(h * step + i < live, id_ref[0, slot], -1)
            spread = jnp.where(group == mine, jnp.concatenate(spread, axis=0), 0.0)
            whi, wlo = split(weights)
            fhi, flo = split(spread)
            left = jnp.concatenate([whi, wlo], axis=1)
            right = jnp.concatenate([fhi, fhi], axis=1)
            if s.L == 128:
                under = jnp.concatenate([flo, jnp.zeros_like(flo)], axis=1)
                res = dot(left, jnp.concatenate([right, under], axis=0), NT)
                res = res[:, : s.L] + res[:, s.L :]
            else:
                res = dot(left, right, NT) + dot(whi, flo, NT)
            results.append(res.reshape(B, B, B, s.L))
        for slot, res in zip(slots, results):
            ys = pl.ds(pl.multiple_of(id_ref[1, slot] * B, B), B)
            zs = pl.ds(pl.multiple_of(id_ref[2, slot] * B, B), B)
            grid_ref[:, ys, zs, :] = grid_ref[:, ys, zs, :] + res
        return carry

    lax.fori_loop(0, (live + step - 1) // step, per_group, 0)


def encode_first_kernel(s, caps, id_ref, in_ref, init_ref, grid_ref, list_ref):
    for a in range(B):
        grid_ref[a] = init_ref[a]
    add_blocks(s, caps, 0, id_ref, in_ref, in_ref, caps[0] * s.C, grid_ref, list_ref)


def encode_last_kernel(
    s, caps, row_ref, id_ref, in_ref, pos_ref, before_ref, table_ref, grid_ref, keep_ref, send_ref,
    list_ref, sum_ref, held_ref, in_sem, out_sems
):
    fetch = pltpu.make_async_copy(before_ref, held_ref, in_sem)
    fetch.start()
    for a in range(B):
        sum_ref[a] = jnp.zeros(sum_ref.shape[1:], F32)
    add_blocks(s, caps, 1, id_ref, in_ref, pos_ref, 0, sum_ref, list_ref)
    fetch.wait()

    def transform(a, carry):
        held_ref[a] = held_ref[a] + sum_ref[a]
        pltpu.make_async_copy(held_ref.at[a], grid_ref.at[a], out_sems.at[a]).start()
        out = grid_to_spectrum(s, lambda y: held_ref[a, y], table_ref[...])
        store_spectrum(s, row_ref[0], a, out, keep_ref, send_ref)
        return carry

    lax.fori_loop(0, B, transform, 0)
    for a in range(B):
        pltpu.make_async_copy(held_ref.at[a], grid_ref.at[a], out_sems.at[a]).wait()


def mixed_rows(rows, whi, wlo):
    hi, lo = split(rows)
    width = whi.shape[1]
    if width == 128 and rows.shape[1] == 128:
        left = jnp.concatenate([hi, lo], axis=1)
        right = jnp.concatenate(
            [jnp.concatenate([whi, wlo], axis=1), jnp.concatenate([whi, jnp.zeros_like(wlo)], axis=1)], axis=0
        )
        res = dot(left, right)
        return res[:, :128] + res[:, 128:]
    return dot(hi, whi) + dot(lo, whi) + dot(hi, wlo)


def mix_kernel(s, grid_ref, mix_ref, bias_ref, out_ref):
    whi, wlo = split(mix_ref[...])
    for y in range(s.Yl):
        out_ref[0, y] = mixed_rows(grid_ref[0, y], whi, wlo) + bias_ref[...]


def readout_kernel(s, grid_ref, mix_ref, out_ref):
    whi, wlo = split(mix_ref[...])
    lane = lax.broadcasted_iota(jnp.int32, (B, s.LB), 1)
    for a in range(B):
        total = jnp.zeros((B, s.LB), F32)
        for by in range(s.byn):
            res = mixed_rows(grid_ref[0, by * B + a], whi, wlo)
            for bz in range(s.NB):
                mine = (lane // (s.bxn * s.byn) == bz) & (lane % s.byn == by)
                total = jnp.where(mine, res[bz * B : (bz + 1) * B], total)
        out_ref[0, a * B : (a + 1) * B, :] = total


def x_forward_kernel(s, keep_ref, recv_ref, table_ref, out_ref):
    M = s.M
    for i in range(s.ny):
        parts = []
        for k in range(s.KL):
            kz = i * s.KL + k
            parts.append(
                jnp.concatenate(
                    [
                        ref[0, pl.ds(ri * s.KZ + kz, s.Xl, stride=s.K2), :]
                        for ri in range(2)
                        for ref in (keep_ref, recv_ref)
                    ],
                    axis=0,
                )
            )
        hi, lo = split(jnp.concatenate(parts, axis=1))
        res = dot(table_ref[...], jnp.concatenate([hi, lo], axis=0))
        res = res[: 2 * M] + res[2 * M :]
        rows = []
        for ri in range(2):
            for k in range(s.KL):
                rows.append(res[ri * M : (ri + 1) * M, k * s.LY : (k + 1) * s.LY])
        out_ref[i] = jnp.concatenate(rows, axis=0).T


def y_spectrum(s, in_ref, table, u_ref, v_ref, cs):
    M = s.M
    both = jnp.concatenate([in_ref[pl.ds(c, s.G, stride=s.cp), :] for c in cs], axis=1)
    hi, lo = split(both)
    res = dot(table, jnp.concatenate([hi, lo], axis=0))
    res = res[: 2 * M] + res[2 * M :]
    out = []
    plus = half_signs(M, s.LK, 1.0)
    for i, c in enumerate(cs):
        part = res[:, i * s.LK : (i + 1) * s.LK]
        wave = part[:M] + plus * swap_halves(part[M:])
        out.append(wave * u_ref[c] + swap_halves(wave) * v_ref[c])
    return out


def y_kernel(s, in_ref, fwd_ref, inv_ref, u_ref, v_ref, out_ref):
    minus = half_signs(s.M, s.LK, -1.0)
    for c in range(0, s.cp, 2):
        prods = y_spectrum(s, in_ref, fwd_ref[...], u_ref, v_ref, (c, c + 1))
        both = jnp.concatenate(
            [jnp.concatenate([p, minus * swap_halves(p)], axis=0) for p in prods], axis=1
        )
        hi, lo = split(both)
        res = dot(inv_ref[...], jnp.concatenate([hi, lo, hi], axis=0))
        for i in range(2):
            out_ref[pl.ds(c + i, s.G, stride=s.cp), :] = res[:, i * s.LK : (i + 1) * s.LK]


def y_last_kernel(s, in_ref, fwd_ref, u_ref, v_ref, out_ref):
    total = jnp.zeros((s.M, s.LK), F32)
    for c in range(0, s.cp, 2):
        prods = y_spectrum(s, in_ref, fwd_ref[...], u_ref, v_ref, (c, c + 1))
        total = total + prods[0] + prods[1]
    M = s.M
    for r in range(2 * s.KL):
        part = total[:, r * M : (r + 1) * M]
        out_ref[r : r + 1, :] = jnp.concatenate([part[m : m + 1] for m in range(M)], axis=1)


def x_inverse_kernel(s, in_ref, table_ref, keep_ref, send_ref):
    for i in range(s.ny):
        hi, lo = split(in_ref[i])
        if s.LK == 128:
            res = dot(table_ref[...], jnp.concatenate([hi, lo, hi], axis=1), NT)
        else:
            t = table_ref[...]
            res = dot(t[:, : s.LK], hi, NT) + dot(t[:, : s.LK], lo, NT) + dot(t[:, 2 * s.LK :], hi, NT)
        for k in range(s.KL):
            for ri in range(2):
                at = (k * 2 + ri) * 2 * s.Xl
                places = pl.ds(ri * s.KZ + i * s.KL + k, s.Xl, stride=s.K2)
                keep_ref[places, :] = res[at : at + s.Xl]
                send_ref[places, :] = res[at + s.Xl : at + 2 * s.Xl]


def gelu(x):
    inner = math.sqrt(2.0 / math.pi) * (x + 0.044715 * (x * x * x))
    return 0.5 * x * (1.0 + jnp.tanh(inner))


def layer_kernel(s, row_ref, mixed_ref, inv_ref, fwd_ref, *refs):
    in_refs, (grid_ref, keep_ref, send_ref) = refs[: s.nx], refs[s.nx :]
    row = row_ref[0]
    groups = by_distance(s, row, [[ref[0, b] for b in range(s.bxn)] for ref in in_refs])
    tiles = block_turn([tile for group in groups for tile in group], s.Yl, s.cp)
    for y in range(0, s.Yl, 4):
        hi, lo = split(jnp.concatenate(tiles[y : y + 4], axis=1))
        res = dot(inv_ref[...], jnp.concatenate([hi, lo, hi], axis=0))
        for i in range(4):
            grid_ref[0, y + i] = gelu(mixed_ref[0, y + i] + res[:, i * s.L : (i + 1) * s.L])
    out = grid_to_spectrum(s, lambda y: grid_ref[0, y], fwd_ref[...])
    store_spectrum(s, row, 0, out, keep_ref, send_ref)


def decode_kernel(
    s, id_ref, base_ref, point_ref, spec_ref, turn_ref, mix_ref, hi_ref, lo_ref, inv_ref, out_ref, s_ref, list_ref
):
    modes = jnp.concatenate([spec_ref[i] for i in range(s.ny)], axis=0)
    real_row = lax.broadcasted_iota(jnp.int32, modes.shape, 0) // s.KL % 2 == 0

    def partner(x):
        return jnp.where(real_row, -pltpu.roll(x, s.K2 - s.KL, 0), pltpu.roll(x, s.KL, 0))

    modes = modes * turn_ref[0:1, :] + partner(modes) * turn_ref[1:2, :]
    mhi, mlo = split(jnp.concatenate([modes, partner(modes)], axis=1))
    wave = dot(jnp.concatenate([mhi, mlo], axis=0), hi_ref[...])
    wave = wave[: s.K2] + wave[s.K2 :] + dot(mhi, lo_ref[...])
    hi, lo = split(wave)
    field = dot(inv_ref[...], jnp.concatenate([hi, lo, hi], axis=0))
    width = s.bxn * s.byn
    per = 128 // width
    fields = []
    for q in range(field.shape[1] // 128):
        tiles = [field[z * B : (z + 1) * B, q * 128 : (q + 1) * 128] for z in range(s.NB)]
        for i, tile in enumerate(block_turn(tiles, per, width)):
            at = (q * per + i) * B
            fields.append(tile + mix_ref[at : at + B, :] + base_ref[0])
    out_ref[...] = jnp.zeros(out_ref.shape, F32)
    cell = lax.broadcasted_iota(jnp.int32, (s.LB, 128), 0)

    shi, slo = split(jnp.concatenate(fields, axis=0))
    s_ref[0], s_ref[1] = shi, slo
    slots = point_ref.shape[1]
    step = 8

    live = live_list(lambda n: id_ref[1, n], slots, step, list_ref)

    def per_group(h, carry):
        at = [list_ref[h * step + i] for i in range(step)]
        pick = jnp.concatenate([jnp.where(cell == id_ref[0, q], 1.0, 0.0).astype(BF) for q in at], axis=1)
        if s.LB == 128:
            vals = dot(jnp.concatenate([s_ref[0], s_ref[1]], axis=1), jnp.concatenate([pick, pick], axis=0))
        else:
            vals = dot(s_ref[0], pick) + dot(s_ref[1], pick)
        for i, q in enumerate(at):
            points = [jnp.broadcast_to(point_ref[d, pl.ds(q, 1), :], (8, 128)) for d in range(3)]
            top = jnp.zeros((B, 128), F32)
            low = jnp.zeros((B, 128), F32)
            for n, tile in enumerate(kernel_tiles(points)):
                top = top + tile * vals[n * B : (n + 1) * B, i * 128 : (i + 1) * 128]
                low = low + tile
            top = jnp.sum(top, axis=0, keepdims=True)
            low = jnp.sum(low, axis=0, keepdims=True)
            out_ref[pl.ds(id_ref[2, q], 1), :] = top / jnp.where(low > 0.0, low, 1.0)
        return carry

    lax.fori_loop(0, (live + step - 1) // step, per_group, 0)


def per_device(
    positions,
    point_feat,
    area,
    block_brick,
    block_count,
    sdf,
    grid_gain,
    mix_w,
    mix_b,
    spec_w,
    readout_w,
):
    nx, ny = lax.axis_size("gx"), lax.axis_size("gy")
    row_x, row_y = lax.axis_index("gx"), lax.axis_index("gy")
    modes = math.isqrt(spec_w.shape[4])
    s = Sizes(nx, ny, sdf.shape[2], point_feat.shape[0], modes, spec_w.shape[2] * ny)
    t = {name: jnp.asarray(value) for name, value in make_tables(s).items()}
    shape = lambda *dims: jax.ShapeDtypeStruct(dims, F32)
    blocks = block_brick.shape[0]
    cap = blocks // ny
    PB = positions.shape[1] // blocks
    C, G, M, L = s.C, s.G, s.M, s.L
    large = cap * 11 // 16
    caps = (large, cap - large)

    *outgoing, slot_of = call(
        functools.partial(pack_kernel, s, caps),
        "pack",
        (
            shape(ny, caps[0] * C + 3 * cap, PB),
            shape(ny, caps[1] * C, PB),
            jax.ShapeDtypeStruct((blocks,), jnp.int32),
        ),
        [SM, SM, VM, ANY, VM],
        (ANY, ANY, SM),
        1e6,
        6e6,
        scratch=[
            pltpu.SMEM((ny + 1,), jnp.int32),
            pltpu.VMEM(point_feat.shape, F32),
            pltpu.VMEM((ny + 1, cap * C, PB), F32),
            pltpu.VMEM((ny + 1, 3, cap, PB), F32),
            pltpu.SemaphoreType.DMA((4,)),
            pltpu.SemaphoreType.DMA((ny, 5)),
        ],
    )(block_brick, block_count, positions, point_feat, area.reshape(blocks, PB))
    early = lax.all_to_all(outgoing[0], "gy", split_axis=0, concat_axis=0, tiled=True)

    def placement(incoming):
        in_pos = incoming[:, caps[0] * C :, :]
        first = in_pos.reshape(ny, 3, cap, PB)[..., 0].transpose(1, 0, 2).reshape(3, ny * cap)
        brick = jnp.floor(first / B).astype(jnp.int32)
        start = jnp.stack([row_x * s.bxn, row_y * s.byn, jnp.zeros_like(row_x)])
        limit = jnp.array([s.bxn - 1, s.byn - 1, s.NB - 1], jnp.int32)
        local = jnp.clip(brick - start[:, None], 0, limit[:, None])
        corner = (local + start[:, None]) * B
        flat = local[2] * (s.bxn * s.byn) + local[0] * s.byn + local[1]
        owned = jnp.where(first[0:1] >= 0.0, local[0:1], -1)
        turn = jnp.where(jnp.arange(ny * cap) % cap < caps[0], 0, 1).astype(jnp.int32)
        turn = jnp.where(first[0] >= 0.0, turn, -1)
        ids = jnp.concatenate([owned, local[1:], corner, flat[None], turn[None]], axis=0)
        return ids, in_pos

    lane = jnp.arange(L)
    lane_bx = lane // s.cp % s.bxn
    same_bx = lane_bx[:, None] == lane_bx[None, :]
    gain_l = jnp.broadcast_to(grid_gain.reshape(nx, 1, s.cp), (nx, s.bxn, s.cp)).reshape(L)
    spread = (
        (jnp.arange(s.bxn)[:, None, None, None] == lane_bx[None, None, None, :])
        & (jnp.arange(s.Yl)[None, :, None, None] == jnp.arange(s.Yl)[None, None, :, None])
    )
    gains = jnp.where(spread, gain_l, 0.0).reshape(s.bxn * s.Yl, s.Yl * L)
    grid_shape = shape(B, s.Yl, G, L)
    grid_block = pl.BlockSpec((1, s.Yl, G, L), lambda a: (a, 0, 0, 0))
    whole = lambda array: pl.BlockSpec(array.shape, lambda a: (0,) * array.ndim)
    init = call(
        functools.partial(field_kernel, s),
        "field",
        grid_shape,
        [pl.BlockSpec((s.bxn, None, s.Yl, G), lambda a: (0, a, 0, 0)), whole(gains)],
        grid_block,
        3e9,
        1e7,
        grid=(B,),
    )(sdf.reshape(s.bxn, B, s.Yl, G), gains)

    on_lanes = lambda v: jnp.broadcast_to(v.reshape(nx, 1, s.cp), (nx, s.bxn, s.cp)).reshape(1, L)
    mixing = mix_w[0].T.reshape(nx, 1, s.cp, nx, 1, s.cp)
    mixing = jnp.broadcast_to(mixing, (nx, s.bxn, s.cp, nx, s.bxn, s.cp)).reshape(L, L)
    mixing = jnp.where(same_bx, mixing, 0.0)
    bias = on_lanes(mix_b[0])
    read_mix = jnp.sum(readout_w[:, None] * mix_w[1], axis=0)
    base = jnp.sum(readout_w * mix_b[1]).reshape(1)
    out_lane = jnp.arange(s.LB)
    reading = jnp.where(lane_bx[:, None] == out_lane[None, :] // s.byn % s.bxn, on_lanes(read_mix).reshape(L, 1), 0.0)
    mine = lax.dynamic_slice_in_dim(readout_w, row_x * s.cp, s.cp)

    def multipliers(w, scale):
        w = w.reshape(2, s.KL, s.cp, M, M)
        if scale is not None:
            w = w * scale[None, None, :, None, None]
        w = w.transpose(2, 4, 0, 1, 3)
        u = jnp.concatenate([w[:, :, 0:1], w[:, :, 0:1]], axis=2).reshape(s.cp, M, s.LK)
        v = jnp.concatenate([-w[:, :, 1:2], w[:, :, 1:2]], axis=2).reshape(s.cp, M, s.LK)
        return u, v

    u0, v0 = multipliers(spec_w[0], None)
    u1, v1 = multipliers(spec_w[1], mine)

    freq = jnp.asarray(s.freq, jnp.int32)
    turn = jnp.mod(freq[None, :] * (row_x * s.Xl) + freq[:, None] * (row_y * s.Yl), G).reshape(1, -1)
    angle = turn.astype(F32) * (2.0 * math.pi / G)
    turns = jnp.concatenate([jnp.cos(angle), jnp.sin(angle)], axis=0)
    x_fwd = lax.dynamic_index_in_dim(t["x_fwd"], row_x, 0, False)
    x_inv = lax.dynamic_index_in_dim(t["x_inv"], row_x, 0, False)
    row = row_x.astype(jnp.int32).reshape(1)
    prepared = (early, outgoing[1], init, mixing, bias, base, reading, u0, v0, u1, v1, turns, x_fwd, x_inv, row)
    early, second, init, mixing, bias, base, reading, u0, v0, u1, v1, turns, x_fwd, x_inv, row = (
        lax.optimization_barrier(prepared)
    )
    late = lax.all_to_all(second, "gy", split_axis=0, concat_axis=0, tiled=True)
    ids, in_pos = placement(early)

    half = s.nx // 2
    spec_shape = shape(half, B, s.bxn, s.K2, s.LY)
    before = call(
        functools.partial(encode_first_kernel, s, caps),
        "encode_first",
        grid_shape,
        [SM, VM, VM],
        VM,
        3e9,
        2e7,
        scratch=[pltpu.SMEM((ny * cap + 8,), jnp.int32)],
    )(ids, early, init)
    grid, keep, send = call(
        functools.partial(encode_last_kernel, s, caps),
        "encode_last",
        (grid_shape, spec_shape, spec_shape),
        [SM, SM, VM, VM, pl.BlockSpec(memory_space=pl.ANY), VM],
        (pl.BlockSpec(memory_space=pl.ANY), VM, VM),
        4e9,
        2.2e7,
        scratch=[
            pltpu.SMEM((ny * cap + 8,), jnp.int32),
            pltpu.VMEM(grid_shape.shape, F32),
            pltpu.VMEM(grid_shape.shape, F32),
            pltpu.SemaphoreType.DMA,
            pltpu.SemaphoreType.DMA((B,)),
        ],
    )(row, ids, late, in_pos, before, t["z_fwd"])

    def exchange(array, distance):
        return lax.ppermute(array, "gx", [(i, i ^ distance) for i in range(nx)])

    def to_modes(keep, send, beside=None):
        recv = exchange(send, 1).reshape(half, s.Xl * s.K2, s.LY)
        keep = keep.reshape(half, s.Xl * s.K2, s.LY)

        def part(d):
            block = pl.BlockSpec((1, s.Xl * s.K2, s.LY), lambda i: (d, 0, 0))
            return call(
                functools.partial(x_forward_kernel, s),
                "x_forward",
                shape(ny, s.LY, s.LK),
                [block, block, pl.BlockSpec(x_fwd.shape, lambda i: (0, 0))],
                pl.BlockSpec((ny, s.LY, s.LK), lambda i: (0, 0, 0)),
                2e8,
                3e6,
                grid=(1,),
                room=16,
            )(keep, recv, x_fwd)

        others = [exchange(part(d), 2 * d) for d in range(1, half)]
        spec = part(0)
        if beside is not None:
            beside, *others = lax.optimization_barrier((beside(), *others))
        for other in others:
            spec = spec + other
        spec = lax.all_to_all(spec, "gy", split_axis=0, concat_axis=0, tiled=True)
        return spec.reshape(G * s.cp, s.LK), beside

    spec, unused = to_modes(keep, send)
    mixed = call(
        functools.partial(mix_kernel, s),
        "mix",
        grid_shape,
        [grid_block, whole(mixing), whole(bias)],
        grid_block,
        2e9,
        1.7e7,
        grid=(B,),
    )(grid, mixing, bias)
    spec = call(
        functools.partial(y_kernel, s), "y_both", shape(G * s.cp, s.LK), [VM] * 5, VM, 1e9, 2e6, room=16
    )(spec, t["y_fwd"], t["y_inv"], u0, v0)
    spec = lax.all_to_all(spec.reshape(ny, s.LY, s.LK), "gy", split_axis=0, concat_axis=0, tiled=True)
    near = [exchange(spec, 2 * d) for d in range(1, half)]
    mixed, *near = lax.optimization_barrier((mixed, *near))
    near = [spec] + near
    fields = []
    for item in near:
        own, other = call(
            functools.partial(x_inverse_kernel, s),
            "x_inverse",
            (shape(s.Xl * s.K2, s.LY),) * 2,
            [VM, VM],
            (VM, VM),
            3e8,
            3e6,
            room=16,
        )(item, x_inv)
        fields += [own, exchange(other, 1)]
    fields = [f.reshape(B, s.bxn, s.K2, s.LY) for f in fields]
    field_block = pl.BlockSpec((1, s.bxn, s.K2, s.LY), lambda a: (a, 0, 0, 0))
    spec_block = pl.BlockSpec((half, 1, s.bxn, s.K2, s.LY), lambda a: (0, a, 0, 0, 0))
    grid, keep, send = call(
        functools.partial(layer_kernel, s),
        "layer",
        (grid_shape, spec_shape, spec_shape),
        [SM, grid_block, whole(t["z_inv"]), whole(t["z_fwd"])] + [field_block] * nx,
        (grid_block, spec_block, spec_block),
        4e9,
        2.1e7,
        grid=(B,),
        room=63,
    )(row, mixed, t["z_inv"], t["z_fwd"], *fields)

    def readout():
        return call(
            functools.partial(readout_kernel, s),
            "readout",
            shape(B, B * B, s.LB),
            [grid_block, whole(reading)],
            pl.BlockSpec((1, B * B, s.LB), lambda a: (a, 0, 0)),
            2e9,
            9e6,
            grid=(B,),
        )(grid, reading), decode_places()

    def decode_places():
        points = in_pos.reshape(ny, 3, cap, PB).transpose(1, 0, 2, 3).reshape(3, ny * cap, PB)
        live = (ids[7] >= 0).astype(jnp.int32)
        where = jnp.stack([ids[6], live, jnp.arange(ny * cap, dtype=jnp.int32)])
        return points - ids[3:6].astype(F32)[:, :, None], where

    spec, (read, (points, where)) = to_modes(keep, send, readout)
    last = call(
        functools.partial(y_last_kernel, s), "y_last", shape(2 * s.KL, M * M), [VM] * 4, VM, 1e9, 1e6, room=16
    )(spec, t["y_fwd"], u1, v1)

    last = functools.reduce(jnp.add, [last] + [exchange(last, e) for e in range(1, nx)])
    last = jnp.broadcast_to(last[None], (ny,) + last.shape)
    last = lax.all_to_all(last, "gy", split_axis=0, concat_axis=0, tiled=True)
    values = call(
        functools.partial(decode_kernel, s),
        "decode",
        shape(ny * cap, PB),
        [SM, SM] + [VM] * 7,
        VM,
        4e9,
        6e6,
        scratch=[pltpu.VMEM((2, B * B * B, s.LB), BF), pltpu.SMEM((ny * cap + 8,), jnp.int32)],
        room=32,
    )(where, base, points, last, turns, read.reshape(B * B * B, s.LB), t["xy_hi"], t["xy_lo"], t["z_last"])
    returned = lax.all_to_all(values.reshape(ny, cap, PB), "gy", split_axis=0, concat_axis=0, tiled=True)
    choose = (slot_of[:, None] == jnp.arange(ny * cap, dtype=jnp.int32)[None, :]).astype(F32)
    pressure = jnp.dot(choose, returned.reshape(ny * cap, PB), precision=lax.Precision.HIGHEST)
    return pressure.reshape(blocks * PB)


def solution(mesh):
    placed = (
        P(None, ("gx", "gy")),
        P(None, ("gx", "gy")),
        P(("gx", "gy")),
        P(("gx", "gy")),
        P(("gx", "gy")),
        P("gx", "gy", None),
        P(),
        P(),
        P(),
        P(None, None, "gy", "gx", None),
        P(),
    )
    return jax.shard_map(
        per_device, mesh=mesh, in_specs=placed, out_specs=P(("gx", "gy")), check_vma=False
    )
```

```python
import functools
import math

import jax
import jax.numpy as jnp
import ml_dtypes
import numpy as np
from jax import lax
from jax.experimental import pallas as pl
from jax.experimental.pallas import tpu as pltpu
from jax.sharding import PartitionSpec as P

B = 8
BF = jnp.bfloat16
F32 = jnp.float32
VM = pl.BlockSpec(memory_space=pltpu.VMEM)
SM = pl.BlockSpec(memory_space=pltpu.SMEM)
MIB = 1024 * 1024


def split(x):
    hi = x.astype(BF)
    lo = (x - hi.astype(F32)).astype(BF)
    return hi, lo


def np_split(table):
    table = np.asarray(table, np.float64).astype(np.float32)
    hi = table.astype(ml_dtypes.bfloat16)
    lo = (table - hi.astype(np.float32)).astype(ml_dtypes.bfloat16)
    return hi, lo


def dot(a, b, contract=((1,), (0,))):
    return lax.dot_general(a, b, (contract, ((), ())), preferred_element_type=F32)


NT = ((1,), (1,))


def call(body, name, out_shape, in_specs, out_specs, flops, moved, grid=None, scratch=(), room=58):
    extra = {} if grid is None else {"grid": grid}
    return pl.pallas_call(
        body,
        name=name,
        out_shape=out_shape,
        in_specs=in_specs,
        out_specs=out_specs,
        scratch_shapes=list(scratch),
        compiler_params=pltpu.CompilerParams(vmem_limit_bytes=room * MIB),
        cost_estimate=pl.CostEstimate(flops=int(flops), bytes_accessed=int(moved), transcendentals=0),
        **extra,
    )


class Sizes:
    def __init__(self, nx, ny, grid, channels, modes, kz):
        self.nx, self.ny, self.G, self.C, self.M, self.KZ = nx, ny, grid, channels, modes, kz
        self.NB = grid // B
        self.bxn = self.NB // nx
        self.byn = self.NB // ny
        self.Xl = grid // nx
        self.Yl = grid // ny
        self.cp = channels // nx
        self.KL = kz // ny
        self.L = channels * self.bxn
        self.LY = self.Yl * self.cp
        self.LK = 2 * self.KL * modes
        self.K2 = 2 * kz
        self.LB = self.NB * self.bxn * self.byn
        self.freq = np.where(np.arange(modes) < modes // 2, np.arange(modes), np.arange(modes) - modes)


def trig(s, places, freqs):
    angle = (np.asarray(places)[:, None] * np.asarray(freqs)[None, :]) % s.G * (2.0 * np.pi / s.G)
    return np.cos(angle), np.sin(angle)


def stack_left(table):
    hi, lo = np_split(table)
    zero = np.zeros_like(lo)
    return np.concatenate([np.concatenate([hi, hi], 1), np.concatenate([lo, zero], 1)], 0)


def wide_left(table):
    hi, lo = np_split(table)
    return np.concatenate([hi, hi, lo], 1)


def make_tables(s):
    t = {}
    c, n = trig(s, np.arange(s.KZ), np.arange(s.G))
    t["z_fwd"] = stack_left(np.concatenate([c, -n], 0))
    back = np.where(np.arange(s.KZ) == 0, 1.0, 2.0)[None, :] / s.G
    c, n = trig(s, np.arange(s.G), np.arange(s.KZ))
    c, n = c * back, -n * back
    t["z_inv"] = wide_left(np.concatenate([c, n], 1))
    t["z_last"] = wide_left(np.stack([c.reshape(s.G, s.ny, s.KL), n.reshape(s.G, s.ny, s.KL)], 2).reshape(s.G, -1))
    local = np.arange(s.Xl).reshape(s.bxn, B).T.reshape(-1)
    fwd, inv = [], []
    for row in range(s.nx):
        places = np.concatenate([row * s.Xl + local, (row ^ 1) * s.Xl + local])
        c, n = trig(s, s.freq, places)
        fwd.append(stack_left(np.concatenate([np.concatenate([c, n], 1), np.concatenate([-n, c], 1)], 0)))
        c, n = c.T, n.T
        table = np.zeros((s.KL, 2, 2 * s.Xl, 2, s.KL, s.M))
        for k in range(s.KL):
            table[k, 0, :, 0, k], table[k, 0, :, 1, k] = c, -n
            table[k, 1, :, 0, k], table[k, 1, :, 1, k] = n, c
        inv.append(wide_left(table.reshape(4 * s.KL * s.Xl, s.LK) / s.G))
    t["x_fwd"] = np.stack(fwd)
    t["x_inv"] = np.stack(inv)
    c, n = trig(s, s.freq, np.arange(s.G))
    t["y_fwd"] = stack_left(np.concatenate([c, n], 0))
    t["y_inv"] = wide_left(np.concatenate([c.T, n.T], 1) / s.G)
    xs = (np.arange(s.bxn)[:, None] * B + np.arange(B)[None, :]).T.reshape(B, 1, s.bxn, 1)
    ys = (np.arange(s.byn)[:, None] * B + np.arange(B)[None, :]).T.reshape(1, B, 1, s.byn)
    full = (B, B, s.bxn, s.byn)
    xs, ys = np.broadcast_to(xs, full).reshape(-1), np.broadcast_to(ys, full).reshape(-1)
    turn = s.freq[None, :, None] * xs[None, None, :] + s.freq[:, None, None] * ys[None, None, :]
    angle = (turn % s.G).reshape(s.M * s.M, -1) * (2.0 * np.pi / s.G)
    t["xy_hi"], t["xy_lo"] = np_split(np.concatenate([np.cos(angle), np.sin(angle)], 0) / (s.G * s.G))
    return t


def block_turn(tiles, blocks, width):
    count = len(tiles)
    if count == blocks and count * width == 128:
        lane = lax.broadcasted_iota(jnp.int32, tiles[0].shape, 1) // width
        tiles = list(tiles)
        step = 1
        while step < count:
            upper = (lane & step) != 0
            for i in range(count):
                if i & step == 0:
                    a, b = tiles[i], tiles[i | step]
                    up = pltpu.roll(b, step * width, 1)
                    down = pltpu.roll(a, 128 - step * width, 1)
                    tiles[i] = jnp.where(upper, up, a)
                    tiles[i | step] = jnp.where(upper, b, down)
            step *= 2
        return tiles
    return [
        jnp.concatenate([tile[:, b * width : (b + 1) * width] for tile in tiles], axis=1)
        for b in range(blocks)
    ]


def swap_halves(x):
    half = x.shape[1] // 2
    if x.shape[1] == 128:
        return pltpu.roll(x, half, 1)
    return jnp.concatenate([x[:, half:], x[:, :half]], axis=1)


def half_signs(rows, width, first):
    lane = lax.broadcasted_iota(jnp.int32, (rows, width), 1)
    return jnp.where(lane < width // 2, first, -first).astype(F32)


def pack_kernel(s, caps, brick_ref, count_ref, pos_ref, feat_ref, area_ref, *refs):
    out_refs, (slot_ref, fill_ref, feat_out, pos_out) = refs[: len(caps)], refs[len(caps) :]
    blocks = brick_ref.shape[0]
    C, cap = s.C, sum(caps)
    for i in range(s.ny):
        fill_ref[i] = 0
        pos_out[i] = jnp.full(pos_out.shape[1:], -1.0, F32)
    fill_ref[s.ny] = 0
    live = count_ref[0]

    def place(n, carry):
        alive = n < live
        dest = jnp.where(alive, (brick_ref[n] // s.NB) % s.NB // s.byn, s.ny)
        order = jnp.where(alive, fill_ref[dest], 0)
        fill_ref[dest] = order + 1
        slot_ref[n] = jnp.where(alive, dest * cap + order, -1)
        lanes = pl.ds(pl.multiple_of(n * 128, 128), 128)
        feats = feat_ref[:, lanes] * area_ref[pl.ds(n, 1), :]
        feat_out[dest, pl.ds(pl.multiple_of(order * C, 8), C), :] = feats
        points = pos_ref[:, lanes]
        for d in range(3):
            pos_out[dest, d, pl.ds(order, 1), :] = points[d : d + 1, :]
        return carry

    lax.fori_loop(0, blocks, place, 0, unroll=8)
    early_ref, late_ref = out_refs
    at = caps[0] * C
    for i in range(s.ny):
        early_ref[i, :at] = feat_out[i, :at]
        late_ref[i] = feat_out[i, at:]
        for d in range(3):
            early_ref[i, at + d * cap : at + (d + 1) * cap] = pos_out[i, d]


def field_kernel(s, sdf_ref, gain_ref, out_ref):
    hi, lo = split(sdf_ref[...].reshape(s.bxn * s.Yl, s.G).T)
    ghi, glo = split(gain_ref[...])
    wide = dot(hi, ghi) + dot(lo, ghi) + dot(hi, glo)
    for y in range(s.Yl):
        out_ref[0, y] = wide[:, y * s.L : (y + 1) * s.L]


def kernel_tiles(points):
    px, py, pz = points
    scale = 1.0 / B
    sub = lax.broadcasted_iota(jnp.int32, pz.shape, 0).astype(F32)
    gz = ((sub + 0.5) - pz) * scale
    gz = gz * gz
    gx = []
    gy = []
    for a in range(B):
        d = (px - (a + 0.5)) * scale
        gx.append(1.0 - d * d)
        d = (py - (a + 0.5)) * scale
        gy.append(d * d + gz)
    tiles = []
    for a in range(B):
        for b in range(B):
            t = jnp.maximum(gx[a] - gy[b], 0.0)
            tiles.append(t * t)
    return tiles


def by_distance(s, row, items):
    bit = 1
    while bit < s.nx:
        far = row & bit != 0
        items = [
            [jnp.where(far, b, a) for a, b in zip(items[e], items[e ^ bit])] for e in range(s.nx)
        ]
        bit *= 2
    return items


def store_spectrum(s, row, a, tiles, keep_ref, send_ref):
    groups = by_distance(s, row, [tiles[g * s.bxn : (g + 1) * s.bxn] for g in range(s.nx)])
    for e in range(s.nx):
        for b in range(s.bxn):
            (send_ref if e & 1 else keep_ref)[e // 2, a, b] = groups[e][b]


def grid_to_spectrum(s, rows_of, table):
    tiles = []
    for y in range(0, s.Yl, 4):
        hi, lo = split(jnp.concatenate([rows_of(y + i) for i in range(4)], axis=1))
        res = dot(table, jnp.concatenate([hi, lo], axis=0))
        res = res[: s.K2] + res[s.K2 :]
        tiles += [res[:, i * s.L : (i + 1) * s.L] for i in range(4)]
    return block_turn(tiles, s.nx * s.bxn, s.cp)


def live_list(alive, slots, step, list_ref):
    def collect(n, live):
        list_ref[live] = n
        return live + alive(n)

    live = lax.fori_loop(0, slots, collect, 0, unroll=8)
    for i in range(step):
        list_ref[live + i] = 0
    return live


def add_blocks(s, caps, turn, id_ref, in_ref, pos_ref, at, grid_ref, list_ref):
    C = s.C
    cap = sum(caps)
    step = 8
    group = lax.broadcasted_iota(jnp.int32, (s.L, 128), 0) // s.cp % s.bxn
    live = live_list(lambda n: jnp.where(id_ref[7, n] == turn, 1, 0), s.ny * cap, step, list_ref)

    def per_group(h, carry):
        results = []
        slots = [list_ref[h * step + i] for i in range(step)]
        for i, slot in enumerate(slots):
            src, j = slot // cap, slot % cap
            points = [
                jnp.broadcast_to(pos_ref[src, pl.ds(at + d * cap + j, 1), :], (8, 128))
                - id_ref[3 + d, slot].astype(F32)
                for d in range(3)
            ]
            weights = jnp.concatenate(kernel_tiles(points), axis=0)
            place = jnp.clip(j - turn * caps[0], 0, caps[turn] - 1)
            feats = in_ref[src, pl.ds(pl.multiple_of(place * C, 8), C), :]
            spread = []
            for g in range(s.nx):
                spread += [feats[g * s.cp : (g + 1) * s.cp]] * s.bxn
            mine = jnp.where(h * step + i < live, id_ref[0, slot], -1)
            spread = jnp.where(group == mine, jnp.concatenate(spread, axis=0), 0.0)
            whi, wlo = split(weights)
            fhi, flo = split(spread)
            left = jnp.concatenate([whi, wlo], axis=1)
            right = jnp.concatenate([fhi, fhi], axis=1)
            if s.L == 128:
                under = jnp.concatenate([flo, jnp.zeros_like(flo)], axis=1)
                res = dot(left, jnp.concatenate([right, under], axis=0), NT)
                res = res[:, : s.L] + res[:, s.L :]
            else:
                res = dot(left, right, NT) + dot(whi, flo, NT)
            results.append(res.reshape(B, B, B, s.L))
        for slot, res in zip(slots, results):
            ys = pl.ds(pl.multiple_of(id_ref[1, slot] * B, B), B)
            zs = pl.ds(pl.multiple_of(id_ref[2, slot] * B, B), B)
            grid_ref[:, ys, zs, :] = grid_ref[:, ys, zs, :] + res
        return carry

    lax.fori_loop(0, (live + step - 1) // step, per_group, 0)


def encode_first_kernel(s, caps, id_ref, in_ref, init_ref, grid_ref, list_ref):
    for a in range(B):
        grid_ref[a] = init_ref[a]
    add_blocks(s, caps, 0, id_ref, in_ref, in_ref, caps[0] * s.C, grid_ref, list_ref)


def encode_last_kernel(
    s, caps, row_ref, id_ref, in_ref, pos_ref, before_ref, table_ref, grid_ref, keep_ref, send_ref,
    list_ref, sum_ref, held_ref, in_sem, out_sems
):
    fetch = pltpu.make_async_copy(before_ref, held_ref, in_sem)
    fetch.start()
    for a in range(B):
        sum_ref[a] = jnp.zeros(sum_ref.shape[1:], F32)
    add_blocks(s, caps, 1, id_ref, in_ref, pos_ref, 0, sum_ref, list_ref)
    fetch.wait()

    def transform(a, carry):
        held_ref[a] = held_ref[a] + sum_ref[a]
        pltpu.make_async_copy(held_ref.at[a], grid_ref.at[a], out_sems.at[a]).start()
        out = grid_to_spectrum(s, lambda y: held_ref[a, y], table_ref[...])
        store_spectrum(s, row_ref[0], a, out, keep_ref, send_ref)
        return carry

    lax.fori_loop(0, B, transform, 0)
    for a in range(B):
        pltpu.make_async_copy(held_ref.at[a], grid_ref.at[a], out_sems.at[a]).wait()


def mixed_rows(rows, whi, wlo):
    hi, lo = split(rows)
    width = whi.shape[1]
    if width == 128 and rows.shape[1] == 128:
        left = jnp.concatenate([hi, lo], axis=1)
        right = jnp.concatenate(
            [jnp.concatenate([whi, wlo], axis=1), jnp.concatenate([whi, jnp.zeros_like(wlo)], axis=1)], axis=0
        )
        res = dot(left, right)
        return res[:, :128] + res[:, 128:]
    return dot(hi, whi) + dot(lo, whi) + dot(hi, wlo)


def mix_kernel(s, grid_ref, mix_ref, bias_ref, out_ref):
    whi, wlo = split(mix_ref[...])
    for y in range(s.Yl):
        out_ref[0, y] = mixed_rows(grid_ref[0, y], whi, wlo) + bias_ref[...]


def readout_kernel(s, grid_ref, mix_ref, out_ref):
    whi, wlo = split(mix_ref[...])
    lane = lax.broadcasted_iota(jnp.int32, (B, s.LB), 1)
    for a in range(B):
        total = jnp.zeros((B, s.LB), F32)
        for by in range(s.byn):
            res = mixed_rows(grid_ref[0, by * B + a], whi, wlo)
            for bz in range(s.NB):
                mine = (lane // (s.bxn * s.byn) == bz) & (lane % s.byn == by)
                total = jnp.where(mine, res[bz * B : (bz + 1) * B], total)
        out_ref[0, a * B : (a + 1) * B, :] = total


def x_forward_kernel(s, keep_ref, recv_ref, table_ref, out_ref):
    M = s.M
    for i in range(s.ny):
        parts = []
        for k in range(s.KL):
            kz = i * s.KL + k
            parts.append(
                jnp.concatenate(
                    [
                        ref[0, pl.ds(ri * s.KZ + kz, s.Xl, stride=s.K2), :]
                        for ri in range(2)
                        for ref in (keep_ref, recv_ref)
                    ],
                    axis=0,
                )
            )
        hi, lo = split(jnp.concatenate(parts, axis=1))
        res = dot(table_ref[...], jnp.concatenate([hi, lo], axis=0))
        res = res[: 2 * M] + res[2 * M :]
        rows = []
        for ri in range(2):
            for k in range(s.KL):
                rows.append(res[ri * M : (ri + 1) * M, k * s.LY : (k + 1) * s.LY])
        out_ref[i] = jnp.concatenate(rows, axis=0).T


def y_spectrum(s, in_ref, table, u_ref, v_ref, cs):
    M = s.M
    both = jnp.concatenate([in_ref[pl.ds(c, s.G, stride=s.cp), :] for c in cs], axis=1)
    hi, lo = split(both)
    res = dot(table, jnp.concatenate([hi, lo], axis=0))
    res = res[: 2 * M] + res[2 * M :]
    out = []
    plus = half_signs(M, s.LK, 1.0)
    for i, c in enumerate(cs):
        part = res[:, i * s.LK : (i + 1) * s.LK]
        wave = part[:M] + plus * swap_halves(part[M:])
        out.append(wave * u_ref[c] + swap_halves(wave) * v_ref[c])
    return out


def y_kernel(s, in_ref, fwd_ref, inv_ref, u_ref, v_ref, out_ref):
    minus = half_signs(s.M, s.LK, -1.0)
    for c in range(0, s.cp, 2):
        prods = y_spectrum(s, in_ref, fwd_ref[...], u_ref, v_ref, (c, c + 1))
        both = jnp.concatenate(
            [jnp.concatenate([p, minus * swap_halves(p)], axis=0) for p in prods], axis=1
        )
        hi, lo = split(both)
        res = dot(inv_ref[...], jnp.concatenate([hi, lo, hi], axis=0))
        for i in range(2):
            out_ref[pl.ds(c + i, s.G, stride=s.cp), :] = res[:, i * s.LK : (i + 1) * s.LK]


def y_last_kernel(s, in_ref, fwd_ref, u_ref, v_ref, out_ref):
    total = jnp.zeros((s.M, s.LK), F32)
    for c in range(0, s.cp, 2):
        prods = y_spectrum(s, in_ref, fwd_ref[...], u_ref, v_ref, (c, c + 1))
        total = total + prods[0] + prods[1]
    M = s.M
    for r in range(2 * s.KL):
        part = total[:, r * M : (r + 1) * M]
        out_ref[r : r + 1, :] = jnp.concatenate([part[m : m + 1] for m in range(M)], axis=1)


def x_inverse_kernel(s, in_ref, table_ref, keep_ref, send_ref):
    for i in range(s.ny):
        hi, lo = split(in_ref[i])
        if s.LK == 128:
            res = dot(table_ref[...], jnp.concatenate([hi, lo, hi], axis=1), NT)
        else:
            t = table_ref[...]
            res = dot(t[:, : s.LK], hi, NT) + dot(t[:, : s.LK], lo, NT) + dot(t[:, 2 * s.LK :], hi, NT)
        for k in range(s.KL):
            for ri in range(2):
                at = (k * 2 + ri) * 2 * s.Xl
                places = pl.ds(ri * s.KZ + i * s.KL + k, s.Xl, stride=s.K2)
                keep_ref[places, :] = res[at : at + s.Xl]
                send_ref[places, :] = res[at + s.Xl : at + 2 * s.Xl]


def gelu(x):
    inner = math.sqrt(2.0 / math.pi) * (x + 0.044715 * (x * x * x))
    return 0.5 * x * (1.0 + jnp.tanh(inner))


def layer_kernel(s, row_ref, mixed_ref, inv_ref, fwd_ref, *refs):
    in_refs, (grid_ref, keep_ref, send_ref) = refs[: s.nx], refs[s.nx :]
    row = row_ref[0]
    groups = by_distance(s, row, [[ref[0, b] for b in range(s.bxn)] for ref in in_refs])
    tiles = block_turn([tile for group in groups for tile in group], s.Yl, s.cp)
    for y in range(0, s.Yl, 4):
        hi, lo = split(jnp.concatenate(tiles[y : y + 4], axis=1))
        res = dot(inv_ref[...], jnp.concatenate([hi, lo, hi], axis=0))
        for i in range(4):
            grid_ref[0, y + i] = gelu(mixed_ref[0, y + i] + res[:, i * s.L : (i + 1) * s.L])
    out = grid_to_spectrum(s, lambda y: grid_ref[0, y], fwd_ref[...])
    store_spectrum(s, row, 0, out, keep_ref, send_ref)


def decode_kernel(
    s, id_ref, base_ref, point_ref, spec_ref, turn_ref, mix_ref, hi_ref, lo_ref, inv_ref, out_ref, s_ref, list_ref
):
    modes = jnp.concatenate([spec_ref[i] for i in range(s.ny)], axis=0)
    real_row = lax.broadcasted_iota(jnp.int32, modes.shape, 0) // s.KL % 2 == 0

    def partner(x):
        return jnp.where(real_row, -pltpu.roll(x, s.K2 - s.KL, 0), pltpu.roll(x, s.KL, 0))

    modes = modes * turn_ref[0:1, :] + partner(modes) * turn_ref[1:2, :]
    mhi, mlo = split(jnp.concatenate([modes, partner(modes)], axis=1))
    wave = dot(jnp.concatenate([mhi, mlo], axis=0), hi_ref[...])
    wave = wave[: s.K2] + wave[s.K2 :] + dot(mhi, lo_ref[...])
    hi, lo = split(wave)
    field = dot(inv_ref[...], jnp.concatenate([hi, lo, hi], axis=0))
    width = s.bxn * s.byn
    per = 128 // width
    fields = []
    for q in range(field.shape[1] // 128):
        tiles = [field[z * B : (z + 1) * B, q * 128 : (q + 1) * 128] for z in range(s.NB)]
        for i, tile in enumerate(block_turn(tiles, per, width)):
            at = (q * per + i) * B
            fields.append(tile + mix_ref[at : at + B, :] + base_ref[0])
    out_ref[...] = jnp.zeros(out_ref.shape, F32)
    cell = lax.broadcasted_iota(jnp.int32, (s.LB, 128), 0)

    shi, slo = split(jnp.concatenate(fields, axis=0))
    s_ref[0], s_ref[1] = shi, slo
    slots = point_ref.shape[1]
    step = 8

    live = live_list(lambda n: id_ref[1, n], slots, step, list_ref)

    def per_group(h, carry):
        at = [list_ref[h * step + i] for i in range(step)]
        pick = jnp.concatenate([jnp.where(cell == id_ref[0, q], 1.0, 0.0).astype(BF) for q in at], axis=1)
        if s.LB == 128:
            vals = dot(jnp.concatenate([s_ref[0], s_ref[1]], axis=1), jnp.concatenate([pick, pick], axis=0))
        else:
            vals = dot(s_ref[0], pick) + dot(s_ref[1], pick)
        for i, q in enumerate(at):
            points = [jnp.broadcast_to(point_ref[d, pl.ds(q, 1), :], (8, 128)) for d in range(3)]
            top = jnp.zeros((B, 128), F32)
            low = jnp.zeros((B, 128), F32)
            for n, tile in enumerate(kernel_tiles(points)):
                top = top + tile * vals[n * B : (n + 1) * B, i * 128 : (i + 1) * 128]
                low = low + tile
            top = jnp.sum(top, axis=0, keepdims=True)
            low = jnp.sum(low, axis=0, keepdims=True)
            out_ref[pl.ds(id_ref[2, q], 1), :] = top / jnp.where(low > 0.0, low, 1.0)
        return carry

    lax.fori_loop(0, (live + step - 1) // step, per_group, 0)


def per_device(
    positions,
    point_feat,
    area,
    block_brick,
    block_count,
    sdf,
    grid_gain,
    mix_w,
    mix_b,
    spec_w,
    readout_w,
):
    nx, ny = lax.axis_size("gx"), lax.axis_size("gy")
    row_x, row_y = lax.axis_index("gx"), lax.axis_index("gy")
    modes = math.isqrt(spec_w.shape[4])
    s = Sizes(nx, ny, sdf.shape[2], point_feat.shape[0], modes, spec_w.shape[2] * ny)
    t = {name: jnp.asarray(value) for name, value in make_tables(s).items()}
    shape = lambda *dims: jax.ShapeDtypeStruct(dims, F32)
    blocks = block_brick.shape[0]
    cap = blocks // ny
    PB = positions.shape[1] // blocks
    C, G, M, L = s.C, s.G, s.M, s.L
    large = cap * 5 // 16 * 2
    caps = (large, cap - large)

    *outgoing, slot_of = call(
        functools.partial(pack_kernel, s, caps),
        "pack",
        (
            shape(ny, caps[0] * C + 3 * cap, PB),
            shape(ny, caps[1] * C, PB),
            jax.ShapeDtypeStruct((blocks,), jnp.int32),
        ),
        [SM, SM, VM, VM, VM],
        (VM, VM, SM),
        1e6,
        6e6,
        scratch=[
            pltpu.SMEM((ny + 1,), jnp.int32),
            pltpu.VMEM((ny + 1, cap * C, PB), F32),
            pltpu.VMEM((ny + 1, 3, cap, PB), F32),
        ],
    )(block_brick, block_count, positions, point_feat, area.reshape(blocks, PB))
    early = lax.all_to_all(outgoing[0], "gy", split_axis=0, concat_axis=0, tiled=True)

    def placement(incoming):
        in_pos = incoming[:, caps[0] * C :, :]
        first = in_pos.reshape(ny, 3, cap, PB)[..., 0].transpose(1, 0, 2).reshape(3, ny * cap)
        brick = jnp.floor(first / B).astype(jnp.int32)
        start = jnp.stack([row_x * s.bxn, row_y * s.byn, jnp.zeros_like(row_x)])
        limit = jnp.array([s.bxn - 1, s.byn - 1, s.NB - 1], jnp.int32)
        local = jnp.clip(brick - start[:, None], 0, limit[:, None])
        corner = (local + start[:, None]) * B
        flat = local[2] * (s.bxn * s.byn) + local[0] * s.byn + local[1]
        owned = jnp.where(first[0:1] >= 0.0, local[0:1], -1)
        turn = jnp.where(jnp.arange(ny * cap) % cap < caps[0], 0, 1).astype(jnp.int32)
        turn = jnp.where(first[0] >= 0.0, turn, -1)
        ids = jnp.concatenate([owned, local[1:], corner, flat[None], turn[None]], axis=0)
        return ids, in_pos

    lane = jnp.arange(L)
    lane_bx = lane // s.cp % s.bxn
    same_bx = lane_bx[:, None] == lane_bx[None, :]
    gain_l = jnp.broadcast_to(grid_gain.reshape(nx, 1, s.cp), (nx, s.bxn, s.cp)).reshape(L)
    spread = (
        (jnp.arange(s.bxn)[:, None, None, None] == lane_bx[None, None, None, :])
        & (jnp.arange(s.Yl)[None, :, None, None] == jnp.arange(s.Yl)[None, None, :, None])
    )
    gains = jnp.where(spread, gain_l, 0.0).reshape(s.bxn * s.Yl, s.Yl * L)
    grid_shape = shape(B, s.Yl, G, L)
    grid_block = pl.BlockSpec((1, s.Yl, G, L), lambda a: (a, 0, 0, 0))
    whole = lambda array: pl.BlockSpec(array.shape, lambda a: (0,) * array.ndim)
    init = call(
        functools.partial(field_kernel, s),
        "field",
        grid_shape,
        [pl.BlockSpec((s.bxn, None, s.Yl, G), lambda a: (0, a, 0, 0)), whole(gains)],
        grid_block,
        3e9,
        1e7,
        grid=(B,),
    )(sdf.reshape(s.bxn, B, s.Yl, G), gains)

    on_lanes = lambda v: jnp.broadcast_to(v.reshape(nx, 1, s.cp), (nx, s.bxn, s.cp)).reshape(1, L)
    mixing = mix_w[0].T.reshape(nx, 1, s.cp, nx, 1, s.cp)
    mixing = jnp.broadcast_to(mixing, (nx, s.bxn, s.cp, nx, s.bxn, s.cp)).reshape(L, L)
    mixing = jnp.where(same_bx, mixing, 0.0)
    bias = on_lanes(mix_b[0])
    read_mix = jnp.sum(readout_w[:, None] * mix_w[1], axis=0)
    base = jnp.sum(readout_w * mix_b[1]).reshape(1)
    out_lane = jnp.arange(s.LB)
    reading = jnp.where(lane_bx[:, None] == out_lane[None, :] // s.byn % s.bxn, on_lanes(read_mix).reshape(L, 1), 0.0)
    mine = lax.dynamic_slice_in_dim(readout_w, row_x * s.cp, s.cp)

    def multipliers(w, scale):
        w = w.reshape(2, s.KL, s.cp, M, M)
        if scale is not None:
            w = w * scale[None, None, :, None, None]
        w = w.transpose(2, 4, 0, 1, 3)
        u = jnp.concatenate([w[:, :, 0:1], w[:, :, 0:1]], axis=2).reshape(s.cp, M, s.LK)
        v = jnp.concatenate([-w[:, :, 1:2], w[:, :, 1:2]], axis=2).reshape(s.cp, M, s.LK)
        return u, v

    u0, v0 = multipliers(spec_w[0], None)
    u1, v1 = multipliers(spec_w[1], mine)

    freq = jnp.asarray(s.freq, jnp.int32)
    turn = jnp.mod(freq[None, :] * (row_x * s.Xl) + freq[:, None] * (row_y * s.Yl), G).reshape(1, -1)
    angle = turn.astype(F32) * (2.0 * math.pi / G)
    turns = jnp.concatenate([jnp.cos(angle), jnp.sin(angle)], axis=0)
    x_fwd = lax.dynamic_index_in_dim(t["x_fwd"], row_x, 0, False)
    x_inv = lax.dynamic_index_in_dim(t["x_inv"], row_x, 0, False)
    row = row_x.astype(jnp.int32).reshape(1)
    prepared = (early, outgoing[1], init, mixing, bias, base, reading, u0, v0, u1, v1, turns, x_fwd, x_inv, row)
    early, second, init, mixing, bias, base, reading, u0, v0, u1, v1, turns, x_fwd, x_inv, row = (
        lax.optimization_barrier(prepared)
    )
    late = lax.all_to_all(second, "gy", split_axis=0, concat_axis=0, tiled=True)
    ids, in_pos = placement(early)

    half = s.nx // 2
    spec_shape = shape(half, B, s.bxn, s.K2, s.LY)
    before = call(
        functools.partial(encode_first_kernel, s, caps),
        "encode_first",
        grid_shape,
        [SM, VM, VM],
        VM,
        3e9,
        2e7,
        scratch=[pltpu.SMEM((ny * cap + 8,), jnp.int32)],
    )(ids, early, init)
    grid, keep, send = call(
        functools.partial(encode_last_kernel, s, caps),
        "encode_last",
        (grid_shape, spec_shape, spec_shape),
        [SM, SM, VM, VM, pl.BlockSpec(memory_space=pl.ANY), VM],
        (pl.BlockSpec(memory_space=pl.ANY), VM, VM),
        4e9,
        2.2e7,
        scratch=[
            pltpu.SMEM((ny * cap + 8,), jnp.int32),
            pltpu.VMEM(grid_shape.shape, F32),
            pltpu.VMEM(grid_shape.shape, F32),
            pltpu.SemaphoreType.DMA,
            pltpu.SemaphoreType.DMA((B,)),
        ],
    )(row, ids, late, in_pos, before, t["z_fwd"])

    def exchange(array, distance):
        return lax.ppermute(array, "gx", [(i, i ^ distance) for i in range(nx)])

    def to_modes(keep, send, beside=None):
        recv = exchange(send, 1).reshape(half, s.Xl * s.K2, s.LY)
        keep = keep.reshape(half, s.Xl * s.K2, s.LY)

        def part(d):
            block = pl.BlockSpec((1, s.Xl * s.K2, s.LY), lambda i: (d, 0, 0))
            return call(
                functools.partial(x_forward_kernel, s),
                "x_forward",
                shape(ny, s.LY, s.LK),
                [block, block, pl.BlockSpec(x_fwd.shape, lambda i: (0, 0))],
                pl.BlockSpec((ny, s.LY, s.LK), lambda i: (0, 0, 0)),
                2e8,
                3e6,
                grid=(1,),
                room=16,
            )(keep, recv, x_fwd)

        others = [exchange(part(d), 2 * d) for d in range(1, half)]
        spec = part(0)
        if beside is not None:
            beside, *others = lax.optimization_barrier((beside(), *others))
        for other in others:
            spec = spec + other
        spec = lax.all_to_all(spec, "gy", split_axis=0, concat_axis=0, tiled=True)
        return spec.reshape(G * s.cp, s.LK), beside

    spec, unused = to_modes(keep, send)
    mixed = call(
        functools.partial(mix_kernel, s),
        "mix",
        grid_shape,
        [grid_block, whole(mixing), whole(bias)],
        grid_block,
        2e9,
        1.7e7,
        grid=(B,),
    )(grid, mixing, bias)
    spec = call(
        functools.partial(y_kernel, s), "y_both", shape(G * s.cp, s.LK), [VM] * 5, VM, 1e9, 2e6, room=16
    )(spec, t["y_fwd"], t["y_inv"], u0, v0)
    spec = lax.all_to_all(spec.reshape(ny, s.LY, s.LK), "gy", split_axis=0, concat_axis=0, tiled=True)
    near = [exchange(spec, 2 * d) for d in range(1, half)]
    mixed, *near = lax.optimization_barrier((mixed, *near))
    near = [spec] + near
    fields = []
    for item in near:
        own, other = call(
            functools.partial(x_inverse_kernel, s),
            "x_inverse",
            (shape(s.Xl * s.K2, s.LY),) * 2,
            [VM, VM],
            (VM, VM),
            3e8,
            3e6,
            room=16,
        )(item, x_inv)
        fields += [own, exchange(other, 1)]
    fields = [f.reshape(B, s.bxn, s.K2, s.LY) for f in fields]
    field_block = pl.BlockSpec((1, s.bxn, s.K2, s.LY), lambda a: (a, 0, 0, 0))
    spec_block = pl.BlockSpec((half, 1, s.bxn, s.K2, s.LY), lambda a: (0, a, 0, 0, 0))
    grid, keep, send = call(
        functools.partial(layer_kernel, s),
        "layer",
        (grid_shape, spec_shape, spec_shape),
        [SM, grid_block, whole(t["z_inv"]), whole(t["z_fwd"])] + [field_block] * nx,
        (grid_block, spec_block, spec_block),
        4e9,
        2.1e7,
        grid=(B,),
        room=63,
    )(row, mixed, t["z_inv"], t["z_fwd"], *fields)

    def readout():
        return call(
            functools.partial(readout_kernel, s),
            "readout",
            shape(B, B * B, s.LB),
            [grid_block, whole(reading)],
            pl.BlockSpec((1, B * B, s.LB), lambda a: (a, 0, 0)),
            2e9,
            9e6,
            grid=(B,),
        )(grid, reading), decode_places()

    def decode_places():
        points = in_pos.reshape(ny, 3, cap, PB).transpose(1, 0, 2, 3).reshape(3, ny * cap, PB)
        live = (ids[7] >= 0).astype(jnp.int32)
        where = jnp.stack([ids[6], live, jnp.arange(ny * cap, dtype=jnp.int32)])
        return points - ids[3:6].astype(F32)[:, :, None], where

    spec, (read, (points, where)) = to_modes(keep, send, readout)
    last = call(
        functools.partial(y_last_kernel, s), "y_last", shape(2 * s.KL, M * M), [VM] * 4, VM, 1e9, 1e6, room=16
    )(spec, t["y_fwd"], u1, v1)

    last = functools.reduce(jnp.add, [last] + [exchange(last, e) for e in range(1, nx)])
    last = jnp.broadcast_to(last[None], (ny,) + last.shape)
    last = lax.all_to_all(last, "gy", split_axis=0, concat_axis=0, tiled=True)
    values = call(
        functools.partial(decode_kernel, s),
        "decode",
        shape(ny * cap, PB),
        [SM, SM] + [VM] * 7,
        VM,
        4e9,
        6e6,
        scratch=[pltpu.VMEM((2, B * B * B, s.LB), BF), pltpu.SMEM((ny * cap + 8,), jnp.int32)],
        room=32,
    )(where, base, points, last, turns, read.reshape(B * B * B, s.LB), t["xy_hi"], t["xy_lo"], t["z_last"])
    returned = lax.all_to_all(values.reshape(ny, cap, PB), "gy", split_axis=0, concat_axis=0, tiled=True)
    choose = (slot_of[:, None] == jnp.arange(ny * cap, dtype=jnp.int32)[None, :]).astype(F32)
    pressure = jnp.dot(choose, returned.reshape(ny * cap, PB), precision=lax.Precision.HIGHEST)
    return pressure.reshape(blocks * PB)


def solution(mesh):
    placed = (
        P(None, ("gx", "gy")),
        P(None, ("gx", "gy")),
        P(("gx", "gy")),
        P(("gx", "gy")),
        P(("gx", "gy")),
        P("gx", "gy", None),
        P(),
        P(),
        P(),
        P(None, None, "gy", "gx", None),
        P(),
    )
    return jax.shard_map(
        per_device, mesh=mesh, in_specs=placed, out_specs=P(("gx", "gy")), check_vma=False
    )
```
